32 devices in a mesh: groups: 2 (over y), row: 16 (over z, x, core).
Axes of the slice: x: 2, y: 2, z: 4, core: 2. Of those that a mesh axis runs over, the one named last changes fastest.
Arguments:
- hidden: bfloat16 [4096, 5120], P(('groups', 'row')), parts along dimension 0, may hold values from -6 to 6
- kv_gain: float32 [5120], replicated, may hold values from 0.5 to 1.5
- kv_weight: bfloat16 [5120, 2048], P('row'), may hold values from -0.25 to 0.25
- query_states: bfloat16 [5120, 256], P('row', 'groups'), parts along dimension 1, may hold values from -6 to 6
- query_gain: float32 [2, 5120], replicated, may hold values from 0.5 to 1.5
- query_weight: bfloat16 [2, 16, 2560, 640], P(None, 'row'), may hold values from -0.078125 to 0.078125
- output_weight: bfloat16 [2, 16, 2560, 640], P(None, 'row'), may hold values from -0.078125 to 0.078125
- block_bounds: int32 [4, 2], P('groups'), parts along dimension 0, may hold values from 0 to 1984, as said below
Outputs:
- mixed: bfloat16 [5120, 256], P('row', 'groups'), parts along dimension 1
The draws below stay inside these ranges and needn't reach their ends.
There are 2 independent parts, one for each index of `groups`. The reference program is written for one: setup_inputs(seed, part) draws one part's arguments, and reference() takes and returns one part's arrays. A program takes and returns all parts, laid end to end along the dimension named above; an argument that names none is the same for every part. Nothing has to cross between parts.
Inputs may be any that keep to these rules, and one draw needn't show every extreme that they name: `block_bounds`: row b is (lowest visible key position, first query position) of query block b; the first is at most the second, and block 0 starts 64 positions before the end of the prefix.
All inputs are finite; a program needn't handle non-finite values.
Results may differ from the reference program's by a relative error of at most 0.035.
Values may be sent and summed in bfloat16 or wider, within the bound.
No kernel may reach another device: no remote copies, remote signals or barrier semaphores. Data moves between devices by JAX's collectives and lax.ppermute only.
A program may use at most 128 MiB of HBM per device.

```python
import jax
import jax.numpy as jnp
from jax import lax

D = 5120
HEADS = 40
KVH = 8
HD = 128
QPK = 5
QBLK = 64
NQB = 2
SECTIONS = 2
TOKENS = 2048
TILES = 2
QROWS = 128


def draw_block_bounds(key, part):
    key_one, key_two = jax.random.split(jax.random.fold_in(key, 11), 2)
    last_start = TOKENS - QBLK
    other_start = jax.random.randint(key_one, (NQB - 1,), 0, last_start + 1).astype(jnp.int32)
    starts = jnp.concatenate([jnp.full((1,), last_start, jnp.int32), other_start])
    floors = jax.random.randint(key_two, (NQB,), 0, starts + 1).astype(jnp.int32)
    return jnp.stack([floors, starts], axis=1).astype(jnp.int32)


def steps_of(rng, dims, cuts, least, high):
    level, own = 1.0, jax.random.fold_in(rng, 6)
    for position, shards_of in cuts:
        heights = jnp.exp(jax.random.uniform(jax.random.fold_in(own, position), (shards_of,), jnp.float32, least / len(cuts), high / len(cuts)))
        level = level * jnp.repeat(heights, dims[position] // shards_of).reshape([-1 if axis == position else 1 for axis in range(len(dims))])
    return level


def bell_draw(rng, extent, scale, limit, cuts=(), held_as=jnp.bfloat16):
    values = scale * jax.random.normal(rng, extent, jnp.float32)
    if cuts:
        values = values * steps_of(rng, extent, cuts, -0.22, 0.18)
    return jnp.clip(values, -limit, limit).astype(held_as)


def setup_inputs(seed: int = 0, part: int = 0) -> dict:
    arg_keys = jax.random.split(jax.random.key(seed), 9)
    part_keys = jax.random.split(jax.random.fold_in(arg_keys[8], part), 9)
    return {
        "hidden": bell_draw(part_keys[0], (TOKENS, D), 1.0, 6.0, ((0, 16),)),
        "kv_gain": jnp.clip(1.0 + 0.1 * jax.random.normal(arg_keys[1], (D,), jnp.float32), 0.5, 1.5),
        "kv_weight": bell_draw(arg_keys[2], (D, 2 * KVH * HD), (D // 9) ** -0.5, 0.25, ((0, 16),)),
        "query_states": bell_draw(part_keys[3], (D, QROWS), 1.0, 6.0, ((0, 16),)),
        "query_gain": jnp.clip(1.0 + 0.1 * jax.random.normal(arg_keys[4], (SECTIONS, D), jnp.float32), 0.5, 1.5),
        "query_weight": bell_draw(arg_keys[5], (SECTIONS, KVH * TILES, D // TILES, QPK * HD), D ** -0.5, 0.078125, ((1, 16),)),
        "output_weight": bell_draw(arg_keys[6], (SECTIONS, KVH * TILES, D // TILES, QPK * HD), (HEADS * HD) ** -0.5, 0.078125, ((1, 16),)),
        "block_bounds": draw_block_bounds(jax.random.fold_in(jax.random.fold_in(arg_keys[8], part), 71), part),
    }


CAP = 30.0
EPSILON = 1e-05

def full_weight(blocks):
    arranged = blocks.reshape(TILES, KVH, D // TILES, QPK * HD)
    return jnp.transpose(arranged, (0, 2, 1, 3)).reshape(D, KVH * QPK * HD)

def reference(hidden, kv_gain, kv_weight, query_states, query_gain, query_weight, output_weight, block_bounds):
    hidden_float = hidden.astype(jnp.float32)
    inverse = lax.rsqrt(lax.optimization_barrier(jnp.mean(hidden_float * hidden_float, axis=1, keepdims=True)) + EPSILON)
    normed = (hidden_float * inverse * kv_gain[None, :]).astype(jnp.bfloat16)
    projected = jnp.dot(normed, kv_weight, preferred_element_type=jnp.float32).astype(jnp.bfloat16)
    projected = projected.reshape(TOKENS, KVH, 2, HD)
    key_pos = jnp.arange(TOKENS, dtype=jnp.int32)
    row_number = jnp.arange(QROWS, dtype=jnp.int32)
    query_pos = jnp.repeat(block_bounds[:, 1], QBLK).astype(jnp.int32) + row_number % QBLK
    query_floor = jnp.repeat(block_bounds[:, 0], QBLK).astype(jnp.int32)
    visible = (key_pos[None, :] <= query_pos[:, None]) & (key_pos[None, :] >= query_floor[:, None])
    stream = query_states
    for section in range(SECTIONS):
        stream_float = stream.astype(jnp.float32)
        squares = lax.optimization_barrier(jnp.sum(stream_float * stream_float, axis=0))
        inverse_q = lax.rsqrt(squares / D + EPSILON)
        scaled = (stream_float * query_gain[section][:, None]).astype(jnp.bfloat16)
        w_query = full_weight(query_weight[section])
        queries = lax.dot_general(scaled, w_query, (((0,), (0,)), ((), ())), preferred_element_type=jnp.float32)
        queries = (queries * inverse_q[:, None]).astype(jnp.bfloat16).reshape(QROWS, KVH, QPK, HD)

        def one_group(group):
            q_group = lax.dynamic_index_in_dim(queries, group, 1, keepdims=False).astype(jnp.float32)
            kv_group = lax.dynamic_index_in_dim(projected, group, 1, keepdims=False)
            key_part = kv_group[:, 0, :].astype(jnp.float32)
            value_part = kv_group[:, 1, :].astype(jnp.float32)
            scores = jnp.einsum('qhd,kd->qhk', q_group, key_part) * HD ** (-0.5)
            capped = CAP * jnp.tanh(scores / CAP)
            weights = jnp.where(visible[:, None, :], jnp.exp(capped), 0.0)
            totals = lax.optimization_barrier(jnp.sum(weights, axis=2))
            rounded = lax.optimization_barrier(weights.astype(jnp.bfloat16)).astype(jnp.float32)
            weighted = jnp.einsum('qhk,kd->qhd', rounded, value_part)
            return weighted / totals[:, :, None]
        attended = lax.map(one_group, jnp.arange(KVH, dtype=jnp.int32))
        attended = jnp.transpose(attended, (1, 0, 2, 3)).reshape(QROWS, KVH * QPK * HD).astype(jnp.bfloat16)
        w_out = full_weight(output_weight[section])
        update = lax.dot_general(w_out, attended, (((1,), (1,)), ((), ())), preferred_element_type=jnp.float32)
        stream = (stream_float + update).astype(jnp.bfloat16)
    return stream
```

```python
import jax
import jax.numpy as jnp
from jax import lax
from jax.sharding import PartitionSpec as P

KVH = 8
HD = 128
QPK = 5
QBLK = 64
CAP = 30.0
EPSILON = 1e-05
BF16 = jnp.bfloat16
F32 = jnp.float32

CHIPS = KVH // 2
ROUNDS = ((3,), (1,), (2,), (0,))


def swapped(value, mask, axis="row"):
    pairs = [(source, source ^ mask) for source in range(lax.axis_size(axis))]
    return lax.ppermute(value, axis, pairs)


def over_tiles(value, tile_count):
    values = [value]
    mask = 1
    while mask < tile_count:
        if len(values) == 1:
            values.append(swapped(values[0], mask * KVH))
        else:
            got = swapped(jnp.stack(values), mask * KVH)
            values.extend(got[place] for place in range(len(values)))
        mask *= 2
    return values


def natural(pieces, index):
    pieces = list(pieces)
    bit = 1
    while bit < len(pieces):
        upper = index // bit % 2 == 1
        pieces = [jnp.where(upper, pieces[j ^ bit], pieces[j]) for j in range(len(pieces))]
        bit *= 2
    return pieces


def key_values_of(hidden, kv_gain, kv_weight):
    lane_count = lax.axis_size("row")
    tile_count = lane_count // KVH
    me = lax.axis_index("row")
    tile, chip, core = me // KVH, me // 2 % CHIPS, me % 2
    rows, depth = hidden.shape
    unit = kv_weight.shape[0]
    pair = 2 * HD

    def head_columns(place, which_core):
        return lax.dynamic_slice_in_dim(kv_weight, ((chip ^ place) * 2 + which_core) * pair, pair, 1)

    order = [place for round_ in ROUNDS for place in round_]
    kept = {place: head_columns(place, core) for place in order}
    traded = swapped(jnp.stack([head_columns(place, 1 - core) for place in order]), 1)
    traded = {place: traded[number] for number, place in enumerate(order)}

    hidden_float = hidden.astype(F32)
    inverse = lax.rsqrt(jnp.mean(hidden_float * hidden_float, axis=1, keepdims=True) + EPSILON)
    normed = (hidden_float * inverse * kv_gain[None, :]).astype(BF16)

    def features(place):
        return jnp.concatenate(
            [
                lax.dynamic_slice_in_dim(
                    normed, ((tile ^ j) * KVH + (chip ^ place) * 2) * unit, 2 * unit, 1
                )
                for j in range(tile_count)
            ],
            axis=1,
        )

    share = lax.axis_size("groups") == 2
    part = lax.axis_index("groups")
    held = []
    for place in range(CHIPS):
        own = features(place)
        held.append(own if place == 0 else swapped(own, 2 * place))
    mine = jnp.concatenate(held, axis=0)
    tokens = jnp.concatenate([mine, swapped(mine, 1)], axis=0)

    total = None
    for round_ in ROUNDS:
        first = jnp.stack([kept[place] for place in round_])
        second = jnp.stack([traded[place] for place in round_])
        low, high = jnp.where(core == 0, first, second), jnp.where(core == 0, second, first)
        blocks = [(low, high)]
        if share:
            far = over_tiles(jnp.where(part == 0, low, high), tile_count)[1:]
            for value in far:
                other = swapped(value, 1, "groups")
                blocks.append((jnp.where(part == 0, value, other), jnp.where(part == 0, other, value)))
        else:
            far = over_tiles(jnp.stack([low, high]), tile_count)[1:]
            blocks.extend((value[0], value[1]) for value in far)
        for number, place in enumerate(round_):
            weight = jnp.concatenate([half[number] for block in blocks for half in block], axis=0)
            partial = lax.dot_general(
                tokens, weight, (((1,), (0,)), ((), ())), preferred_element_type=F32
            )
            if place:
                partial = swapped(partial.astype(BF16), 2 * place).astype(F32)
            pieces = partial.reshape(2, CHIPS, rows, pair)
            pieces = jnp.stack([pieces[:, j ^ place] for j in range(CHIPS)], axis=1)
            total = pieces if total is None else total + pieces
    key_values = total.astype(BF16).reshape(2 * CHIPS * rows, pair)
    sources = jnp.stack(
        [tile * KVH + (chip ^ j) * 2 + (core ^ e) for e in range(2) for j in range(CHIPS)]
    )
    key_pos = (sources[:, None] * rows + jnp.arange(rows, dtype=jnp.int32)[None, :]).reshape(-1)
    return key_values, key_pos


def gather_rows(own):
    me = lax.axis_index("row")
    chip, core = me // 2 % CHIPS, me % 2
    chips = [own] + [swapped(own, 2 * place) for place in range(1, CHIPS)]
    ours = jnp.stack(natural(chips, chip))
    theirs = swapped(ours, 1)
    low, high = jnp.where(core == 0, ours, theirs), jnp.where(core == 0, theirs, ours)
    return jnp.stack([low, high], axis=1).reshape(KVH * own.shape[0], own.shape[1])


def scatter_rows(update, rows):
    me = lax.axis_index("row")
    chip, core = me // 2 % CHIPS, me % 2
    split = update.reshape(CHIPS, 2, rows, update.shape[1])
    kept = jnp.where(core == 0, split[:, 0], split[:, 1])
    sent = jnp.where(core == 0, split[:, 1], split[:, 0])
    both = kept + swapped(sent.astype(BF16), 1).astype(F32)
    total = lax.dynamic_index_in_dim(both, chip, 0, keepdims=False)
    for place in range(1, CHIPS):
        piece = lax.dynamic_index_in_dim(both, chip ^ place, 0, keepdims=False)
        total = total + swapped(piece.astype(BF16), 2 * place).astype(F32)
    return total


def attend_rows(queries, query_pos, query_floor, key_values, key_pos):
    row_count = queries.shape[0]
    head_count = queries.shape[1] // HD
    key_part = key_values[:, :HD]
    value_part = key_values[:, HD:]
    grouped = queries.reshape(row_count, head_count, HD)
    scores = jnp.einsum("rhd,kd->rhk", grouped, key_part, preferred_element_type=F32) * HD ** (-0.5)
    capped = CAP * jnp.tanh(scores / CAP)
    visible = (key_pos[None, :] <= query_pos[:, None]) & (key_pos[None, :] >= query_floor[:, None])
    weights = jnp.where(visible[:, None, :], jnp.exp(capped), 0.0)
    totals = jnp.sum(weights, axis=2)
    weighted = jnp.einsum(
        "rhk,kd->rhd", weights.astype(BF16), value_part, preferred_element_type=F32
    )
    return weighted.reshape(row_count, head_count * HD), totals


def on_device(
    hidden, kv_gain, kv_weight, query_states, query_gain, query_weight, output_weight, block_bounds
):
    tile_count = lax.axis_size("row") // KVH
    tile = lax.axis_index("row") // KVH
    depth = hidden.shape[1]
    slice_depth = query_weight.shape[2]
    query_count = query_states.shape[1]
    row_number = jnp.arange(query_count, dtype=jnp.int32)
    query_pos = jnp.repeat(block_bounds[:, 1], QBLK) + row_number % QBLK
    query_floor = jnp.repeat(block_bounds[:, 0], QBLK)

    key_values, key_pos = key_values_of(hidden, kv_gain, kv_weight)
    own_rows = query_states
    for section in range(query_gain.shape[0]):
        stream = gather_rows(own_rows).astype(F32)
        squares = jnp.sum(stream * stream, axis=0)
        gain = lax.dynamic_slice_in_dim(query_gain[section], tile * slice_depth, slice_depth)
        scaled = (stream * gain[:, None]).astype(BF16)
        partial = lax.dot_general(
            scaled, query_weight[section, 0], (((0,), (0,)), ((), ())), preferred_element_type=F32
        )
        square_sum = sum(over_tiles(squares.astype(BF16), tile_count)[1:], squares)
        query_sum = sum(over_tiles(partial.astype(BF16), tile_count)[1:], partial)
        inverse = lax.rsqrt(square_sum / depth + EPSILON)
        queries = (query_sum * inverse[:, None]).astype(BF16)
        weighted, totals = attend_rows(queries, query_pos, query_floor, key_values, key_pos)
        total_sum = sum(over_tiles(totals.astype(BF16), tile_count)[1:], totals)
        weighted_sum = sum(over_tiles(weighted.astype(BF16), tile_count)[1:], weighted)
        attended = (
            (weighted_sum.reshape(query_count, QPK, HD) / total_sum[:, :, None])
            .reshape(query_count, QPK * HD)
            .astype(BF16)
        )
        update = lax.dot_general(
            output_weight[section, 0], attended, (((1,), (1,)), ((), ())), preferred_element_type=F32
        )
        own_rows = (
            own_rows.astype(F32) + scatter_rows(update, own_rows.shape[0])
        ).astype(BF16)
    return own_rows


def solution(mesh):
    in_specs = (
        P(("groups", "row"), None),
        P(),
        P("row", None),
        P("row", "groups"),
        P(),
        P(None, "row", None, None),
        P(None, "row", None, None),
        P("groups", None),
    )
    return jax.shard_map(
        on_device, mesh=mesh, in_specs=in_specs, out_specs=P("row", "groups"), check_vma=False
    )
```

```python
import functools

import jax
import jax.numpy as jnp
from jax import lax
from jax.experimental import pallas as pl
from jax.experimental.pallas import tpu as pltpu
from jax.sharding import PartitionSpec as P

KVH = 8
HD = 128
QPK = 5
QBLK = 64
CAP = 30.0
EPSILON = 1e-05
BF16 = jnp.bfloat16
F32 = jnp.float32

CHIPS = KVH // 2
ROUNDS = ((3,), (1,), (2,), (0,))


def swapped(value, mask, axis="row"):
    pairs = [(source, source ^ mask) for source in range(lax.axis_size(axis))]
    return lax.ppermute(value, axis, pairs)


def over_tiles(value, tile_count):
    values = [value]
    mask = 1
    while mask < tile_count:
        if len(values) == 1:
            values.append(swapped(values[0], mask * KVH))
        else:
            got = swapped(jnp.stack(values), mask * KVH)
            values.extend(got[place] for place in range(len(values)))
        mask *= 2
    return values


def natural(pieces, index):
    pieces = list(pieces)
    bit = 1
    while bit < len(pieces):
        upper = index // bit % 2 == 1
        pieces = [jnp.where(upper, pieces[j ^ bit], pieces[j]) for j in range(len(pieces))]
        bit *= 2
    return pieces


def arrange_kernel(pair, heads_ref, weight_ref, *refs):
    out_refs, sems = refs[:-1], refs[-1]
    copies = []
    for out_ref in out_refs:
        for place in range(out_ref.shape[0]):
            column = pl.multiple_of(heads_ref[len(copies)] * pair, pair)
            copies.append(
                pltpu.make_async_copy(
                    weight_ref.at[:, pl.ds(column, pair)], out_ref.at[place], sems.at[len(copies)]
                )
            )
    for copy in copies:
        copy.start()
    for copy in copies:
        copy.wait()


def arranged(weight, groups, pair):
    unit = weight.shape[0]
    heads = [head for group in groups for head in group]
    if unit % 16:
        columns = [lax.dynamic_slice_in_dim(weight, head * pair, pair, 1) for head in heads]
        results = []
        for group in groups:
            results.append(jnp.stack(columns[: len(group)]))
            columns = columns[len(group) :]
        return results
    return pl.pallas_call(
        functools.partial(arrange_kernel, pair),
        out_shape=[jax.ShapeDtypeStruct((len(group), unit, pair), weight.dtype) for group in groups],
        in_specs=[
            pl.BlockSpec(memory_space=pltpu.SMEM),
            pl.BlockSpec(memory_space=pl.ANY),
        ],
        out_specs=[pl.BlockSpec(memory_space=pl.ANY)] * len(groups),
        scratch_shapes=[pltpu.SemaphoreType.DMA((len(heads),))],
        name="arrange_weight",
    )(jnp.stack(heads).astype(jnp.int32), weight)


def norm_kernel(width, starts_ref, hidden_ref, gain_ref, *refs):
    out_refs, normed = refs[:-1], refs[-1]
    hidden = hidden_ref[...].astype(F32)
    inverse = lax.rsqrt(jnp.mean(hidden * hidden, axis=1, keepdims=True) + EPSILON)
    normed[...] = (hidden * inverse * gain_ref[...]).astype(BF16)
    number = 0
    for out_ref in out_refs:
        for place in range(out_ref.shape[1] // width):
            start = pl.multiple_of(starts_ref[number] * width, 128)
            out_ref[:, place * width : (place + 1) * width] = normed[:, pl.ds(start, width)]
            number += 1


def normed_features(hidden, gain, groups, width):
    rows, depth = hidden.shape
    if width % 128 or rows % 16:
        hidden_float = hidden.astype(F32)
        inverse = lax.rsqrt(jnp.mean(hidden_float * hidden_float, axis=1, keepdims=True) + EPSILON)
        normed = (hidden_float * inverse * gain[None, :]).astype(BF16)
        return [
            jnp.concatenate(
                [lax.dynamic_slice_in_dim(normed, block * width, width, 1) for block in group], axis=1
            )
            for group in groups
        ]
    blocks = [block for group in groups for block in group]
    vmem = pl.BlockSpec(memory_space=pltpu.VMEM)
    return pl.pallas_call(
        functools.partial(norm_kernel, width),
        out_shape=[jax.ShapeDtypeStruct((rows, len(group) * width), BF16) for group in groups],
        in_specs=[pl.BlockSpec(memory_space=pltpu.SMEM), vmem, vmem],
        out_specs=[vmem] * len(groups),
        scratch_shapes=[pltpu.VMEM((rows, depth), BF16)],
        compiler_params=pltpu.CompilerParams(vmem_limit_bytes=32 * 1024 * 1024),
        name="norm_hidden",
    )(jnp.stack(blocks).astype(jnp.int32), hidden, gain[None, :])


def key_values_of(hidden, kv_gain, kv_weight):
    lane_count = lax.axis_size("row")
    tile_count = lane_count // KVH
    me = lax.axis_index("row")
    tile, chip, core = me // KVH, me // 2 % CHIPS, me % 2
    rows = hidden.shape[0]
    unit = kv_weight.shape[0]
    pair = 2 * HD
    share = lax.axis_size("groups") == 2
    part = lax.axis_index("groups") if share else 0

    order = [place for round_ in ROUNDS for place in round_]
    heads = {place: (chip ^ place) * 2 + core for place in order}
    others = {place: (chip ^ place) * 2 + 1 - core for place in order}
    sent = [[heads[place] ^ part for place in round_] for round_ in ROUNDS]
    pieces = arranged(
        kv_weight, sent + [[others[p] for p in order], [heads[p] for p in order]], pair
    )
    sent, traded, kept = pieces[: len(ROUNDS)], pieces[-2], pieces[-1]

    def to_tile(value, j, flip):
        if not share:
            return swapped(value, j * KVH)
        pairs = [
            (g * lane_count + d, g * lane_count + (d ^ (j * KVH) ^ (g if flip else 0)))
            for g in range(2)
            for d in range(lane_count)
        ]
        return lax.ppermute(value, ("groups", "row"), pairs)

    far = [[to_tile(value, j, True) for j in range(1, tile_count)] for value in sent]
    traded = swapped(traded, 1)

    width = 2 * unit
    features = normed_features(
        hidden,
        kv_gain,
        [
            [(tile ^ j) * CHIPS + (chip ^ place) for j in range(tile_count)]
            for place in range(CHIPS)
        ],
        width,
    )
    held = [features[0]] + [swapped(features[p], 2 * p) for p in range(1, CHIPS)]
    mine = jnp.concatenate(held, axis=0)
    tokens = jnp.concatenate([mine, swapped(mine, 1)], axis=0)

    total = None
    place_in_order = 0
    for number, round_ in enumerate(ROUNDS):
        span = slice(place_in_order, place_in_order + len(round_))
        place_in_order += len(round_)
        blocks = [(kept[span], traded[span])]
        for j, value in enumerate(far[number], 1):
            if share:
                other = swapped(value, 1, "groups")
                blocks.append((jnp.where(part == 0, value, other), jnp.where(part == 0, other, value)))
            else:
                blocks.append((value, to_tile(traded[span], j, False)))
        blocks = [
            (jnp.where(core == 0, own, other), jnp.where(core == 0, other, own))
            for own, other in blocks
        ]
        for inner, place in enumerate(round_):
            weight = jnp.concatenate([half[inner] for block in blocks for half in block], axis=0)
            partial = lax.dot_general(
                tokens, weight, (((1,), (0,)), ((), ())), preferred_element_type=F32
            )
            if place:
                partial = swapped(partial.astype(BF16), 2 * place).astype(F32)
            pieces = partial.reshape(2, CHIPS, rows, pair)
            pieces = jnp.stack([pieces[:, j ^ place] for j in range(CHIPS)], axis=1)
            total = pieces if total is None else total + pieces
    key_values = total.astype(BF16).reshape(2 * CHIPS * rows, pair)
    sources = jnp.stack(
        [tile * KVH + (chip ^ j) * 2 + (core ^ e) for e in range(2) for j in range(CHIPS)]
    )
    key_pos = (sources[:, None] * rows + jnp.arange(rows, dtype=jnp.int32)[None, :]).reshape(-1)
    return key_values, key_pos


def gather_rows(own):
    me = lax.axis_index("row")
    chip, core = me // 2 % CHIPS, me % 2
    chips = [own] + [swapped(own, 2 * place) for place in range(1, CHIPS)]
    ours = jnp.stack(natural(chips, chip))
    theirs = swapped(ours, 1)
    low, high = jnp.where(core == 0, ours, theirs), jnp.where(core == 0, theirs, ours)
    return jnp.stack([low, high], axis=1).reshape(KVH * own.shape[0], own.shape[1])


def scatter_rows(update, rows):
    me = lax.axis_index("row")
    chip, core = me // 2 % CHIPS, me % 2
    split = update.reshape(CHIPS, 2, rows, update.shape[1])
    kept = jnp.where(core == 0, split[:, 0], split[:, 1])
    sent = jnp.where(core == 0, split[:, 1], split[:, 0])
    both = kept + swapped(sent.astype(BF16), 1).astype(F32)
    total = lax.dynamic_index_in_dim(both, chip, 0, keepdims=False)
    for place in range(1, CHIPS):
        piece = lax.dynamic_index_in_dim(both, chip ^ place, 0, keepdims=False)
        total = total + swapped(piece.astype(BF16), 2 * place).astype(F32)
    return total


def attend_rows(queries, query_pos, query_floor, key_values, key_pos):
    row_count = queries.shape[0]
    head_count = queries.shape[1] // HD
    key_part = key_values[:, :HD]
    value_part = key_values[:, HD:]
    grouped = queries.reshape(row_count, head_count, HD)
    scores = jnp.einsum("rhd,kd->rhk", grouped, key_part, preferred_element_type=F32) * HD ** (-0.5)
    capped = CAP * jnp.tanh(scores / CAP)
    visible = (key_pos[None, :] <= query_pos[:, None]) & (key_pos[None, :] >= query_floor[:, None])
    weights = jnp.where(visible[:, None, :], jnp.exp(capped), 0.0)
    totals = jnp.sum(weights, axis=2)
    weighted = jnp.einsum(
        "rhk,kd->rhd", weights.astype(BF16), value_part, preferred_element_type=F32
    )
    return weighted.reshape(row_count, head_count * HD), totals


def on_device(
    hidden, kv_gain, kv_weight, query_states, query_gain, query_weight, output_weight, block_bounds
):
    tile_count = lax.axis_size("row") // KVH
    tile = lax.axis_index("row") // KVH
    depth = hidden.shape[1]
    slice_depth = query_weight.shape[2]
    query_count = query_states.shape[1]
    row_number = jnp.arange(query_count, dtype=jnp.int32)
    query_pos = jnp.repeat(block_bounds[:, 1], QBLK) + row_number % QBLK
    query_floor = jnp.repeat(block_bounds[:, 0], QBLK)

    key_values, key_pos = key_values_of(hidden, kv_gain, kv_weight)
    own_rows = query_states
    for section in range(query_gain.shape[0]):
        stream = gather_rows(own_rows).astype(F32)
        squares = jnp.sum(stream * stream, axis=0)
        gain = lax.dynamic_slice_in_dim(query_gain[section], tile * slice_depth, slice_depth)
        scaled = (stream * gain[:, None]).astype(BF16)
        partial = lax.dot_general(
            scaled, query_weight[section, 0], (((0,), (0,)), ((), ())), preferred_element_type=F32
        )
        square_sum = sum(over_tiles(squares.astype(BF16), tile_count)[1:], squares)
        query_sum = sum(over_tiles(partial.astype(BF16), tile_count)[1:], partial)
        inverse = lax.rsqrt(square_sum / depth + EPSILON)
        queries = (query_sum * inverse[:, None]).astype(BF16)
        weighted, totals = attend_rows(queries, query_pos, query_floor, key_values, key_pos)
        total_sum = sum(over_tiles(totals.astype(BF16), tile_count)[1:], totals)
        weighted_sum = sum(over_tiles(weighted.astype(BF16), tile_count)[1:], weighted)
        attended = (
            (weighted_sum.reshape(query_count, QPK, HD) / total_sum[:, :, None])
            .reshape(query_count, QPK * HD)
            .astype(BF16)
        )
        update = lax.dot_general(
            output_weight[section, 0], attended, (((1,), (1,)), ((), ())), preferred_element_type=F32
        )
        own_rows = (
            own_rows.astype(F32) + scatter_rows(update, own_rows.shape[0])
        ).astype(BF16)
    return own_rows


def solution(mesh):
    in_specs = (
        P(("groups", "row"), None),
        P(),
        P("row", None),
        P("row", "groups"),
        P(),
        P(None, "row", None, None),
        P(None, "row", None, None),
        P("groups", None),
    )
    return jax.shard_map(
        on_device, mesh=mesh, in_specs=in_specs, out_specs=P("row", "groups"), check_vma=False
    )
```

```python
import functools

import jax
import jax.numpy as jnp
from jax import lax
from jax.experimental import pallas as pl
from jax.experimental.pallas import tpu as pltpu
from jax.sharding import PartitionSpec as P

KVH = 8
HD = 128
QPK = 5
QBLK = 64
CAP = 30.0
EPSILON = 1e-05
BF16 = jnp.bfloat16
F32 = jnp.float32

CHIPS = KVH // 2
ROUNDS = ((3,), (1,), (2,), (0,))


def swapped(value, mask, axis="row"):
    pairs = [(source, source ^ mask) for source in range(lax.axis_size(axis))]
    return lax.ppermute(value, axis, pairs)


def over_tiles(value, tile_count):
    values = [value]
    mask = 1
    while mask < tile_count:
        if len(values) == 1:
            values.append(swapped(values[0], mask * KVH))
        else:
            got = swapped(jnp.stack(values), mask * KVH)
            values.extend(got[place] for place in range(len(values)))
        mask *= 2
    return values


def natural(pieces, index):
    pieces = list(pieces)
    bit = 1
    while bit < len(pieces):
        upper = index // bit % 2 == 1
        pieces = [jnp.where(upper, pieces[j ^ bit], pieces[j]) for j in range(len(pieces))]
        bit *= 2
    return pieces


def arrange_kernel(pair, heads_ref, weight_ref, *out_refs):
    number = 0
    for out_ref in out_refs:
        for place in range(out_ref.shape[0]):
            column = pl.multiple_of(heads_ref[number] * pair, pair)
            out_ref[place] = weight_ref[:, pl.ds(column, pair)]
            number += 1


def arranged(weight, groups, pair):
    unit = weight.shape[0]
    heads = [head for group in groups for head in group]
    if unit % 16:
        columns = [lax.dynamic_slice_in_dim(weight, head * pair, pair, 1) for head in heads]
        results = []
        for group in groups:
            results.append(jnp.stack(columns[: len(group)]))
            columns = columns[len(group) :]
        return results
    vmem = pl.BlockSpec(memory_space=pltpu.VMEM)
    return pl.pallas_call(
        functools.partial(arrange_kernel, pair),
        out_shape=[jax.ShapeDtypeStruct((len(group), unit, pair), weight.dtype) for group in groups],
        in_specs=[pl.BlockSpec(memory_space=pltpu.SMEM), vmem],
        out_specs=[vmem] * len(groups),
        compiler_params=pltpu.CompilerParams(vmem_limit_bytes=16 * 1024 * 1024),
        name="arrange_weight",
    )(jnp.stack(heads).astype(jnp.int32), weight)


def norm_kernel(width, starts_ref, hidden_ref, gain_ref, extra_ref, *refs):
    out_refs, normed = refs[:-1], refs[-1]
    rows = hidden_ref.shape[0]
    hidden = hidden_ref[...].astype(F32)
    inverse = lax.rsqrt(jnp.mean(hidden * hidden, axis=1, keepdims=True) + EPSILON)
    normed[...] = (hidden * inverse * gain_ref[...]).astype(BF16)
    number = 0
    for out_ref in out_refs:
        for place in range(out_ref.shape[1] // width):
            start = pl.multiple_of(starts_ref[number] * width, 128)
            out_ref[:rows, place * width : (place + 1) * width] = normed[:, pl.ds(start, width)]
            number += 1
        out_ref[rows:, :] = extra_ref[...]


def normed_features(hidden, gain, groups, width, extra):
    rows, depth = hidden.shape
    if width % 128 or rows % 16 or extra.shape[0] % 16:
        hidden_float = hidden.astype(F32)
        inverse = lax.rsqrt(jnp.mean(hidden_float * hidden_float, axis=1, keepdims=True) + EPSILON)
        normed = (hidden_float * inverse * gain[None, :]).astype(BF16)
        return [
            jnp.concatenate(
                [
                    jnp.concatenate(
                        [
                            lax.dynamic_slice_in_dim(normed, block * width, width, 1)
                            for block in group
                        ],
                        axis=1,
                    ),
                    extra,
                ],
                axis=0,
            )
            for group in groups
        ]
    blocks = [block for group in groups for block in group]
    vmem = pl.BlockSpec(memory_space=pltpu.VMEM)
    return pl.pallas_call(
        functools.partial(norm_kernel, width),
        out_shape=[
            jax.ShapeDtypeStruct((rows + extra.shape[0], len(group) * width), BF16)
            for group in groups
        ],
        in_specs=[pl.BlockSpec(memory_space=pltpu.SMEM), vmem, vmem, vmem],
        out_specs=[vmem] * len(groups),
        scratch_shapes=[pltpu.VMEM((rows, depth), BF16)],
        compiler_params=pltpu.CompilerParams(vmem_limit_bytes=32 * 1024 * 1024),
        name="norm_hidden",
    )(jnp.stack(blocks).astype(jnp.int32), hidden, gain[None, :], extra)


def in_order(ours, theirs, core):
    low, high = jnp.where(core == 0, ours, theirs), jnp.where(core == 0, theirs, ours)
    return jnp.stack([low, high], axis=1).reshape(-1, ours.shape[-1])


def key_values_of(hidden, kv_gain, kv_weight, query_states):
    lane_count = lax.axis_size("row")
    tile_count = lane_count // KVH
    me = lax.axis_index("row")
    tile, chip, core = me // KVH, me // 2 % CHIPS, me % 2
    rows = hidden.shape[0]
    unit = kv_weight.shape[0]
    pair = 2 * HD
    share = lax.axis_size("groups") == 2
    part = lax.axis_index("groups") if share else 0

    order = [place for round_ in ROUNDS for place in round_]
    heads = {place: (chip ^ place) * 2 + core for place in order}
    others = {place: (chip ^ place) * 2 + 1 - core for place in order}
    sent = [[heads[place] ^ part for place in round_] for round_ in ROUNDS]
    pieces = arranged(
        kv_weight, sent + [[others[p] for p in order], [heads[p] for p in order]], pair
    )
    sent, traded, kept = pieces[: len(ROUNDS)], pieces[-2], pieces[-1]

    def to_tile(value, j, flip):
        if not share:
            return swapped(value, j * KVH)
        pairs = [
            (g * lane_count + d, g * lane_count + (d ^ (j * KVH) ^ (g if flip else 0)))
            for g in range(2)
            for d in range(lane_count)
        ]
        return lax.ppermute(value, ("groups", "row"), pairs)

    far = [[to_tile(value, j, True) for j in range(1, tile_count)] for value in sent]
    traded = swapped(traded, 1)

    width = 2 * unit
    features = normed_features(
        hidden,
        kv_gain,
        [
            [(tile ^ j) * CHIPS + (chip ^ place) for j in range(tile_count)]
            for place in range(CHIPS)
        ],
        width,
        query_states.reshape(-1, tile_count * width),
    )
    held = [features[0]] + [swapped(features[p], 2 * p) for p in range(1, CHIPS)]
    mine = jnp.stack(held)
    mine, far[0] = lax.optimization_barrier((mine, far[0]))
    theirs = swapped(mine, 1)
    tokens = jnp.concatenate([held[p][:rows] for p in range(CHIPS)] + [theirs[p, :rows] for p in range(CHIPS)])
    ours, theirs = (
        jnp.stack(natural([value[p, rows:].reshape(query_states.shape) for p in range(CHIPS)], chip))
        for value in (mine, theirs)
    )
    stream = in_order(ours, theirs, core)

    total = None
    place_in_order = 0
    for number, round_ in enumerate(ROUNDS):
        span = slice(place_in_order, place_in_order + len(round_))
        place_in_order += len(round_)
        blocks = [(kept[span], traded[span])]
        for j, value in enumerate(far[number], 1):
            if share:
                other = swapped(value, 1, "groups")
                blocks.append((jnp.where(part == 0, value, other), jnp.where(part == 0, other, value)))
            else:
                blocks.append((value, to_tile(traded[span], j, False)))
        blocks = [
            (jnp.where(core == 0, own, other), jnp.where(core == 0, other, own))
            for own, other in blocks
        ]
        for inner, place in enumerate(round_):
            weight = jnp.concatenate([half[inner] for block in blocks for half in block], axis=0)
            partial = lax.dot_general(
                tokens, weight, (((1,), (0,)), ((), ())), preferred_element_type=F32
            )
            if place:
                partial = swapped(partial.astype(BF16), 2 * place).astype(F32)
            pieces = partial.reshape(2, CHIPS, rows, pair)
            pieces = jnp.stack([pieces[:, j ^ place] for j in range(CHIPS)], axis=1)
            total = pieces if total is None else total + pieces
    key_values = total.astype(BF16).reshape(2 * CHIPS * rows, pair)
    sources = jnp.stack(
        [tile * KVH + (chip ^ j) * 2 + (core ^ e) for e in range(2) for j in range(CHIPS)]
    )
    key_pos = (sources[:, None] * rows + jnp.arange(rows, dtype=jnp.int32)[None, :]).reshape(-1)
    return key_values, key_pos, stream


def gather_rows(own):
    me = lax.axis_index("row")
    chip, core = me // 2 % CHIPS, me % 2
    chips = [own] + [swapped(own, 2 * place) for place in range(1, CHIPS)]
    ours = jnp.stack(natural(chips, chip))
    return in_order(ours, swapped(ours, 1), core)


def scatter_rows(update, rows):
    me = lax.axis_index("row")
    chip, core = me // 2 % CHIPS, me % 2
    split = update.reshape(CHIPS, 2, rows, update.shape[1])
    kept = jnp.where(core == 0, split[:, 0], split[:, 1])
    sent = jnp.where(core == 0, split[:, 1], split[:, 0])
    both = kept + swapped(sent.astype(BF16), 1).astype(F32)
    total = lax.dynamic_index_in_dim(both, chip, 0, keepdims=False)
    for place in range(1, CHIPS):
        piece = lax.dynamic_index_in_dim(both, chip ^ place, 0, keepdims=False)
        total = total + swapped(piece.astype(BF16), 2 * place).astype(F32)
    return total


def attend_rows(queries, query_pos, query_floor, key_values, key_pos):
    row_count = queries.shape[0]
    head_count = queries.shape[1] // HD
    key_part = key_values[:, :HD]
    value_part = key_values[:, HD:]
    grouped = queries.reshape(row_count, head_count, HD)
    scores = jnp.einsum("rhd,kd->rhk", grouped, key_part, preferred_element_type=F32) * HD ** (-0.5)
    capped = CAP * jnp.tanh(scores / CAP)
    visible = (key_pos[None, :] <= query_pos[:, None]) & (key_pos[None, :] >= query_floor[:, None])
    weights = jnp.where(visible[:, None, :], jnp.exp(capped), 0.0)
    totals = jnp.sum(weights, axis=2)
    weighted = jnp.einsum(
        "rhk,kd->rhd", weights.astype(BF16), value_part, preferred_element_type=F32
    )
    return weighted.reshape(row_count, head_count * HD), totals


def on_device(
    hidden, kv_gain, kv_weight, query_states, query_gain, query_weight, output_weight, block_bounds
):
    tile_count = lax.axis_size("row") // KVH
    tile = lax.axis_index("row") // KVH
    depth = hidden.shape[1]
    slice_depth = query_weight.shape[2]
    query_count = query_states.shape[1]
    row_number = jnp.arange(query_count, dtype=jnp.int32)
    query_pos = jnp.repeat(block_bounds[:, 1], QBLK) + row_number % QBLK
    query_floor = jnp.repeat(block_bounds[:, 0], QBLK)

    key_values, key_pos, stream = key_values_of(hidden, kv_gain, kv_weight, query_states)
    own_rows = query_states
    for section in range(query_gain.shape[0]):
        if section:
            stream = gather_rows(own_rows)
        stream = stream.astype(F32)
        squares = jnp.sum(stream * stream, axis=0)
        gain = lax.dynamic_slice_in_dim(query_gain[section], tile * slice_depth, slice_depth)
        scaled = (stream * gain[:, None]).astype(BF16)
        partial = lax.dot_general(
            scaled, query_weight[section, 0], (((0,), (0,)), ((), ())), preferred_element_type=F32
        )
        square_sum = sum(over_tiles(squares.astype(BF16), tile_count)[1:], squares)
        query_sum = sum(over_tiles(partial.astype(BF16), tile_count)[1:], partial)
        inverse = lax.rsqrt(square_sum / depth + EPSILON)
        queries = (query_sum * inverse[:, None]).astype(BF16)
        weighted, totals = attend_rows(queries, query_pos, query_floor, key_values, key_pos)
        total_sum = sum(over_tiles(totals.astype(BF16), tile_count)[1:], totals)
        weighted_sum = sum(over_tiles(weighted.astype(BF16), tile_count)[1:], weighted)
        attended = (
            (weighted_sum.reshape(query_count, QPK, HD) / total_sum[:, :, None])
            .reshape(query_count, QPK * HD)
            .astype(BF16)
        )
        update = lax.dot_general(
            output_weight[section, 0], attended, (((1,), (1,)), ((), ())), preferred_element_type=F32
        )
        own_rows = (
            own_rows.astype(F32) + scatter_rows(update, own_rows.shape[0])
        ).astype(BF16)
    return own_rows


def solution(mesh):
    in_specs = (
        P(("groups", "row"), None),
        P(),
        P("row", None),
        P("row", "groups"),
        P(),
        P(None, "row", None, None),
        P(None, "row", None, None),
        P("groups", None),
    )
    return jax.shard_map(
        on_device, mesh=mesh, in_specs=in_specs, out_specs=P("row", "groups"), check_vma=False
    )
```

```python
import functools

import jax
import jax.numpy as jnp
from jax import lax
from jax.experimental import pallas as pl
from jax.experimental.pallas import tpu as pltpu
from jax.sharding import PartitionSpec as P

KVH = 8
HD = 128
QPK = 5
QBLK = 64
CAP = 30.0
EPSILON = 1e-05
BF16 = jnp.bfloat16
F32 = jnp.float32

CHIPS = KVH // 2
ROUNDS = ((1, 2), (3, 0))


def swapped(value, mask, axis="row"):
    pairs = [(source, source ^ mask) for source in range(lax.axis_size(axis))]
    return lax.ppermute(value, axis, pairs)


def over_tiles(value, tile_count):
    values = [value]
    mask = 1
    while mask < tile_count:
        if len(values) == 1:
            values.append(swapped(values[0], mask * KVH))
        else:
            got = swapped(jnp.stack(values), mask * KVH)
            values.extend(got[place] for place in range(len(values)))
        mask *= 2
    return values


def natural(pieces, index):
    pieces = list(pieces)
    bit = 1
    while bit < len(pieces):
        upper = index // bit % 2 == 1
        pieces = [jnp.where(upper, pieces[j ^ bit], pieces[j]) for j in range(len(pieces))]
        bit *= 2
    return pieces


def arrange_kernel(pair, heads_ref, weight_ref, *out_refs):
    number = 0
    for out_ref in out_refs:
        for place in range(out_ref.shape[0]):
            column = pl.multiple_of(heads_ref[number] * pair, pair)
            out_ref[place] = weight_ref[:, pl.ds(column, pair)]
            number += 1


def arranged(weight, groups, pair):
    unit = weight.shape[0]
    heads = [head for group in groups for head in group]
    if unit % 16:
        columns = [lax.dynamic_slice_in_dim(weight, head * pair, pair, 1) for head in heads]
        results = []
        for group in groups:
            results.append(jnp.stack(columns[: len(group)]))
            columns = columns[len(group) :]
        return results
    vmem = pl.BlockSpec(memory_space=pltpu.VMEM)
    return pl.pallas_call(
        functools.partial(arrange_kernel, pair),
        out_shape=[jax.ShapeDtypeStruct((len(group), unit, pair), weight.dtype) for group in groups],
        in_specs=[pl.BlockSpec(memory_space=pltpu.SMEM), vmem],
        out_specs=[vmem] * len(groups),
        compiler_params=pltpu.CompilerParams(vmem_limit_bytes=16 * 1024 * 1024),
        name="arrange_weight",
    )(jnp.stack(heads).astype(jnp.int32), weight)


def norm_kernel(width, starts_ref, hidden_ref, gain_ref, extra_ref, *refs):
    out_refs, normed = refs[:-1], refs[-1]
    rows = hidden_ref.shape[0]
    hidden = hidden_ref[...].astype(F32)
    inverse = lax.rsqrt(jnp.mean(hidden * hidden, axis=1, keepdims=True) + EPSILON)
    normed[...] = (hidden * inverse * gain_ref[...]).astype(BF16)
    number = 0
    for out_ref in out_refs:
        for place in range(out_ref.shape[1] // width):
            start = pl.multiple_of(starts_ref[number] * width, 128)
            out_ref[:rows, place * width : (place + 1) * width] = normed[:, pl.ds(start, width)]
            number += 1
        out_ref[rows:, :] = extra_ref[...]


def normed_features(hidden, gain, groups, width, extra):
    rows, depth = hidden.shape
    if width % 128 or rows % 16 or extra.shape[0] % 16:
        hidden_float = hidden.astype(F32)
        inverse = lax.rsqrt(jnp.mean(hidden_float * hidden_float, axis=1, keepdims=True) + EPSILON)
        normed = (hidden_float * inverse * gain[None, :]).astype(BF16)
        return [
            jnp.concatenate(
                [
                    jnp.concatenate(
                        [
                            lax.dynamic_slice_in_dim(normed, block * width, width, 1)
                            for block in group
                        ],
                        axis=1,
                    ),
                    extra,
                ],
                axis=0,
            )
            for group in groups
        ]
    blocks = [block for group in groups for block in group]
    vmem = pl.BlockSpec(memory_space=pltpu.VMEM)
    return pl.pallas_call(
        functools.partial(norm_kernel, width),
        out_shape=[
            jax.ShapeDtypeStruct((rows + extra.shape[0], len(group) * width), BF16)
            for group in groups
        ],
        in_specs=[pl.BlockSpec(memory_space=pltpu.SMEM), vmem, vmem, vmem],
        out_specs=[vmem] * len(groups),
        scratch_shapes=[pltpu.VMEM((rows, depth), BF16)],
        compiler_params=pltpu.CompilerParams(vmem_limit_bytes=32 * 1024 * 1024),
        name="norm_hidden",
    )(jnp.stack(blocks).astype(jnp.int32), hidden, gain[None, :], extra)


def project_kernel(rows, first_ref, mine_ref, theirs_ref, *refs):
    out_ref, weight = refs[-2:]
    blocks = refs[:-2]
    unit = blocks[0].shape[1]
    for head in range(out_ref.shape[0]):
        for tile in range(len(blocks) // 2):
            base = 2 * unit * tile
            first = pl.multiple_of(base + first_ref[tile] * unit, unit)
            second = pl.multiple_of(base + (1 - first_ref[tile]) * unit, unit)
            weight[pl.ds(first, unit), :] = blocks[2 * tile][head]
            weight[pl.ds(second, unit), :] = blocks[2 * tile + 1][head]
        for half, tokens_ref in enumerate((mine_ref, theirs_ref)):
            tokens = tokens_ref[:, :rows, :].reshape(-1, tokens_ref.shape[2])
            result = jnp.dot(tokens, weight[...], preferred_element_type=F32)
            out_ref[head, half] = result.astype(BF16).reshape(out_ref.shape[2:])


def projected(mine, theirs, blocks, rows):
    heads, unit, pair = blocks[0][0].shape
    depth = mine.shape[2]
    shape = (heads, 2, CHIPS, rows, pair)
    if unit % 16 or rows % 16:
        ordered = [
            jnp.where(first == 0, a, b) for one, two, first in blocks for a, b in ((one, two), (two, one))
        ]
        weight = jnp.concatenate(ordered, axis=1)
        tokens = jnp.stack([mine[:, :rows], theirs[:, :rows]])
        result = jnp.einsum("epsd,hdc->hepsc", tokens, weight, preferred_element_type=F32)
        return list(result.astype(BF16))
    vmem = pl.BlockSpec(memory_space=pltpu.VMEM)
    pieces = [piece for one, two, _ in blocks for piece in (one, two)]
    return list(
        pl.pallas_call(
            functools.partial(project_kernel, rows),
            out_shape=jax.ShapeDtypeStruct(shape, BF16),
            in_specs=[pl.BlockSpec(memory_space=pltpu.SMEM)] + [vmem] * (2 + len(pieces)),
            out_specs=vmem,
            scratch_shapes=[pltpu.VMEM((depth, pair), BF16)],
            compiler_params=pltpu.CompilerParams(vmem_limit_bytes=40 * 1024 * 1024),
            cost_estimate=pl.CostEstimate(
                flops=2 * heads * 2 * CHIPS * rows * depth * pair,
                bytes_accessed=4 * CHIPS * rows * depth,
                transcendentals=0,
            ),
            name="project",
        )(jnp.stack([first for _, _, first in blocks]).astype(jnp.int32), mine, theirs, *pieces)
    )


def in_order(ours, theirs, core):
    low, high = jnp.where(core == 0, ours, theirs), jnp.where(core == 0, theirs, ours)
    return jnp.stack([low, high], axis=1).reshape(-1, ours.shape[-1])


def key_values_of(hidden, kv_gain, kv_weight, query_states):
    lane_count = lax.axis_size("row")
    tile_count = lane_count // KVH
    me = lax.axis_index("row")
    tile, chip, core = me // KVH, me // 2 % CHIPS, me % 2
    rows = hidden.shape[0]
    unit = kv_weight.shape[0]
    pair = 2 * HD
    share = lax.axis_size("groups") == 2
    part = lax.axis_index("groups") if share else 0

    order = [place for round_ in ROUNDS for place in round_]
    heads = {place: (chip ^ place) * 2 + core for place in order}
    others = {place: (chip ^ place) * 2 + 1 - core for place in order}
    sent = [[heads[place] ^ part for place in round_] for round_ in ROUNDS]
    pieces = arranged(
        kv_weight, sent + [[others[p] for p in order], [heads[p] for p in order]], pair
    )
    sent, traded, kept = pieces[: len(ROUNDS)], pieces[-2], pieces[-1]

    def to_tile(value, j, flip):
        if not share:
            return swapped(value, j * KVH)
        pairs = [
            (g * lane_count + d, g * lane_count + (d ^ (j * KVH) ^ (g if flip else 0)))
            for g in range(2)
            for d in range(lane_count)
        ]
        return lax.ppermute(value, ("groups", "row"), pairs)

    far = [[to_tile(value, j, True) for j in range(1, tile_count)] for value in sent]
    traded = swapped(traded, 1)

    width = 2 * unit
    features = normed_features(
        hidden,
        kv_gain,
        [
            [(tile ^ j) * CHIPS + (chip ^ place) for j in range(tile_count)]
            for place in range(CHIPS)
        ],
        width,
        query_states.reshape(-1, tile_count * width),
    )
    held = [features[0]] + [swapped(features[p], 2 * p) for p in range(1, CHIPS)]
    mine = jnp.stack(held)
    mine, far[0] = lax.optimization_barrier((mine, far[0]))
    theirs = swapped(mine, 1)
    ours, others = (
        jnp.stack(natural([value[p, rows:].reshape(query_states.shape) for p in range(CHIPS)], chip))
        for value in (mine, theirs)
    )
    stream = in_order(ours, others, core)

    total = None
    done = 0
    for number, round_ in enumerate(ROUNDS):
        span = slice(done, done + len(round_))
        done += len(round_)
        blocks = [(kept[span], traded[span], core)]
        for j, value in enumerate(far[number], 1):
            if share:
                blocks.append((value, swapped(value, 1, "groups"), core ^ part))
            else:
                blocks.append((value, to_tile(traded[span], j, False), core))
        partials = projected(mine, theirs, blocks, rows)
        for partial, place in zip(partials, round_):
            if place:
                partial = swapped(partial, 2 * place)
            pieces = jnp.stack([partial[:, j ^ place] for j in range(CHIPS)], axis=1).astype(F32)
            total = pieces if total is None else total + pieces
    key_values = total.astype(BF16).reshape(2 * CHIPS * rows, pair)
    sources = jnp.stack(
        [tile * KVH + (chip ^ j) * 2 + (core ^ e) for e in range(2) for j in range(CHIPS)]
    )
    key_pos = (sources[:, None] * rows + jnp.arange(rows, dtype=jnp.int32)[None, :]).reshape(-1)
    return key_values, key_pos, stream


def gather_rows(own):
    me = lax.axis_index("row")
    chip, core = me // 2 % CHIPS, me % 2
    chips = [own] + [swapped(own, 2 * place) for place in range(1, CHIPS)]
    ours = jnp.stack(natural(chips, chip))
    return in_order(ours, swapped(ours, 1), core)


def scatter_rows(update, rows):
    me = lax.axis_index("row")
    chip, core = me // 2 % CHIPS, me % 2
    split = update.reshape(CHIPS, 2, rows, update.shape[1])
    kept = jnp.where(core == 0, split[:, 0], split[:, 1])
    sent = jnp.where(core == 0, split[:, 1], split[:, 0])
    both = kept + swapped(sent.astype(BF16), 1).astype(F32)
    total = lax.dynamic_index_in_dim(both, chip, 0, keepdims=False)
    for place in range(1, CHIPS):
        piece = lax.dynamic_index_in_dim(both, chip ^ place, 0, keepdims=False)
        total = total + swapped(piece.astype(BF16), 2 * place).astype(F32)
    return total


def attend_rows(queries, query_pos, query_floor, key_values, key_pos):
    row_count = queries.shape[0]
    head_count = queries.shape[1] // HD
    key_part = key_values[:, :HD]
    value_part = key_values[:, HD:]
    grouped = queries.reshape(row_count, head_count, HD)
    scores = jnp.einsum("rhd,kd->rhk", grouped, key_part, preferred_element_type=F32) * HD ** (-0.5)
    capped = CAP * jnp.tanh(scores / CAP)
    visible = (key_pos[None, :] <= query_pos[:, None]) & (key_pos[None, :] >= query_floor[:, None])
    weights = jnp.where(visible[:, None, :], jnp.exp(capped), 0.0)
    totals = jnp.sum(weights, axis=2)
    weighted = jnp.einsum(
        "rhk,kd->rhd", weights.astype(BF16), value_part, preferred_element_type=F32
    )
    return weighted.reshape(row_count, head_count * HD), totals


def on_device(
    hidden, kv_gain, kv_weight, query_states, query_gain, query_weight, output_weight, block_bounds
):
    tile_count = lax.axis_size("row") // KVH
    tile = lax.axis_index("row") // KVH
    depth = hidden.shape[1]
    slice_depth = query_weight.shape[2]
    query_count = query_states.shape[1]
    row_number = jnp.arange(query_count, dtype=jnp.int32)
    query_pos = jnp.repeat(block_bounds[:, 1], QBLK) + row_number % QBLK
    query_floor = jnp.repeat(block_bounds[:, 0], QBLK)

    key_values, key_pos, stream = key_values_of(hidden, kv_gain, kv_weight, query_states)
    own_rows = query_states
    for section in range(query_gain.shape[0]):
        if section:
            stream = gather_rows(own_rows)
        stream = stream.astype(F32)
        squares = jnp.sum(stream * stream, axis=0)
        gain = lax.dynamic_slice_in_dim(query_gain[section], tile * slice_depth, slice_depth)
        scaled = (stream * gain[:, None]).astype(BF16)
        partial = lax.dot_general(
            scaled, query_weight[section, 0], (((0,), (0,)), ((), ())), preferred_element_type=F32
        )
        square_sum = sum(over_tiles(squares.astype(BF16), tile_count)[1:], squares)
        query_sum = sum(over_tiles(partial.astype(BF16), tile_count)[1:], partial)
        inverse = lax.rsqrt(square_sum / depth + EPSILON)
        queries = (query_sum * inverse[:, None]).astype(BF16)
        weighted, totals = attend_rows(queries, query_pos, query_floor, key_values, key_pos)
        total_sum = sum(over_tiles(totals.astype(BF16), tile_count)[1:], totals)
        weighted_sum = sum(over_tiles(weighted.astype(BF16), tile_count)[1:], weighted)
        attended = (
            (weighted_sum.reshape(query_count, QPK, HD) / total_sum[:, :, None])
            .reshape(query_count, QPK * HD)
            .astype(BF16)
        )
        update = lax.dot_general(
            output_weight[section, 0], attended, (((1,), (1,)), ((), ())), preferred_element_type=F32
        )
        own_rows = (
            own_rows.astype(F32) + scatter_rows(update, own_rows.shape[0])
        ).astype(BF16)
    return own_rows


def solution(mesh):
    in_specs = (
        P(("groups", "row"), None),
        P(),
        P("row", None),
        P("row", "groups"),
        P(),
        P(None, "row", None, None),
        P(None, "row", None, None),
        P("groups", None),
    )
    return jax.shard_map(
        on_device, mesh=mesh, in_specs=in_specs, out_specs=P("row", "groups"), check_vma=False
    )
```

```python
import functools

import jax
import jax.numpy as jnp
from jax import lax
from jax.experimental import pallas as pl
from jax.experimental.pallas import tpu as pltpu
from jax.sharding import PartitionSpec as P

KVH = 8
HD = 128
QPK = 5
QBLK = 64
CAP = 30.0
EPSILON = 1e-05
BF16 = jnp.bfloat16
F32 = jnp.float32

CHIPS = KVH // 2
ROUNDS = ((1, 2), (3, 0))
PROJECT_COST = 8


def swapped(value, mask, axis="row"):
    pairs = [(source, source ^ mask) for source in range(lax.axis_size(axis))]
    return lax.ppermute(value, axis, pairs)


def over_tiles(value, tile_count):
    values = [value]
    mask = 1
    while mask < tile_count:
        if len(values) == 1:
            values.append(swapped(values[0], mask * KVH))
        else:
            got = swapped(jnp.stack(values), mask * KVH)
            values.extend(got[place] for place in range(len(values)))
        mask *= 2
    return values


def natural(pieces, index):
    pieces = list(pieces)
    bit = 1
    while bit < len(pieces):
        upper = index // bit % 2 == 1
        pieces = [jnp.where(upper, pieces[j ^ bit], pieces[j]) for j in range(len(pieces))]
        bit *= 2
    return pieces


def prepare_kernel(
    pair, counts, width, heads_ref, starts_ref, weight_any, hidden_any, gain_any, extra_any, *refs
):
    weight_ref, hidden_ref, gain_ref, extra_ref, normed, sems = refs[-6:]
    head_refs, out_refs = refs[: len(counts)], refs[len(counts) : -6]
    rows = hidden_ref.shape[0]
    lanes = extra_ref.shape[1]
    more = out_refs[0].shape[0] - rows
    copies = [
        pltpu.make_async_copy(source, target, sems.at[number])
        for number, (source, target) in enumerate(
            (
                (weight_any, weight_ref),
                (hidden_any, hidden_ref),
                (gain_any, gain_ref),
                (extra_any, extra_ref),
            )
        )
    ]
    for copy in copies:
        copy.start()
    copies[0].wait()
    number = 0
    for head_ref in head_refs:
        for place in range(head_ref.shape[0]):
            column = pl.multiple_of(heads_ref[number] * pair, pair)
            head_ref[place] = weight_ref[:, pl.ds(column, pair)]
            number += 1
    for copy in copies[1:]:
        copy.wait()
    hidden = hidden_ref[...].astype(F32)
    inverse = lax.rsqrt(jnp.mean(hidden * hidden, axis=1, keepdims=True) + EPSILON)
    normed[...] = (hidden * inverse * gain_ref[...]).astype(BF16)
    number = 0
    for out_ref in out_refs:
        for place in range(out_ref.shape[1] // width):
            start = pl.multiple_of(starts_ref[number] * width, 128)
            out_ref[:rows, place * width : (place + 1) * width] = normed[:, pl.ds(start, width)]
            number += 1
        for block in range(out_ref.shape[1] // lanes):
            out_ref[rows:, block * lanes : (block + 1) * lanes] = extra_ref[
                block * more : (block + 1) * more, :
            ]


def in_kernels(unit, rows):
    return unit % 64 == 0 and rows % 16 == 0


def prepared(weight, head_groups, pair, hidden, gain, groups, width, extra, kernels):
    rows, depth = hidden.shape
    total_width = len(groups[0]) * width
    more = extra.size // total_width
    if not kernels:
        columns = [
            jnp.stack([lax.dynamic_slice_in_dim(weight, head * pair, pair, 1) for head in group])
            for group in head_groups
        ]
        hidden_float = hidden.astype(F32)
        inverse = lax.rsqrt(jnp.mean(hidden_float * hidden_float, axis=1, keepdims=True) + EPSILON)
        normed = (hidden_float * inverse * gain[None, :]).astype(BF16)
        results = []
        for group in groups:
            blocks = [lax.dynamic_slice_in_dim(normed, block * width, width, 1) for block in group]
            rest = extra.reshape(more, total_width)
            results.append(jnp.concatenate([jnp.concatenate(blocks, axis=1), rest], axis=0))
        return columns, results
    counts = [len(group) for group in head_groups]
    vmem = pl.BlockSpec(memory_space=pltpu.VMEM)
    smem = pl.BlockSpec(memory_space=pltpu.SMEM)
    results = pl.pallas_call(
        functools.partial(prepare_kernel, pair, counts, width),
        out_shape=[jax.ShapeDtypeStruct((count, weight.shape[0], pair), BF16) for count in counts]
        + [jax.ShapeDtypeStruct((rows + more, total_width), BF16) for group in groups],
        in_specs=[smem, smem] + [pl.BlockSpec(memory_space=pltpu.HBM)] * 4,
        out_specs=[vmem] * (len(counts) + len(groups)),
        scratch_shapes=[
            pltpu.VMEM(weight.shape, BF16),
            pltpu.VMEM((rows, depth), BF16),
            pltpu.VMEM((1, depth), F32),
            pltpu.VMEM(extra.shape, BF16),
            pltpu.VMEM((rows, depth), BF16),
            pltpu.SemaphoreType.DMA((4,)),
        ],
        compiler_params=pltpu.CompilerParams(vmem_limit_bytes=60 * 1024 * 1024),
        name="prepare",
    )(
        jnp.stack([head for group in head_groups for head in group]).astype(jnp.int32),
        jnp.stack([block for group in groups for block in group]).astype(jnp.int32),
        weight,
        hidden,
        gain[None, :],
        extra,
    )
    return results[: len(counts)], results[len(counts) :]


def project_kernel(rows, heads, pair, start, first_ref, heads_ref, weight_any, traded_ref, *refs):
    token_refs, refs = refs[: 2 * CHIPS], refs[2 * CHIPS :]
    own, weight, sem = refs[-3:]
    out_refs = refs[-3 - heads : -3]
    blocks = refs[: -3 - heads]
    unit = own.shape[0]
    get_own = pltpu.make_async_copy(weight_any, own, sem)
    get_own.start()

    def put(head, tile, second, value):
        which = 1 - first_ref[tile] if second else first_ref[tile]
        base = pl.multiple_of(2 * unit * tile + which * unit, unit)
        weight[pl.ds(base, unit), head * pair : (head + 1) * pair] = value

    for head in range(heads):
        put(head, 0, 1, traded_ref[start + head])
        for number, block_ref in enumerate(blocks):
            put(head, 1 + number // 2, number % 2, block_ref[head])
    get_own.wait()
    for head in range(heads):
        column = pl.multiple_of(heads_ref[head] * pair, pair)
        put(head, 0, 0, own[:, pl.ds(column, pair)])
    for number, token_ref in enumerate(token_refs):
        span = slice(number * rows, (number + 1) * rows)
        result = jnp.dot(token_ref[:rows, :], weight[...], preferred_element_type=F32).astype(BF16)
        for head, out_ref in enumerate(out_refs):
            out_ref[span, :] = result[:, head * pair : (head + 1) * pair]


def projected(tokens, heads, pair, kv_weight, traded, start, firsts, blocks, rows, kernels):
    unit, depth = kv_weight.shape[0], tokens[0].shape[1]
    count = len(tokens) * rows
    firsts = jnp.stack(firsts).astype(jnp.int32)
    if not kernels:
        kept = jnp.stack([lax.dynamic_slice_in_dim(kv_weight, h * pair, pair, 1) for h in heads])
        pieces = [kept, traded[start : start + len(heads)]] + blocks
        ordered = []
        for tile in range(len(pieces) // 2):
            one, two = pieces[2 * tile : 2 * tile + 2]
            first = firsts[tile] == 0
            ordered += [jnp.where(first, one, two), jnp.where(first, two, one)]
        weight = jnp.concatenate(ordered, axis=1)
        tokens = jnp.concatenate([piece[:rows] for piece in tokens])
        result = jnp.einsum("td,hdc->htc", tokens, weight, preferred_element_type=F32)
        return list(result.astype(BF16))
    vmem = pl.BlockSpec(memory_space=pltpu.VMEM)
    smem = pl.BlockSpec(memory_space=pltpu.SMEM)
    return list(
        pl.pallas_call(
            functools.partial(project_kernel, rows, len(heads), pair, start),
            out_shape=[jax.ShapeDtypeStruct((count, pair), BF16)] * len(heads),
            in_specs=[smem, smem, pl.BlockSpec(memory_space=pltpu.HBM), vmem]
            + [vmem] * (len(tokens) + len(blocks)),
            out_specs=[vmem] * len(heads),
            scratch_shapes=[
                pltpu.VMEM(kv_weight.shape, BF16),
                pltpu.VMEM((depth, len(heads) * pair), BF16),
                pltpu.SemaphoreType.DMA,
            ],
            compiler_params=pltpu.CompilerParams(vmem_limit_bytes=20 * 1024 * 1024),
            cost_estimate=pl.CostEstimate(
                flops=PROJECT_COST * 2 * len(heads) * count * depth * pair,
                bytes_accessed=2 * count * depth,
                transcendentals=0,
            ),
            name="project",
        )(firsts, jnp.stack(heads).astype(jnp.int32), kv_weight, traded, *tokens, *blocks)
    )


def query_kernel(lanes, place_ref, gain_ref, weight_ref, *refs):
    piece_refs, refs = refs[:-7], refs[-7:]
    sent_ref, kept_ref, squares_sent_ref, squares_ref, stream, parts, sems = refs
    unit = stream.shape[0] // KVH
    more = parts.shape[1]
    blocks = parts.shape[2] // lanes
    sources = [
        piece_ref.at[place] if len(piece_ref.shape) == 3 else piece_ref
        for piece_ref in piece_refs
        for place in range(CHIPS if len(piece_ref.shape) == 3 else 1)
    ]
    bases = [
        pl.multiple_of(
            ((place_ref[0] ^ number % CHIPS) * 2 + (place_ref[1] ^ number // CHIPS)) * unit, unit
        )
        for number in range(KVH)
    ]
    packed = sources[0].shape[1] != lanes
    copies = []
    for number, source in enumerate(sources):
        if packed:
            source, target = source.at[source.shape[0] - more :], parts.at[number]
        else:
            target = stream.at[pl.ds(bases[number], unit)]
        copies.append(pltpu.make_async_copy(source, target, sems.at[number]))
        copies[-1].start()
    for number, copy in enumerate(copies):
        copy.wait()
        for block in range(blocks if packed else 0):
            stream[pl.ds(pl.multiple_of(bases[number] + block * more, more), more), :] = parts[
                number, :, block * lanes : (block + 1) * lanes
            ]
    rows = stream[...].astype(F32).T
    squares = jnp.sum(rows * rows, axis=1, keepdims=True)
    scaled = (rows * gain_ref[...]).astype(BF16)
    partial = jnp.dot(scaled, weight_ref[...], preferred_element_type=F32)
    kept_ref[...] = partial
    sent_ref[...] = partial.astype(BF16)
    spread = jnp.broadcast_to(squares, (lanes, lanes))
    squares_ref[...] = spread
    across = spread.T[:8]
    high = across.astype(BF16)
    squares_sent_ref[:8] = high
    squares_sent_ref[8:] = (across - high.astype(F32)).astype(BF16)


def spread_back(pair_ref, lanes):
    across = pair_ref[:8].astype(F32) + pair_ref[8:].astype(F32)
    return jnp.concatenate([across, jnp.zeros((lanes - 8, lanes), F32)], axis=0).T


def attend_kernel(depth, others, query_pos_ref, query_floor_ref, key_pos_ref, kv_ref, *refs):
    kept_ref, squares_ref = refs[:2]
    far = refs[2 : 2 + 2 * others]
    sent_ref, out_ref, totals_sent_ref, totals_ref = refs[2 + 2 * others :]
    lanes = kept_ref.shape[0]
    queries = kept_ref[...]
    squares = squares_ref[:, :1]
    for other in range(others):
        queries = queries + far[2 * other][...].astype(F32)
        squares = squares + spread_back(far[2 * other + 1], lanes)[:, :1]
    queries = (queries * lax.rsqrt(squares / depth + EPSILON)).astype(BF16)
    visible = (key_pos_ref[...] <= query_pos_ref[...]) & (key_pos_ref[...] >= query_floor_ref[...])
    keys, values = kv_ref[:, :HD], kv_ref[:, HD:]
    lane = lax.broadcasted_iota(jnp.int32, (lanes, lanes), 1)
    totals = jnp.zeros((lanes, lanes), F32)
    for head in range(queries.shape[1] // HD):
        span = slice(head * HD, (head + 1) * HD)
        scores = lax.dot_general(
            queries[:, span], keys, (((1,), (1,)), ((), ())), preferred_element_type=F32
        ) * HD ** (-0.5)
        weights = jnp.where(visible, jnp.exp(CAP * jnp.tanh(scores / CAP)), 0.0)
        totals = jnp.where(lane == head, jnp.sum(weights, axis=1, keepdims=True), totals)
        weighted = jnp.dot(weights.astype(BF16), values, preferred_element_type=F32)
        out_ref[:, span] = weighted
        sent_ref[:, span] = weighted.astype(BF16)
    totals_ref[...] = totals
    across = totals.T[:8]
    high = across.astype(BF16)
    totals_sent_ref[:8] = high
    totals_sent_ref[8:] = (across - high.astype(F32)).astype(BF16)


def update_kernel(others, place_ref, weight_ref, kept_ref, totals_ref, *refs):
    far, (own_ref, sent_ref) = refs[: 2 * others], refs[2 * others :]
    lanes = kept_ref.shape[0]
    unit = own_ref.shape[1]
    weighted = kept_ref[...]
    totals = totals_ref[...]
    for other in range(others):
        weighted = weighted + far[2 * other][...].astype(F32)
        totals = totals + spread_back(far[2 * other + 1], lanes)
    attended = jnp.concatenate(
        [
            (weighted[:, head * HD : (head + 1) * HD] / totals[:, head : head + 1]).astype(BF16)
            for head in range(weighted.shape[1] // HD)
        ],
        axis=1,
    )
    for core, out_ref in enumerate((own_ref, sent_ref)):
        for chip in range(CHIPS):
            base = ((place_ref[0] ^ chip) * 2 + (place_ref[1] ^ core)) * unit
            update = lax.dot_general(
                weight_ref[pl.ds(pl.multiple_of(base, unit), unit), :],
                attended,
                (((1,), (1,)), ((), ())),
                preferred_element_type=F32,
            )
            out_ref[chip] = update.astype(out_ref.dtype)


def call(kernel, name, out_shape, scalars, arrays, scratch=(), flops=0, loose=()):
    vmem = pl.BlockSpec(memory_space=pltpu.VMEM)
    smem = pl.BlockSpec(memory_space=pltpu.SMEM)
    return pl.pallas_call(
        kernel,
        out_shape=out_shape,
        in_specs=[smem] * len(scalars)
        + [vmem] * len(arrays)
        + [pl.BlockSpec(memory_space=pl.ANY)] * len(loose),
        out_specs=[vmem] * len(out_shape),
        scratch_shapes=list(scratch),
        compiler_params=pltpu.CompilerParams(vmem_limit_bytes=20 * 1024 * 1024),
        cost_estimate=pl.CostEstimate(
            flops=flops, bytes_accessed=sum(2 * a.size for a in arrays), transcendentals=0
        ),
        name=name,
    )(*scalars, *arrays, *loose)


def in_order(ours, theirs, core):
    low, high = jnp.where(core == 0, ours, theirs), jnp.where(core == 0, theirs, ours)
    return jnp.stack([low, high], axis=1).reshape(-1, ours.shape[-1])


def key_values_of(hidden, kv_gain, kv_weight, query_states, meanwhile):
    lane_count = lax.axis_size("row")
    tile_count = lane_count // KVH
    me = lax.axis_index("row")
    tile, chip, core = me // KVH, me // 2 % CHIPS, me % 2
    rows = hidden.shape[0]
    unit = kv_weight.shape[0]
    pair = 2 * HD
    share = lax.axis_size("groups") == 2
    part = lax.axis_index("groups") if share else 0

    order = [place for round_ in ROUNDS for place in round_]
    heads = {place: (chip ^ place) * 2 + core for place in order}
    others = {place: (chip ^ place) * 2 + 1 - core for place in order}
    sent = [[heads[place] ^ part for place in round_] for round_ in ROUNDS]
    kernels = in_kernels(unit, rows)
    width = 2 * unit
    pieces, features = prepared(
        kv_weight,
        sent + [[others[p] for p in order]],
        pair,
        hidden,
        kv_gain,
        [
            [(tile ^ j) * CHIPS + (chip ^ place) for j in range(tile_count)]
            for place in range(CHIPS)
        ],
        width,
        query_states,
        kernels,
    )
    sent, traded = pieces[:-1], pieces[-1]

    def to_tile(value, j, flip):
        if not share:
            return swapped(value, j * KVH)
        pairs = [
            (g * lane_count + d, g * lane_count + (d ^ (j * KVH) ^ (g if flip else 0)))
            for g in range(2)
            for d in range(lane_count)
        ]
        return lax.ppermute(value, ("groups", "row"), pairs)

    far = [[to_tile(value, j, True) for j in range(1, tile_count)] for value in sent]
    held = [features[0]] + [swapped(features[p], 2 * p) for p in range(1, CHIPS)]

    traded, held[1] = lax.optimization_barrier((traded, held[1]))
    traded = swapped(traded, 1)

    def shared(number):
        blocks = []
        for j, value in enumerate(far[number], 1):
            other = swapped(value, 1, "groups") if share else to_tile(traded[number], j, False)
            blocks += [value, other]
        return blocks

    firsts = [core] + [core ^ part] * (tile_count - 1)
    blocks = shared(0)
    held[2], held[3], blocks, far = lax.optimization_barrier((held[2], held[3], blocks, far))
    tokens = held + [swapped(piece, 1) for piece in held]
    total = None
    done = 0
    for number, round_ in enumerate(ROUNDS):
        if number:
            blocks = shared(number)
        here = [heads[place] for place in round_]
        partials = projected(
            tokens, here, pair, kv_weight, traded, done, firsts, blocks, rows, kernels
        )
        done += len(round_)
        if number == 0:
            partials, tokens = lax.optimization_barrier((partials, tokens))
            results = meanwhile(tokens)
        for partial, place in zip(partials, round_):
            if place:
                partial = swapped(partial, 2 * place)
            pieces = partial.reshape(2, CHIPS, rows, pair).astype(F32)
            pieces = jnp.stack([pieces[:, j ^ place] for j in range(CHIPS)], axis=1)
            total = pieces if total is None else total + pieces
    key_values = total.astype(BF16).reshape(2 * CHIPS * rows, pair)
    sources = jnp.stack(
        [tile * KVH + (chip ^ j) * 2 + (core ^ e) for e in range(2) for j in range(CHIPS)]
    )
    key_pos = (sources[:, None] * rows + jnp.arange(rows, dtype=jnp.int32)[None, :]).reshape(-1)
    return key_values, key_pos, results


def gather_rows(own):
    ours = [own] + [swapped(own, 2 * place) for place in range(1, CHIPS)]
    theirs = swapped(jnp.stack(ours), 1)
    return ours + [theirs]


def scatter_rows(kept, sent):
    both = kept + swapped(sent, 1).astype(F32)
    total = both[0]
    for place in range(1, CHIPS):
        total = total + swapped(both[place].astype(BF16), 2 * place).astype(F32)
    return total


def attend_rows(queries, query_pos, query_floor, key_values, key_pos):
    row_count = queries.shape[0]
    head_count = queries.shape[1] // HD
    key_part = key_values[:, :HD]
    value_part = key_values[:, HD:]
    grouped = queries.reshape(row_count, head_count, HD)
    scores = jnp.einsum("rhd,kd->rhk", grouped, key_part, preferred_element_type=F32) * HD ** (-0.5)
    capped = CAP * jnp.tanh(scores / CAP)
    visible = (key_pos[None, :] <= query_pos[:, None]) & (key_pos[None, :] >= query_floor[:, None])
    weights = jnp.where(visible[:, None, :], jnp.exp(capped), 0.0)
    totals = jnp.sum(weights, axis=2)
    weighted = jnp.einsum(
        "rhk,kd->rhd", weights.astype(BF16), value_part, preferred_element_type=F32
    )
    return weighted.reshape(row_count, head_count * HD), totals


def on_device(
    hidden, kv_gain, kv_weight, query_states, query_gain, query_weight, output_weight, block_bounds
):
    tile_count = lax.axis_size("row") // KVH
    tile = lax.axis_index("row") // KVH
    depth = hidden.shape[1]
    slice_depth = query_weight.shape[2]
    query_count = query_states.shape[1]
    row_number = jnp.arange(query_count, dtype=jnp.int32)
    query_pos = jnp.repeat(block_bounds[:, 1], QBLK) + row_number % QBLK
    query_floor = jnp.repeat(block_bounds[:, 0], QBLK)

    me = lax.axis_index("row")
    chip, core = me // 2 % CHIPS, me % 2
    place_now = jnp.stack([chip, core]).astype(jnp.int32)
    unit, rows = query_states.shape[0], hidden.shape[0]
    kernels = in_kernels(unit, rows)
    width = query_weight.shape[3]
    own_rows = query_states
    small = jax.ShapeDtypeStruct((16, query_count), BF16)
    spread = jax.ShapeDtypeStruct((query_count, query_count), F32)
    wide = [jax.ShapeDtypeStruct((query_count, width), kind) for kind in (BF16, F32)]
    flops = 2 * query_count * slice_depth * width

    def query_parts(section, pieces):
        gain = lax.dynamic_slice_in_dim(query_gain[section], tile * slice_depth, slice_depth)
        if not kernels:
            pieces = [
                part
                for piece in pieces
                for part in (piece if piece.ndim == 3 else [piece[-(own_rows.size // piece.shape[1]) :]])
            ]
            pieces = [piece.reshape(own_rows.shape) for piece in pieces]
            ours, theirs = (
                jnp.stack(natural(half, chip)) for half in (pieces[:CHIPS], pieces[CHIPS:])
            )
            stream = in_order(ours, theirs, core).astype(F32)
            scaled = (stream * gain[:, None]).astype(BF16)
            partial = lax.dot_general(
                scaled, query_weight[section, 0], (((0,), (0,)), ((), ())), preferred_element_type=F32
            )
            squares = jnp.sum(stream * stream, axis=0)
            return partial.astype(BF16), partial, squares.astype(BF16), squares
        return call(
            functools.partial(query_kernel, query_count),
            "query",
            wide + [small, spread],
            [place_now],
            [gain[None, :], query_weight[section, 0]],
            [
                pltpu.VMEM((slice_depth, query_count), BF16),
                pltpu.VMEM((KVH, own_rows.size // (2 * unit * tile_count), 2 * unit * tile_count), BF16),
                pltpu.SemaphoreType.DMA((KVH,)),
            ],
            flops,
            pieces,
        )

    key_values, key_pos, parts = key_values_of(
        hidden, kv_gain, kv_weight, query_states, functools.partial(query_parts, 0)
    )
    positions = [query_pos[:, None], query_floor[:, None], key_pos[None, :]]
    for section in range(query_gain.shape[0]):
        if section:
            parts = query_parts(section, gather_rows(own_rows))
        sent, partial, squares_sent, squares = parts
        if kernels:
            far = zip(over_tiles(sent, tile_count)[1:], over_tiles(squares_sent, tile_count)[1:])
            sent, weighted, totals_sent, totals = call(
                functools.partial(attend_kernel, depth, tile_count - 1),
                "attend",
                wide + [small, spread],
                [],
                positions + [key_values, partial, squares] + [value for pair in far for value in pair],
                (),
                flops // 2,
            )
            far = zip(over_tiles(sent, tile_count)[1:], over_tiles(totals_sent, tile_count)[1:])
            shape = (CHIPS, unit, query_count)
            kept, sent = call(
                functools.partial(update_kernel, tile_count - 1),
                "update",
                [jax.ShapeDtypeStruct(shape, F32), jax.ShapeDtypeStruct(shape, BF16)],
                [place_now],
                [output_weight[section, 0], weighted, totals]
                + [value for pair in far for value in pair],
                (),
                flops,
            )
        else:
            square_sum = sum(over_tiles(squares_sent, tile_count)[1:], squares)
            query_sum = sum(over_tiles(sent, tile_count)[1:], partial)
            inverse = lax.rsqrt(square_sum / depth + EPSILON)
            queries = (query_sum * inverse[:, None]).astype(BF16)
            weighted, totals = attend_rows(queries, query_pos, query_floor, key_values, key_pos)
            total_sum = sum(over_tiles(totals.astype(BF16), tile_count)[1:], totals)
            weighted_sum = sum(over_tiles(weighted.astype(BF16), tile_count)[1:], weighted)
            attended = (
                (weighted_sum.reshape(query_count, QPK, HD) / total_sum[:, :, None])
                .reshape(query_count, QPK * HD)
                .astype(BF16)
            )
            update = lax.dot_general(
                output_weight[section, 0],
                attended,
                (((1,), (1,)), ((), ())),
                preferred_element_type=F32,
            )
            split = update.reshape(CHIPS, 2, unit, query_count)
            kept = jnp.where(core == 0, split[:, 0], split[:, 1])
            sent = jnp.where(core == 0, split[:, 1], split[:, 0]).astype(BF16)
            kept, sent = (jnp.stack(natural(value, chip)) for value in (kept, sent))
        own_rows = (own_rows.astype(F32) + scatter_rows(kept, sent)).astype(BF16)
    return own_rows


def solution(mesh):
    in_specs = (
        P(("groups", "row"), None),
        P(),
        P("row", None),
        P("row", "groups"),
        P(),
        P(None, "row", None, None),
        P(None, "row", None, None),
        P("groups", None),
    )
    return jax.shard_map(
        on_device, mesh=mesh, in_specs=in_specs, out_specs=P("row", "groups"), check_vma=False
    )
```

```python
import functools

import jax
import jax.numpy as jnp
from jax import lax
from jax.experimental import pallas as pl
from jax.experimental.pallas import tpu as pltpu
from jax.sharding import PartitionSpec as P

KVH = 8
HD = 128
QPK = 5
QBLK = 64
CAP = 30.0
EPSILON = 1e-05
BF16 = jnp.bfloat16
F32 = jnp.float32

CHIPS = KVH // 2
ROUNDS = ((1, 2), (3, 0))
PROJECT_COST = 8


def swapped(value, mask, axis="row"):
    pairs = [(source, source ^ mask) for source in range(lax.axis_size(axis))]
    return lax.ppermute(value, axis, pairs)


def over_tiles(value, tile_count):
    values = [value]
    mask = 1
    while mask < tile_count:
        if len(values) == 1:
            values.append(swapped(values[0], mask * KVH))
        else:
            got = swapped(jnp.stack(values), mask * KVH)
            values.extend(got[place] for place in range(len(values)))
        mask *= 2
    return values


def natural(pieces, index):
    pieces = list(pieces)
    bit = 1
    while bit < len(pieces):
        upper = index // bit % 2 == 1
        pieces = [jnp.where(upper, pieces[j ^ bit], pieces[j]) for j in range(len(pieces))]
        bit *= 2
    return pieces


def prepare_kernel(
    pair, heads, blocks, width, place_ref, weight_any, hidden_any, gain_any, extra_any, *refs
):
    weight_ref, hidden_ref, gain_ref, extra_ref, normed, sems = refs[-6:]
    head_refs, out_refs = refs[: len(heads)], refs[len(heads) : -6]
    place_now = [place_ref[number] for number in range(4)]
    rows = hidden_ref.shape[0]
    lanes = extra_ref.shape[1]
    more = out_refs[0].shape[0] - rows
    copies = [
        pltpu.make_async_copy(source, target, sems.at[number])
        for number, (source, target) in enumerate(
            (
                (weight_any, weight_ref),
                (hidden_any, hidden_ref),
                (gain_any, gain_ref),
                (extra_any, extra_ref),
            )
        )
    ]
    for copy in copies:
        copy.start()
    copies[0].wait()
    for head_ref, group in zip(head_refs, heads):
        for number, head in enumerate(group):
            column = pl.multiple_of(head(*place_now) * pair, pair)
            head_ref[number] = weight_ref[:, pl.ds(column, pair)]
    for copy in copies[1:]:
        copy.wait()
    hidden = hidden_ref[...].astype(F32)
    inverse = lax.rsqrt(jnp.mean(hidden * hidden, axis=1, keepdims=True) + EPSILON)
    normed[...] = (hidden * inverse * gain_ref[...]).astype(BF16)
    for out_ref, group in zip(out_refs, blocks):
        for number, block in enumerate(group):
            start = pl.multiple_of(block(*place_now) * width, 128)
            out_ref[:rows, number * width : (number + 1) * width] = normed[:, pl.ds(start, width)]
        for block in range(out_ref.shape[1] // lanes):
            out_ref[rows:, block * lanes : (block + 1) * lanes] = extra_ref[
                block * more : (block + 1) * more, :
            ]


def in_kernels(unit, rows):
    return unit % 64 == 0 and rows % 16 == 0


def prepared(weight, head_groups, pair, hidden, gain, groups, width, extra, place_now, kernels):
    rows, depth = hidden.shape
    total_width = len(groups[0]) * width
    more = extra.size // total_width
    if not kernels:
        now = [place_now[number] for number in range(4)]
        columns = [
            jnp.stack(
                [lax.dynamic_slice_in_dim(weight, head(*now) * pair, pair, 1) for head in group]
            )
            for group in head_groups
        ]
        hidden_float = hidden.astype(F32)
        inverse = lax.rsqrt(jnp.mean(hidden_float * hidden_float, axis=1, keepdims=True) + EPSILON)
        normed = (hidden_float * inverse * gain[None, :]).astype(BF16)
        results = []
        for group in groups:
            blocks = [
                lax.dynamic_slice_in_dim(normed, block(*now) * width, width, 1) for block in group
            ]
            rest = extra.reshape(more, total_width)
            results.append(jnp.concatenate([jnp.concatenate(blocks, axis=1), rest], axis=0))
        return columns, results
    counts = [len(group) for group in head_groups]
    vmem = pl.BlockSpec(memory_space=pltpu.VMEM)
    smem = pl.BlockSpec(memory_space=pltpu.SMEM)
    results = pl.pallas_call(
        functools.partial(prepare_kernel, pair, head_groups, groups, width),
        out_shape=[jax.ShapeDtypeStruct((count, weight.shape[0], pair), BF16) for count in counts]
        + [jax.ShapeDtypeStruct((rows + more, total_width), BF16) for group in groups],
        in_specs=[smem] + [pl.BlockSpec(memory_space=pltpu.HBM)] * 4,
        out_specs=[vmem] * (len(counts) + len(groups)),
        scratch_shapes=[
            pltpu.VMEM(weight.shape, BF16),
            pltpu.VMEM((rows, depth), BF16),
            pltpu.VMEM((1, depth), F32),
            pltpu.VMEM(extra.shape, BF16),
            pltpu.VMEM((rows, depth), BF16),
            pltpu.SemaphoreType.DMA((4,)),
        ],
        compiler_params=pltpu.CompilerParams(vmem_limit_bytes=60 * 1024 * 1024),
        name="prepare",
    )(
        place_now,
        weight,
        hidden,
        gain[None, :],
        extra,
    )
    return results[: len(counts)], results[len(counts) :]


def stage_kernel(pair, heads, place_ref, weight_ref, tokens_ref, kept_ref, own_ref):
    place_now = [place_ref[number] for number in range(4)]
    for number, head in enumerate(heads):
        column = pl.multiple_of(head(*place_now) * pair, pair)
        kept_ref[number] = weight_ref[:, pl.ds(column, pair)]
    own_ref[...] = tokens_ref[: own_ref.shape[0], :]


def staged(weight, heads, pair, tokens, place_now, kernels):
    if not kernels:
        now = [place_now[number] for number in range(4)]
        columns = [lax.dynamic_slice_in_dim(weight, head(*now) * pair, pair, 1) for head in heads]
        return jnp.stack(columns), tokens
    shapes = [
        jax.ShapeDtypeStruct((len(heads), weight.shape[0], pair), BF16),
        jax.ShapeDtypeStruct(tokens.shape, BF16),
    ]
    return call(
        functools.partial(stage_kernel, pair, heads),
        "stage",
        shapes,
        [place_now],
        [weight, tokens],
    )


def project_kernel(rows, heads, start, first_ref, kept_ref, traded_ref, *refs):
    token_refs, refs = refs[: 2 * CHIPS], refs[2 * CHIPS :]
    weight = refs[-1]
    out_refs = refs[-1 - heads : -1]
    blocks = refs[: -1 - heads]
    unit, pair = kept_ref.shape[1:]

    def put(head, tile, second, value):
        which = 1 - first_ref[tile] if second else first_ref[tile]
        base = pl.multiple_of(2 * unit * tile + which * unit, unit)
        weight[pl.ds(base, unit), head * pair : (head + 1) * pair] = value

    for head in range(heads):
        put(head, 0, 0, kept_ref[start + head])
        put(head, 0, 1, traded_ref[start + head])
        for number, block_ref in enumerate(blocks):
            put(head, 1 + number // 2, number % 2, block_ref[head])
    for number, token_ref in enumerate(token_refs):
        span = slice(number * rows, (number + 1) * rows)
        result = jnp.dot(token_ref[:rows, :], weight[...], preferred_element_type=F32).astype(BF16)
        for head, out_ref in enumerate(out_refs):
            out_ref[span, :] = result[:, head * pair : (head + 1) * pair]


def projected(tokens, heads, kept, traded, start, firsts, blocks, rows, kernels):
    unit, pair = kept.shape[1:]
    depth = tokens[0].shape[1]
    count = len(tokens) * rows
    firsts = jnp.stack(firsts).astype(jnp.int32)
    if not kernels:
        pieces = [kept[start : start + heads], traded[start : start + heads]] + blocks
        ordered = []
        for tile in range(len(pieces) // 2):
            one, two = pieces[2 * tile : 2 * tile + 2]
            first = firsts[tile] == 0
            ordered += [jnp.where(first, one, two), jnp.where(first, two, one)]
        weight = jnp.concatenate(ordered, axis=1)
        tokens = jnp.concatenate([piece[:rows] for piece in tokens])
        result = jnp.einsum("td,hdc->htc", tokens, weight, preferred_element_type=F32)
        return list(result.astype(BF16))
    vmem = pl.BlockSpec(memory_space=pltpu.VMEM)
    smem = pl.BlockSpec(memory_space=pltpu.SMEM)
    return list(
        pl.pallas_call(
            functools.partial(project_kernel, rows, heads, start),
            out_shape=[jax.ShapeDtypeStruct((count, pair), BF16)] * heads,
            in_specs=[smem] + [vmem] * (2 + len(tokens) + len(blocks)),
            out_specs=[vmem] * heads,
            scratch_shapes=[pltpu.VMEM((depth, heads * pair), BF16)],
            compiler_params=pltpu.CompilerParams(vmem_limit_bytes=20 * 1024 * 1024),
            cost_estimate=pl.CostEstimate(
                flops=PROJECT_COST * 2 * heads * count * depth * pair,
                bytes_accessed=2 * count * depth,
                transcendentals=0,
            ),
            name="project",
        )(firsts, kept, traded, *tokens, *blocks)
    )


def query_kernel(lanes, place_ref, gain_ref, weight_ref, *refs):
    piece_refs, refs = refs[:-7], refs[-7:]
    sent_ref, kept_ref, squares_sent_ref, squares_ref, stream, parts, sems = refs
    unit = stream.shape[0] // KVH
    more = parts.shape[1]
    blocks = parts.shape[2] // lanes
    sources = [
        piece_ref.at[place] if len(piece_ref.shape) == 3 else piece_ref
        for piece_ref in piece_refs
        for place in range(CHIPS if len(piece_ref.shape) == 3 else 1)
    ]
    bases = [
        pl.multiple_of(
            ((place_ref[0] ^ number % CHIPS) * 2 + (place_ref[1] ^ number // CHIPS)) * unit, unit
        )
        for number in range(KVH)
    ]
    packed = sources[0].shape[1] != lanes
    copies = []
    for number, source in enumerate(sources):
        if packed:
            source, target = source.at[source.shape[0] - more :], parts.at[number]
        else:
            target = stream.at[pl.ds(bases[number], unit)]
        copies.append(pltpu.make_async_copy(source, target, sems.at[number]))
        copies[-1].start()
    for number, copy in enumerate(copies):
        copy.wait()
        for block in range(blocks if packed else 0):
            stream[pl.ds(pl.multiple_of(bases[number] + block * more, more), more), :] = parts[
                number, :, block * lanes : (block + 1) * lanes
            ]
    rows = stream[...].astype(F32).T
    squares = jnp.sum(rows * rows, axis=1, keepdims=True)
    scaled = (rows * gain_ref[...]).astype(BF16)
    partial = jnp.dot(scaled, weight_ref[...], preferred_element_type=F32)
    kept_ref[...] = partial
    sent_ref[...] = partial.astype(BF16)
    spread = jnp.broadcast_to(squares, (lanes, lanes))
    squares_ref[...] = spread
    across = spread.T[:8]
    high = across.astype(BF16)
    squares_sent_ref[:8] = high
    squares_sent_ref[8:] = (across - high.astype(F32)).astype(BF16)


def spread_back(pair_ref, lanes):
    across = pair_ref[:8].astype(F32) + pair_ref[8:].astype(F32)
    return jnp.concatenate([across, jnp.zeros((lanes - 8, lanes), F32)], axis=0).T


def attend_kernel(depth, others, query_pos_ref, query_floor_ref, key_pos_ref, kv_ref, *refs):
    kept_ref, squares_ref = refs[:2]
    far = refs[2 : 2 + 2 * others]
    sent_ref, out_ref, totals_sent_ref, totals_ref = refs[2 + 2 * others :]
    lanes = kept_ref.shape[0]
    queries = kept_ref[...]
    squares = squares_ref[:, :1]
    for other in range(others):
        queries = queries + far[2 * other][...].astype(F32)
        squares = squares + spread_back(far[2 * other + 1], lanes)[:, :1]
    queries = (queries * lax.rsqrt(squares / depth + EPSILON)).astype(BF16)
    visible = (key_pos_ref[...] <= query_pos_ref[...]) & (key_pos_ref[...] >= query_floor_ref[...])
    keys, values = kv_ref[:, :HD], kv_ref[:, HD:]
    lane = lax.broadcasted_iota(jnp.int32, (lanes, lanes), 1)
    totals = jnp.zeros((lanes, lanes), F32)
    for head in range(queries.shape[1] // HD):
        span = slice(head * HD, (head + 1) * HD)
        scores = lax.dot_general(
            queries[:, span], keys, (((1,), (1,)), ((), ())), preferred_element_type=F32
        ) * HD ** (-0.5)
        weights = jnp.where(visible, jnp.exp(CAP * jnp.tanh(scores / CAP)), 0.0)
        totals = jnp.where(lane == head, jnp.sum(weights, axis=1, keepdims=True), totals)
        weighted = jnp.dot(weights.astype(BF16), values, preferred_element_type=F32)
        out_ref[:, span] = weighted
        sent_ref[:, span] = weighted.astype(BF16)
    totals_ref[...] = totals
    across = totals.T[:8]
    high = across.astype(BF16)
    totals_sent_ref[:8] = high
    totals_sent_ref[8:] = (across - high.astype(F32)).astype(BF16)


def update_kernel(others, place_ref, weight_ref, kept_ref, totals_ref, *refs):
    far, (own_ref, sent_ref) = refs[: 2 * others], refs[2 * others :]
    lanes = kept_ref.shape[0]
    unit = own_ref.shape[1]
    weighted = kept_ref[...]
    totals = totals_ref[...]
    for other in range(others):
        weighted = weighted + far[2 * other][...].astype(F32)
        totals = totals + spread_back(far[2 * other + 1], lanes)
    attended = jnp.concatenate(
        [
            (weighted[:, head * HD : (head + 1) * HD] / totals[:, head : head + 1]).astype(BF16)
            for head in range(weighted.shape[1] // HD)
        ],
        axis=1,
    )
    for core, out_ref in enumerate((own_ref, sent_ref)):
        for chip in range(CHIPS):
            base = ((place_ref[0] ^ chip) * 2 + (place_ref[1] ^ core)) * unit
            update = lax.dot_general(
                weight_ref[pl.ds(pl.multiple_of(base, unit), unit), :],
                attended,
                (((1,), (1,)), ((), ())),
                preferred_element_type=F32,
            )
            out_ref[chip] = update.astype(out_ref.dtype)


def call(kernel, name, out_shape, scalars, arrays, scratch=(), flops=0, loose=()):
    vmem = pl.BlockSpec(memory_space=pltpu.VMEM)
    smem = pl.BlockSpec(memory_space=pltpu.SMEM)
    return pl.pallas_call(
        kernel,
        out_shape=out_shape,
        in_specs=[smem] * len(scalars)
        + [vmem] * len(arrays)
        + [pl.BlockSpec(memory_space=pl.ANY)] * len(loose),
        out_specs=[vmem] * len(out_shape),
        scratch_shapes=list(scratch),
        compiler_params=pltpu.CompilerParams(vmem_limit_bytes=20 * 1024 * 1024),
        cost_estimate=pl.CostEstimate(
            flops=flops, bytes_accessed=sum(2 * a.size for a in arrays), transcendentals=0
        ),
        name=name,
    )(*scalars, *arrays, *loose)


def in_order(ours, theirs, core):
    low, high = jnp.where(core == 0, ours, theirs), jnp.where(core == 0, theirs, ours)
    return jnp.stack([low, high], axis=1).reshape(-1, ours.shape[-1])


def key_values_of(hidden, kv_gain, kv_weight, query_states, place_now, meanwhile):
    lane_count = lax.axis_size("row")
    tile_count = lane_count // KVH
    me = lax.axis_index("row")
    tile, chip, core = me // KVH, me // 2 % CHIPS, me % 2
    rows = hidden.shape[0]
    unit = kv_weight.shape[0]
    pair = 2 * HD
    share = lax.axis_size("groups") == 2
    part = lax.axis_index("groups") if share else 0

    order = [place for round_ in ROUNDS for place in round_]

    def kept_head(place):
        return lambda chip, core, tile, part: (chip ^ place) * 2 + core

    def sent_head(place):
        return lambda chip, core, tile, part: ((chip ^ place) * 2 + core) ^ part

    def other_head(place):
        return lambda chip, core, tile, part: (chip ^ place) * 2 + 1 - core

    def block(place, j):
        return lambda chip, core, tile, part: (tile ^ j) * CHIPS + (chip ^ place)

    kernels = in_kernels(unit, rows)
    width = 2 * unit
    pieces, features = prepared(
        kv_weight,
        [[sent_head(place) for place in round_] for round_ in ROUNDS]
        + [[other_head(place) for place in order]],
        pair,
        hidden,
        kv_gain,
        [[block(place, j) for j in range(tile_count)] for place in range(CHIPS)],
        width,
        query_states,
        place_now,
        kernels,
    )
    sent, traded = pieces[:-1], pieces[-1]

    def to_tile(value, j, flip):
        if not share:
            return swapped(value, j * KVH)
        pairs = [
            (g * lane_count + d, g * lane_count + (d ^ (j * KVH) ^ (g if flip else 0)))
            for g in range(2)
            for d in range(lane_count)
        ]
        return lax.ppermute(value, ("groups", "row"), pairs)

    far = [[to_tile(value, j, True) for j in range(1, tile_count)] for value in sent]
    held = [features[0]] + [swapped(features[p], 2 * p) for p in range(1, CHIPS)]

    traded, held[1] = lax.optimization_barrier((traded, held[1]))
    traded = swapped(traded, 1)

    def shared(number):
        start = sum(len(round_) for round_ in ROUNDS[:number])
        return [
            swapped(value, 1, "groups")
            if share
            else to_tile(traded[start : start + len(ROUNDS[number])], j, False)
            for j, value in enumerate(far[number], 1)
        ]

    firsts = [core] + [core ^ part] * (tile_count - 1)
    kv_weight, own, _ = lax.optimization_barrier((kv_weight, held[0], far[0]))
    kept, own = staged(
        kv_weight, [kept_head(place) for place in order], pair, own, place_now, kernels
    )
    held[1], kept, own = lax.optimization_barrier((held[1], kept, own))
    halves = [shared(number) for number in range(len(ROUNDS))]
    held[2], held[3], halves[0], far = lax.optimization_barrier((held[2], held[3], halves[0], far))
    tokens = held + [swapped(piece, 1) for piece in held]
    tokens[0] = own
    total = None
    done = 0
    for number, round_ in enumerate(ROUNDS):
        blocks = [piece for pair_ in zip(far[number], halves[number]) for piece in pair_]
        partials = projected(
            tokens, len(round_), kept, traded, done, firsts, blocks, rows, kernels
        )
        done += len(round_)
        if number == 0:
            partials, tokens = lax.optimization_barrier((partials, tokens))
            results = meanwhile(tokens)
        for partial, place in zip(partials, round_):
            if place:
                partial = swapped(partial, 2 * place)
            pieces = partial.reshape(2, CHIPS, rows, pair).astype(F32)
            pieces = jnp.stack([pieces[:, j ^ place] for j in range(CHIPS)], axis=1)
            total = pieces if total is None else total + pieces
    key_values = total.astype(BF16).reshape(2 * CHIPS * rows, pair)
    sources = jnp.stack(
        [tile * KVH + (chip ^ j) * 2 + (core ^ e) for e in range(2) for j in range(CHIPS)]
    )
    key_pos = (sources[:, None] * rows + jnp.arange(rows, dtype=jnp.int32)[None, :]).reshape(-1)
    return key_values, key_pos, results


def gather_rows(own):
    ours = [own] + [swapped(own, 2 * place) for place in range(1, CHIPS)]
    theirs = swapped(jnp.stack(ours), 1)
    return ours + [theirs]


def scatter_rows(kept, sent):
    both = kept + swapped(sent, 1).astype(F32)
    total = both[0]
    for place in range(1, CHIPS):
        total = total + swapped(both[place].astype(BF16), 2 * place).astype(F32)
    return total


def attend_rows(queries, query_pos, query_floor, key_values, key_pos):
    row_count = queries.shape[0]
    head_count = queries.shape[1] // HD
    key_part = key_values[:, :HD]
    value_part = key_values[:, HD:]
    grouped = queries.reshape(row_count, head_count, HD)
    scores = jnp.einsum("rhd,kd->rhk", grouped, key_part, preferred_element_type=F32) * HD ** (-0.5)
    capped = CAP * jnp.tanh(scores / CAP)
    visible = (key_pos[None, :] <= query_pos[:, None]) & (key_pos[None, :] >= query_floor[:, None])
    weights = jnp.where(visible[:, None, :], jnp.exp(capped), 0.0)
    totals = jnp.sum(weights, axis=2)
    weighted = jnp.einsum(
        "rhk,kd->rhd", weights.astype(BF16), value_part, preferred_element_type=F32
    )
    return weighted.reshape(row_count, head_count * HD), totals


def on_device(
    hidden, kv_gain, kv_weight, query_states, query_gain, query_weight, output_weight, block_bounds
):
    tile_count = lax.axis_size("row") // KVH
    tile = lax.axis_index("row") // KVH
    depth = hidden.shape[1]
    slice_depth = query_weight.shape[2]
    query_count = query_states.shape[1]
    row_number = jnp.arange(query_count, dtype=jnp.int32)
    query_pos = jnp.repeat(block_bounds[:, 1], QBLK) + row_number % QBLK
    query_floor = jnp.repeat(block_bounds[:, 0], QBLK)

    me = lax.axis_index("row")
    chip, core = me // 2 % CHIPS, me % 2
    part = lax.axis_index("groups") if lax.axis_size("groups") == 2 else 0
    place_now = jnp.stack([chip, core, tile, part]).astype(jnp.int32)
    unit, rows = query_states.shape[0], hidden.shape[0]
    kernels = in_kernels(unit, rows)
    width = query_weight.shape[3]
    own_rows = query_states
    small = jax.ShapeDtypeStruct((16, query_count), BF16)
    spread = jax.ShapeDtypeStruct((query_count, query_count), F32)
    wide = [jax.ShapeDtypeStruct((query_count, width), kind) for kind in (BF16, F32)]
    flops = 2 * query_count * slice_depth * width

    def query_parts(section, pieces):
        gain = lax.dynamic_slice_in_dim(query_gain[section], tile * slice_depth, slice_depth)
        if not kernels:
            pieces = [
                part
                for piece in pieces
                for part in (piece if piece.ndim == 3 else [piece[-(own_rows.size // piece.shape[1]) :]])
            ]
            pieces = [piece.reshape(own_rows.shape) for piece in pieces]
            ours, theirs = (
                jnp.stack(natural(half, chip)) for half in (pieces[:CHIPS], pieces[CHIPS:])
            )
            stream = in_order(ours, theirs, core).astype(F32)
            scaled = (stream * gain[:, None]).astype(BF16)
            partial = lax.dot_general(
                scaled, query_weight[section, 0], (((0,), (0,)), ((), ())), preferred_element_type=F32
            )
            squares = jnp.sum(stream * stream, axis=0)
            return partial.astype(BF16), partial, squares.astype(BF16), squares
        return call(
            functools.partial(query_kernel, query_count),
            "query",
            wide + [small, spread],
            [place_now],
            [gain[None, :], query_weight[section, 0]],
            [
                pltpu.VMEM((slice_depth, query_count), BF16),
                pltpu.VMEM((KVH, own_rows.size // (2 * unit * tile_count), 2 * unit * tile_count), BF16),
                pltpu.SemaphoreType.DMA((KVH,)),
            ],
            flops,
            pieces,
        )

    key_values, key_pos, parts = key_values_of(
        hidden, kv_gain, kv_weight, query_states, place_now, functools.partial(query_parts, 0)
    )
    positions = [query_pos[:, None], query_floor[:, None], key_pos[None, :]]
    for section in range(query_gain.shape[0]):
        if section:
            parts = query_parts(section, gather_rows(own_rows))
        sent, partial, squares_sent, squares = parts
        if kernels:
            far = zip(over_tiles(sent, tile_count)[1:], over_tiles(squares_sent, tile_count)[1:])
            sent, weighted, totals_sent, totals = call(
                functools.partial(attend_kernel, depth, tile_count - 1),
                "attend",
                wide + [small, spread],
                [],
                positions + [key_values, partial, squares] + [value for pair in far for value in pair],
                (),
                flops // 2,
            )
            far = zip(over_tiles(sent, tile_count)[1:], over_tiles(totals_sent, tile_count)[1:])
            shape = (CHIPS, unit, query_count)
            kept, sent = call(
                functools.partial(update_kernel, tile_count - 1),
                "update",
                [jax.ShapeDtypeStruct(shape, F32), jax.ShapeDtypeStruct(shape, BF16)],
                [place_now],
                [output_weight[section, 0], weighted, totals]
                + [value for pair in far for value in pair],
                (),
                flops,
            )
        else:
            square_sum = sum(over_tiles(squares_sent, tile_count)[1:], squares)
            query_sum = sum(over_tiles(sent, tile_count)[1:], partial)
            inverse = lax.rsqrt(square_sum / depth + EPSILON)
            queries = (query_sum * inverse[:, None]).astype(BF16)
            weighted, totals = attend_rows(queries, query_pos, query_floor, key_values, key_pos)
            total_sum = sum(over_tiles(totals.astype(BF16), tile_count)[1:], totals)
            weighted_sum = sum(over_tiles(weighted.astype(BF16), tile_count)[1:], weighted)
            attended = (
                (weighted_sum.reshape(query_count, QPK, HD) / total_sum[:, :, None])
                .reshape(query_count, QPK * HD)
                .astype(BF16)
            )
            update = lax.dot_general(
                output_weight[section, 0],
                attended,
                (((1,), (1,)), ((), ())),
                preferred_element_type=F32,
            )
            split = update.reshape(CHIPS, 2, unit, query_count)
            kept = jnp.where(core == 0, split[:, 0], split[:, 1])
            sent = jnp.where(core == 0, split[:, 1], split[:, 0]).astype(BF16)
            kept, sent = (jnp.stack(natural(value, chip)) for value in (kept, sent))
        own_rows = (own_rows.astype(F32) + scatter_rows(kept, sent)).astype(BF16)
    return own_rows


def solution(mesh):
    in_specs = (
        P(("groups", "row"), None),
        P(),
        P("row", None),
        P("row", "groups"),
        P(),
        P(None, "row", None, None),
        P(None, "row", None, None),
        P("groups", None),
    )
    return jax.shard_map(
        on_device, mesh=mesh, in_specs=in_specs, out_specs=P("row", "groups"), check_vma=False
    )
```

```python
import functools

import jax
import jax.numpy as jnp
from jax import lax
from jax.experimental import pallas as pl
from jax.experimental.pallas import tpu as pltpu
from jax.sharding import PartitionSpec as P

KVH = 8
HD = 128
QPK = 5
QBLK = 64
CAP = 30.0
EPSILON = 1e-05
BF16 = jnp.bfloat16
F32 = jnp.float32

CHIPS = KVH // 2
ROUNDS = ((1, 2), (3, 0))
PROJECT_COST = 8


def swapped(value, mask, axis="row"):
    pairs = [(source, source ^ mask) for source in range(lax.axis_size(axis))]
    return lax.ppermute(value, axis, pairs)


def over_tiles(value, tile_count):
    values = [value]
    mask = 1
    while mask < tile_count:
        if len(values) == 1:
            values.append(swapped(values[0], mask * KVH))
        else:
            got = swapped(jnp.stack(values), mask * KVH)
            values.extend(got[place] for place in range(len(values)))
        mask *= 2
    return values


def natural(pieces, index):
    pieces = list(pieces)
    bit = 1
    while bit < len(pieces):
        upper = index // bit % 2 == 1
        pieces = [jnp.where(upper, pieces[j ^ bit], pieces[j]) for j in range(len(pieces))]
        bit *= 2
    return pieces


def prepare_kernel(
    pair, heads, blocks, width, place_ref, weight_any, hidden_any, gain_any, extra_any, *refs
):
    weight_ref, hidden_ref, gain_ref, extra_ref, normed, sems = refs[-6:]
    head_refs, out_refs = refs[: len(heads)], refs[len(heads) : -6]
    place_now = [place_ref[number] for number in range(4)]
    rows = hidden_ref.shape[0]
    lanes = extra_ref.shape[1]
    more = out_refs[0].shape[0] - rows
    copies = [
        pltpu.make_async_copy(source, target, sems.at[number])
        for number, (source, target) in enumerate(
            (
                (weight_any, weight_ref),
                (hidden_any, hidden_ref),
                (gain_any, gain_ref),
                (extra_any, extra_ref),
            )
        )
    ]
    for copy in copies:
        copy.start()
    copies[0].wait()
    for head_ref, group in zip(head_refs, heads):
        for number, head in enumerate(group):
            column = pl.multiple_of(head(*place_now) * pair, pair)
            head_ref[number] = weight_ref[:, pl.ds(column, pair)]
    for copy in copies[1:]:
        copy.wait()
    hidden = hidden_ref[...].astype(F32)
    inverse = lax.rsqrt(jnp.mean(hidden * hidden, axis=1, keepdims=True) + EPSILON)
    normed[...] = (hidden * inverse * gain_ref[...]).astype(BF16)
    for out_ref, group in zip(out_refs, blocks):
        for number, block in enumerate(group):
            start = pl.multiple_of(block(*place_now) * width, 128)
            out_ref[:rows, number * width : (number + 1) * width] = normed[:, pl.ds(start, width)]
        for block in range(out_ref.shape[1] // lanes):
            out_ref[rows:, block * lanes : (block + 1) * lanes] = extra_ref[
                block * more : (block + 1) * more, :
            ]


def in_kernels(unit, rows):
    return unit % 64 == 0 and rows % 16 == 0


def prepared(weight, head_groups, pair, hidden, gain, groups, width, extra, place_now, kernels):
    rows, depth = hidden.shape
    total_width = len(groups[0]) * width
    more = extra.size // total_width
    if not kernels:
        now = [place_now[number] for number in range(4)]
        columns = [
            jnp.stack(
                [lax.dynamic_slice_in_dim(weight, head(*now) * pair, pair, 1) for head in group]
            )
            for group in head_groups
        ]
        hidden_float = hidden.astype(F32)
        inverse = lax.rsqrt(jnp.mean(hidden_float * hidden_float, axis=1, keepdims=True) + EPSILON)
        normed = (hidden_float * inverse * gain[None, :]).astype(BF16)
        results = []
        for group in groups:
            blocks = [
                lax.dynamic_slice_in_dim(normed, block(*now) * width, width, 1) for block in group
            ]
            rest = extra.reshape(more, total_width)
            results.append(jnp.concatenate([jnp.concatenate(blocks, axis=1), rest], axis=0))
        return columns, results
    counts = [len(group) for group in head_groups]
    vmem = pl.BlockSpec(memory_space=pltpu.VMEM)
    smem = pl.BlockSpec(memory_space=pltpu.SMEM)
    results = pl.pallas_call(
        functools.partial(prepare_kernel, pair, head_groups, groups, width),
        out_shape=[jax.ShapeDtypeStruct((count, weight.shape[0], pair), BF16) for count in counts]
        + [jax.ShapeDtypeStruct((rows + more, total_width), BF16) for group in groups],
        in_specs=[smem] + [pl.BlockSpec(memory_space=pltpu.HBM)] * 4,
        out_specs=[vmem] * (len(counts) + len(groups)),
        scratch_shapes=[
            pltpu.VMEM(weight.shape, BF16),
            pltpu.VMEM((rows, depth), BF16),
            pltpu.VMEM((1, depth), F32),
            pltpu.VMEM(extra.shape, BF16),
            pltpu.VMEM((rows, depth), BF16),
            pltpu.SemaphoreType.DMA((4,)),
        ],
        compiler_params=pltpu.CompilerParams(vmem_limit_bytes=60 * 1024 * 1024),
        name="prepare",
    )(
        place_now,
        weight,
        hidden,
        gain[None, :],
        extra,
    )
    return results[: len(counts)], results[len(counts) :]


def stage_kernel(pair, heads, place_ref, weight_ref, tokens_ref, kept_ref, own_ref):
    place_now = [place_ref[number] for number in range(4)]
    for number, head in enumerate(heads):
        column = pl.multiple_of(head(*place_now) * pair, pair)
        kept_ref[number] = weight_ref[:, pl.ds(column, pair)]
    own_ref[...] = tokens_ref[: own_ref.shape[0], :]


def staged(weight, heads, pair, tokens, place_now, kernels):
    if not kernels:
        now = [place_now[number] for number in range(4)]
        columns = [lax.dynamic_slice_in_dim(weight, head(*now) * pair, pair, 1) for head in heads]
        return jnp.stack(columns), tokens
    shapes = [
        jax.ShapeDtypeStruct((len(heads), weight.shape[0], pair), BF16),
        jax.ShapeDtypeStruct(tokens.shape, BF16),
    ]
    return call(
        functools.partial(stage_kernel, pair, heads),
        "stage",
        shapes,
        [place_now],
        [weight, tokens],
    )


def project_kernel(rows, heads, start, first_ref, kept_ref, traded_ref, *refs):
    token_refs, refs = refs[: 2 * CHIPS], refs[2 * CHIPS :]
    weight = refs[-1]
    out_refs = refs[-1 - heads : -1]
    blocks = refs[: -1 - heads]
    unit, pair = kept_ref.shape[1:]

    def put(head, tile, second, value):
        which = 1 - first_ref[tile] if second else first_ref[tile]
        base = pl.multiple_of(2 * unit * tile + which * unit, unit)
        weight[pl.ds(base, unit), head * pair : (head + 1) * pair] = value

    for head in range(heads):
        put(head, 0, 0, kept_ref[start + head])
        put(head, 0, 1, traded_ref[start + head])
        for number, block_ref in enumerate(blocks):
            put(head, 1 + number // 2, number % 2, block_ref[head])
    for number, token_ref in enumerate(token_refs):
        span = slice(number * rows, (number + 1) * rows)
        result = jnp.dot(token_ref[:rows, :], weight[...], preferred_element_type=F32).astype(BF16)
        for head, out_ref in enumerate(out_refs):
            out_ref[span, :] = result[:, head * pair : (head + 1) * pair]


def projected(tokens, heads, kept, traded, start, firsts, blocks, rows, kernels):
    unit, pair = kept.shape[1:]
    depth = tokens[0].shape[1]
    count = len(tokens) * rows
    firsts = jnp.stack(firsts).astype(jnp.int32)
    if not kernels:
        pieces = [kept[start : start + heads], traded[start : start + heads]] + blocks
        ordered = []
        for tile in range(len(pieces) // 2):
            one, two = pieces[2 * tile : 2 * tile + 2]
            first = firsts[tile] == 0
            ordered += [jnp.where(first, one, two), jnp.where(first, two, one)]
        weight = jnp.concatenate(ordered, axis=1)
        tokens = jnp.concatenate([piece[:rows] for piece in tokens])
        result = jnp.einsum("td,hdc->htc", tokens, weight, preferred_element_type=F32)
        return list(result.astype(BF16))
    vmem = pl.BlockSpec(memory_space=pltpu.VMEM)
    smem = pl.BlockSpec(memory_space=pltpu.SMEM)
    return list(
        pl.pallas_call(
            functools.partial(project_kernel, rows, heads, start),
            out_shape=[jax.ShapeDtypeStruct((count, pair), BF16)] * heads,
            in_specs=[smem] + [vmem] * (2 + len(tokens) + len(blocks)),
            out_specs=[vmem] * heads,
            scratch_shapes=[pltpu.VMEM((depth, heads * pair), BF16)],
            compiler_params=pltpu.CompilerParams(vmem_limit_bytes=20 * 1024 * 1024),
            cost_estimate=pl.CostEstimate(
                flops=PROJECT_COST * 2 * heads * count * depth * pair,
                bytes_accessed=2 * count * depth,
                transcendentals=0,
            ),
            name="project",
        )(firsts, kept, traded, *tokens, *blocks)
    )


def query_kernel(lanes, place_ref, gain_ref, weight_ref, *refs):
    piece_refs, refs = refs[:-9], refs[-9:]
    results, own_ref, (stream, turned, parts, sems) = refs[:4], refs[4], refs[5:]
    unit = stream.shape[0] // KVH
    more = parts.shape[1]
    blocks = parts.shape[2] // lanes
    sources = [
        piece_ref.at[place] if len(piece_ref.shape) == 3 else piece_ref
        for piece_ref in piece_refs
        for place in range(CHIPS if len(piece_ref.shape) == 3 else 1)
    ]
    bases = [
        pl.multiple_of(
            ((place_ref[0] ^ number % CHIPS) * 2 + (place_ref[1] ^ number // CHIPS)) * unit, unit
        )
        for number in range(KVH)
    ]
    packed = sources[0].shape[1] != lanes
    copies = []
    for number, source in enumerate(sources):
        if packed:
            source, target = source.at[source.shape[0] - more :], parts.at[number]
        else:
            target = stream.at[pl.ds(bases[number], unit)]
        copies.append(pltpu.make_async_copy(source, target, sems.at[number]))
        copies[-1].start()
    for number, copy in enumerate(copies):
        copy.wait()
        for block in range(blocks if packed else 0):
            stream[pl.ds(pl.multiple_of(bases[number] + block * more, more), more), :] = parts[
                number, :, block * lanes : (block + 1) * lanes
            ]
    turned[...] = stream[...].astype(F32).T
    query_step(turned[...], gain_ref, weight_ref, *results)
    half = own_ref.shape[0]
    own_ref[...] = turned[pl.ds(pl.multiple_of(place_ref[1] * half, half), half), :].astype(BF16)


def query_step(rows, gain_ref, weight_ref, sent_ref, kept_ref, squares_sent_ref, squares_ref):
    squares = jnp.sum(rows * rows, axis=1, keepdims=True)
    scaled = (rows * gain_ref[...]).astype(BF16)
    partial = jnp.dot(scaled, weight_ref[...], preferred_element_type=F32)
    kept_ref[...] = partial
    sent_ref[...] = partial.astype(BF16)
    spread = jnp.broadcast_to(squares, squares_ref.shape)
    squares_ref[...] = spread
    across = spread.T[:8]
    high = across.astype(BF16)
    squares_sent_ref[:8] = high
    squares_sent_ref[8:] = (across - high.astype(F32)).astype(BF16)


def both_cores(place_ref, ours_ref, theirs_ref, rows):
    half = ours_ref.shape[0]
    for which, ref in ((place_ref[1], ours_ref), (1 - place_ref[1], theirs_ref)):
        rows[pl.ds(pl.multiple_of(which * half, half), half), :] = ref[...]


def later_query_kernel(place_ref, gain_ref, weight_ref, ours_ref, theirs_ref, *refs):
    results, rows = refs[:-1], refs[-1]
    both_cores(place_ref, ours_ref, theirs_ref, rows)
    query_step(rows[...].astype(F32), gain_ref, weight_ref, *results)


def own_rows_kernel(place_ref, ours_ref, theirs_ref, out_ref, rows, turned):
    both_cores(place_ref, ours_ref, theirs_ref, rows)
    unit = out_ref.shape[0]
    column = pl.multiple_of(place_ref[0] * 2 * unit, 2 * unit)
    turned[...] = rows[:, pl.ds(column, 2 * unit)].astype(F32).T
    out_ref[...] = turned[pl.ds(pl.multiple_of(place_ref[1] * unit, unit), unit), :].astype(BF16)


def spread_back(pair_ref, lanes):
    across = pair_ref[:8].astype(F32) + pair_ref[8:].astype(F32)
    return jnp.concatenate([across, jnp.zeros((lanes - 8, lanes), F32)], axis=0).T


def attend_kernel(depth, others, query_pos_ref, query_floor_ref, key_pos_ref, kv_ref, *refs):
    kept_ref, squares_ref = refs[:2]
    far = refs[2 : 2 + 2 * others]
    sent_ref, out_ref, totals_sent_ref, totals_ref = refs[2 + 2 * others :]
    lanes = kept_ref.shape[0]
    queries = kept_ref[...]
    squares = squares_ref[:, :1]
    for other in range(others):
        queries = queries + far[2 * other][...].astype(F32)
        squares = squares + spread_back(far[2 * other + 1], lanes)[:, :1]
    queries = (queries * lax.rsqrt(squares / depth + EPSILON)).astype(BF16)
    visible = (key_pos_ref[...] <= query_pos_ref[...]) & (key_pos_ref[...] >= query_floor_ref[...])
    keys, values = kv_ref[:, :HD], kv_ref[:, HD:]
    lane = lax.broadcasted_iota(jnp.int32, (lanes, lanes), 1)
    totals = jnp.zeros((lanes, lanes), F32)
    for head in range(queries.shape[1] // HD):
        span = slice(head * HD, (head + 1) * HD)
        scores = lax.dot_general(
            queries[:, span], keys, (((1,), (1,)), ((), ())), preferred_element_type=F32
        ) * HD ** (-0.5)
        weights = jnp.where(visible, jnp.exp(CAP * jnp.tanh(scores / CAP)), 0.0)
        totals = jnp.where(lane == head, jnp.sum(weights, axis=1, keepdims=True), totals)
        weighted = jnp.dot(weights.astype(BF16), values, preferred_element_type=F32)
        out_ref[:, span] = weighted
        sent_ref[:, span] = weighted.astype(BF16)
    totals_ref[...] = totals
    across = totals.T[:8]
    high = across.astype(BF16)
    totals_sent_ref[:8] = high
    totals_sent_ref[8:] = (across - high.astype(F32)).astype(BF16)


def attended_of(others, kept_ref, totals_ref, far):
    lanes = kept_ref.shape[0]
    weighted = kept_ref[...]
    totals = totals_ref[...]
    for other in range(others):
        weighted = weighted + far[2 * other][...].astype(F32)
        totals = totals + spread_back(far[2 * other + 1], lanes)
    return jnp.concatenate(
        [
            (weighted[:, head * HD : (head + 1) * HD] / totals[:, head : head + 1]).astype(BF16)
            for head in range(weighted.shape[1] // HD)
        ],
        axis=1,
    )


def update_rows_kernel(others, place_ref, weight_ref, kept_ref, totals_ref, *refs):
    far, (own_ref, sent_ref, update) = refs[: 2 * others], refs[2 * others :]
    attended = attended_of(others, kept_ref, totals_ref, far)
    update[...] = lax.dot_general(
        attended, weight_ref[...], (((1,), (1,)), ((), ())), preferred_element_type=F32
    )
    half = own_ref.shape[0]
    for which, out_ref in ((place_ref[1], own_ref), (1 - place_ref[1], sent_ref)):
        rows = update[pl.ds(pl.multiple_of(which * half, half), half), :]
        out_ref[...] = rows.astype(out_ref.dtype)


def update_kernel(others, place_ref, weight_ref, kept_ref, totals_ref, *refs):
    far, (own_ref, sent_ref) = refs[: 2 * others], refs[2 * others :]
    unit = own_ref.shape[1]
    attended = attended_of(others, kept_ref, totals_ref, far)
    for core, out_ref in enumerate((own_ref, sent_ref)):
        for chip in range(CHIPS):
            base = ((place_ref[0] ^ chip) * 2 + (place_ref[1] ^ core)) * unit
            update = lax.dot_general(
                weight_ref[pl.ds(pl.multiple_of(base, unit), unit), :],
                attended,
                (((1,), (1,)), ((), ())),
                preferred_element_type=F32,
            )
            out_ref[chip] = update.astype(out_ref.dtype)


def call(kernel, name, out_shape, scalars, arrays, scratch=(), flops=0, loose=()):
    vmem = pl.BlockSpec(memory_space=pltpu.VMEM)
    smem = pl.BlockSpec(memory_space=pltpu.SMEM)
    return pl.pallas_call(
        kernel,
        out_shape=out_shape,
        in_specs=[smem] * len(scalars)
        + [vmem] * len(arrays)
        + [pl.BlockSpec(memory_space=pl.ANY)] * len(loose),
        out_specs=[vmem] * len(out_shape),
        scratch_shapes=list(scratch),
        compiler_params=pltpu.CompilerParams(vmem_limit_bytes=20 * 1024 * 1024),
        cost_estimate=pl.CostEstimate(
            flops=flops, bytes_accessed=sum(2 * a.size for a in arrays), transcendentals=0
        ),
        name=name,
    )(*scalars, *arrays, *loose)


def in_order(ours, theirs, core):
    low, high = jnp.where(core == 0, ours, theirs), jnp.where(core == 0, theirs, ours)
    return jnp.stack([low, high], axis=1).reshape(-1, ours.shape[-1])


def key_values_of(hidden, kv_gain, kv_weight, query_states, place_now, meanwhile):
    lane_count = lax.axis_size("row")
    tile_count = lane_count // KVH
    me = lax.axis_index("row")
    tile, chip, core = me // KVH, me // 2 % CHIPS, me % 2
    rows = hidden.shape[0]
    unit = kv_weight.shape[0]
    pair = 2 * HD
    share = lax.axis_size("groups") == 2
    part = lax.axis_index("groups") if share else 0

    order = [place for round_ in ROUNDS for place in round_]

    def kept_head(place):
        return lambda chip, core, tile, part: (chip ^ place) * 2 + core

    def sent_head(place):
        return lambda chip, core, tile, part: ((chip ^ place) * 2 + core) ^ part

    def other_head(place):
        return lambda chip, core, tile, part: (chip ^ place) * 2 + 1 - core

    def block(place, j):
        return lambda chip, core, tile, part: (tile ^ j) * CHIPS + (chip ^ place)

    kernels = in_kernels(unit, rows)
    width = 2 * unit
    pieces, features = prepared(
        kv_weight,
        [[sent_head(place) for place in round_] for round_ in ROUNDS]
        + [[other_head(place) for place in order]],
        pair,
        hidden,
        kv_gain,
        [[block(place, j) for j in range(tile_count)] for place in range(CHIPS)],
        width,
        query_states,
        place_now,
        kernels,
    )
    sent, traded = pieces[:-1], pieces[-1]

    def to_tile(value, j, flip):
        if not share:
            return swapped(value, j * KVH)
        pairs = [
            (g * lane_count + d, g * lane_count + (d ^ (j * KVH) ^ (g if flip else 0)))
            for g in range(2)
            for d in range(lane_count)
        ]
        return lax.ppermute(value, ("groups", "row"), pairs)

    far = [[to_tile(value, j, True) for j in range(1, tile_count)] for value in sent]
    held = [features[0]] + [swapped(features[p], 2 * p) for p in range(1, CHIPS)]

    traded, held[1] = lax.optimization_barrier((traded, held[1]))
    traded = swapped(traded, 1)

    def shared(number):
        start = sum(len(round_) for round_ in ROUNDS[:number])
        return [
            swapped(value, 1, "groups")
            if share
            else to_tile(traded[start : start + len(ROUNDS[number])], j, False)
            for j, value in enumerate(far[number], 1)
        ]

    firsts = [core] + [core ^ part] * (tile_count - 1)
    kv_weight, own, _ = lax.optimization_barrier((kv_weight, held[0], far[0]))
    kept, own = staged(
        kv_weight, [kept_head(place) for place in order], pair, own, place_now, kernels
    )
    held[1], kept, own = lax.optimization_barrier((held[1], kept, own))
    halves = [shared(number) for number in range(len(ROUNDS))]
    held[2], held[3], halves[0], far = lax.optimization_barrier((held[2], held[3], halves[0], far))
    tokens = held + [swapped(piece, 1) for piece in held]
    tokens[0] = own
    total = None
    done = 0
    for number, round_ in enumerate(ROUNDS):
        blocks = [piece for pair_ in zip(far[number], halves[number]) for piece in pair_]
        partials = projected(
            tokens, len(round_), kept, traded, done, firsts, blocks, rows, kernels
        )
        done += len(round_)
        if number == 0:
            partials, tokens = lax.optimization_barrier((partials, tokens))
            results = meanwhile(tokens)
        for partial, place in zip(partials, round_):
            if place:
                partial = swapped(partial, 2 * place)
            pieces = partial.reshape(2, CHIPS, rows, pair).astype(F32)
            pieces = jnp.stack([pieces[:, j ^ place] for j in range(CHIPS)], axis=1)
            total = pieces if total is None else total + pieces
    key_values = total.astype(BF16).reshape(2 * CHIPS * rows, pair)
    sources = jnp.stack(
        [tile * KVH + (chip ^ j) * 2 + (core ^ e) for e in range(2) for j in range(CHIPS)]
    )
    key_pos = (sources[:, None] * rows + jnp.arange(rows, dtype=jnp.int32)[None, :]).reshape(-1)
    return key_values, key_pos, results


def gather_rows(own):
    ours = [own] + [swapped(own, 2 * place) for place in range(1, CHIPS)]
    theirs = swapped(jnp.stack(ours), 1)
    return ours + [theirs]


def scatter_rows(kept, sent):
    both = kept + swapped(sent, 1).astype(F32)
    total = both[0]
    for place in range(1, CHIPS):
        total = total + swapped(both[place].astype(BF16), 2 * place).astype(F32)
    return total


def reduce_rows(kept, sent):
    both = (kept + swapped(sent, 1).astype(F32)).astype(BF16)
    halves = jnp.split(both, 2, axis=1)
    for masks in ((2, 4), (4, 2)):
        halves = [
            (half.astype(F32) + swapped(half, mask).astype(F32)).astype(BF16)
            for half, mask in zip(halves, masks)
        ]
    return jnp.concatenate(halves, axis=1)


def attend_rows(queries, query_pos, query_floor, key_values, key_pos):
    row_count = queries.shape[0]
    head_count = queries.shape[1] // HD
    key_part = key_values[:, :HD]
    value_part = key_values[:, HD:]
    grouped = queries.reshape(row_count, head_count, HD)
    scores = jnp.einsum("rhd,kd->rhk", grouped, key_part, preferred_element_type=F32) * HD ** (-0.5)
    capped = CAP * jnp.tanh(scores / CAP)
    visible = (key_pos[None, :] <= query_pos[:, None]) & (key_pos[None, :] >= query_floor[:, None])
    weights = jnp.where(visible[:, None, :], jnp.exp(capped), 0.0)
    totals = jnp.sum(weights, axis=2)
    weighted = jnp.einsum(
        "rhk,kd->rhd", weights.astype(BF16), value_part, preferred_element_type=F32
    )
    return weighted.reshape(row_count, head_count * HD), totals


def on_device(
    hidden, kv_gain, kv_weight, query_states, query_gain, query_weight, output_weight, block_bounds
):
    tile_count = lax.axis_size("row") // KVH
    tile = lax.axis_index("row") // KVH
    depth = hidden.shape[1]
    slice_depth = query_weight.shape[2]
    query_count = query_states.shape[1]
    row_number = jnp.arange(query_count, dtype=jnp.int32)
    query_pos = jnp.repeat(block_bounds[:, 1], QBLK) + row_number % QBLK
    query_floor = jnp.repeat(block_bounds[:, 0], QBLK)

    me = lax.axis_index("row")
    chip, core = me // 2 % CHIPS, me % 2
    part = lax.axis_index("groups") if lax.axis_size("groups") == 2 else 0
    place_now = jnp.stack([chip, core, tile, part]).astype(jnp.int32)
    unit, rows = query_states.shape[0], hidden.shape[0]
    kernels = in_kernels(unit, rows)
    width = query_weight.shape[3]
    own_rows = query_states
    small = jax.ShapeDtypeStruct((16, query_count), BF16)
    spread = jax.ShapeDtypeStruct((query_count, query_count), F32)
    wide = [jax.ShapeDtypeStruct((query_count, width), kind) for kind in (BF16, F32)]
    flops = 2 * query_count * slice_depth * width
    halved = jax.ShapeDtypeStruct((query_count // 2, slice_depth), BF16)

    def query_parts(section, pieces):
        gain = lax.dynamic_slice_in_dim(query_gain[section], tile * slice_depth, slice_depth)
        if not kernels:
            pieces = [
                part
                for piece in pieces
                for part in (piece if piece.ndim == 3 else [piece[-(own_rows.size // piece.shape[1]) :]])
            ]
            pieces = [piece.reshape(own_rows.shape) for piece in pieces]
            ours, theirs = (
                jnp.stack(natural(half, chip)) for half in (pieces[:CHIPS], pieces[CHIPS:])
            )
            stream = in_order(ours, theirs, core).astype(F32)
            scaled = (stream * gain[:, None]).astype(BF16)
            partial = lax.dot_general(
                scaled, query_weight[section, 0], (((0,), (0,)), ((), ())), preferred_element_type=F32
            )
            squares = jnp.sum(stream * stream, axis=0)
            return partial.astype(BF16), partial, squares.astype(BF16), squares
        return call(
            functools.partial(query_kernel, query_count),
            "query",
            wide + [small, spread, halved],
            [place_now],
            [gain[None, :], query_weight[section, 0]],
            [
                pltpu.VMEM((slice_depth, query_count), BF16),
                pltpu.VMEM((query_count, slice_depth), F32),
                pltpu.VMEM((KVH, own_rows.size // (2 * unit * tile_count), 2 * unit * tile_count), BF16),
                pltpu.SemaphoreType.DMA((KVH,)),
            ],
            flops,
            pieces,
        )

    key_values, key_pos, parts = key_values_of(
        hidden, kv_gain, kv_weight, query_states, place_now, functools.partial(query_parts, 0)
    )
    positions = [query_pos[:, None], query_floor[:, None], key_pos[None, :]]
    if kernels:
        stream, parts = parts[4], parts[:4]
    sections = query_gain.shape[0]
    for section in range(sections):
        if section and not kernels:
            parts = query_parts(section, gather_rows(own_rows))
        sent, partial, squares_sent, squares = parts
        if kernels:
            far = zip(over_tiles(sent, tile_count)[1:], over_tiles(squares_sent, tile_count)[1:])
            sent, weighted, totals_sent, totals = call(
                functools.partial(attend_kernel, depth, tile_count - 1),
                "attend",
                wide + [small, spread],
                [],
                positions + [key_values, partial, squares] + [value for pair in far for value in pair],
                (),
                flops // 2,
            )
            far = zip(over_tiles(sent, tile_count)[1:], over_tiles(totals_sent, tile_count)[1:])
            arrays = [output_weight[section, 0], weighted, totals]
            arrays += [value for pair in far for value in pair]
            if section + 1 < sections:
                kept, sent = call(
                    functools.partial(update_rows_kernel, tile_count - 1),
                    "update",
                    [jax.ShapeDtypeStruct(halved.shape, F32), halved],
                    [place_now],
                    arrays,
                    [pltpu.VMEM((query_count, slice_depth), F32)],
                    flops,
                )
                stream = (stream.astype(F32) + reduce_rows(kept, sent).astype(F32)).astype(BF16)
                theirs = swapped(stream, 1)
                gain = lax.dynamic_slice_in_dim(
                    query_gain[section + 1], tile * slice_depth, slice_depth
                )
                parts = call(
                    later_query_kernel,
                    "query",
                    wide + [small, spread],
                    [place_now],
                    [gain[None, :], query_weight[section + 1, 0], stream, theirs],
                    [pltpu.VMEM((query_count, slice_depth), BF16)],
                    flops,
                )
                own_rows = call(
                    own_rows_kernel,
                    "own_rows",
                    [jax.ShapeDtypeStruct(own_rows.shape, BF16)],
                    [place_now],
                    [stream, theirs],
                    [
                        pltpu.VMEM((query_count, slice_depth), BF16),
                        pltpu.VMEM((2 * unit, query_count), F32),
                    ],
                )[0]
                continue
            shape = (CHIPS, unit, query_count)
            kept, sent = call(
                functools.partial(update_kernel, tile_count - 1),
                "update",
                [jax.ShapeDtypeStruct(shape, F32), jax.ShapeDtypeStruct(shape, BF16)],
                [place_now],
                arrays,
                (),
                flops,
            )
        else:
            square_sum = sum(over_tiles(squares_sent, tile_count)[1:], squares)
            query_sum = sum(over_tiles(sent, tile_count)[1:], partial)
            inverse = lax.rsqrt(square_sum / depth + EPSILON)
            queries = (query_sum * inverse[:, None]).astype(BF16)
            weighted, totals = attend_rows(queries, query_pos, query_floor, key_values, key_pos)
            total_sum = sum(over_tiles(totals.astype(BF16), tile_count)[1:], totals)
            weighted_sum = sum(over_tiles(weighted.astype(BF16), tile_count)[1:], weighted)
            attended = (
                (weighted_sum.reshape(query_count, QPK, HD) / total_sum[:, :, None])
                .reshape(query_count, QPK * HD)
                .astype(BF16)
            )
            update = lax.dot_general(
                output_weight[section, 0],
                attended,
                (((1,), (1,)), ((), ())),
                preferred_element_type=F32,
            )
            split = update.reshape(CHIPS, 2, unit, query_count)
            kept = jnp.where(core == 0, split[:, 0], split[:, 1])
            sent = jnp.where(core == 0, split[:, 1], split[:, 0]).astype(BF16)
            kept, sent = (jnp.stack(natural(value, chip)) for value in (kept, sent))
        own_rows = (own_rows.astype(F32) + scatter_rows(kept, sent)).astype(BF16)
    return own_rows


def solution(mesh):
    in_specs = (
        P(("groups", "row"), None),
        P(),
        P("row", None),
        P("row", "groups"),
        P(),
        P(None, "row", None, None),
        P(None, "row", None, None),
        P("groups", None),
    )
    return jax.shard_map(
        on_device, mesh=mesh, in_specs=in_specs, out_specs=P("row", "groups"), check_vma=False
    )
```

```python
import functools

import jax
import jax.numpy as jnp
from jax import lax
from jax.experimental import pallas as pl
from jax.experimental.pallas import tpu as pltpu
from jax.sharding import PartitionSpec as P

KVH = 8
HD = 128
QPK = 5
QBLK = 64
CAP = 30.0
EPSILON = 1e-05
LOG2_E = 1.4426950408889634
BF16 = jnp.bfloat16
F32 = jnp.float32

CHIPS = KVH // 2
ROUNDS = ((2, 1), (3, 0))
PROJECT_COST = 8
BAND = 32
HEADS_AT_ONCE = (2, 2)


def swapped(value, mask, axis="row"):
    pairs = [(source, source ^ mask) for source in range(lax.axis_size(axis))]
    return lax.ppermute(value, axis, pairs)


def over_tiles(value, tile_count):
    values = [value]
    mask = 1
    while mask < tile_count:
        if len(values) == 1:
            values.append(swapped(values[0], mask * KVH))
        else:
            got = swapped(jnp.stack(values), mask * KVH)
            values.extend(got[place] for place in range(len(values)))
        mask *= 2
    return values


def natural(pieces, index):
    pieces = list(pieces)
    bit = 1
    while bit < len(pieces):
        upper = index // bit % 2 == 1
        pieces = [jnp.where(upper, pieces[j ^ bit], pieces[j]) for j in range(len(pieces))]
        bit *= 2
    return pieces


def prepare_kernel(
    pair, heads, blocks, width, place_ref, weight_any, hidden_any, gain_any, extra_any, *refs
):
    weight_ref, hidden_ref, gain_ref, extra_ref, normed, sems = refs[-6:]
    results = len(heads) + len(blocks)
    targets, refs = refs[:results], refs[results:-6]
    place_now = [place_ref[number] for number in range(4)]
    rows = hidden_ref.shape[0]
    lanes = extra_ref.shape[1]
    bands = [slice(band, band + BAND) for band in range(0, rows, BAND)]
    pairs = [(weight_any, weight_ref), (gain_any, gain_ref), (extra_any, extra_ref)]
    pairs += [(hidden_any.at[band], hidden_ref.at[band]) for band in bands]
    copies = [
        pltpu.make_async_copy(source, target, sems.at[number])
        for number, (source, target) in enumerate(pairs)
    ]
    outs = [
        pltpu.make_async_copy(source, target, sems.at[len(copies) + number])
        for number, (source, target) in enumerate(zip(refs, targets))
    ]
    for copy in copies:
        copy.start()
    copies[0].wait()
    for head_ref, group, out in zip(refs, heads, outs):
        for number, head in enumerate(group):
            column = pl.multiple_of(head(*place_now) * pair, pair)
            head_ref[number] = weight_ref[:, pl.ds(column, pair)]
        out.start()
    copies[1].wait()
    copies[2].wait()
    for band, copy in zip(bands, copies[3:]):
        copy.wait()
        hidden = hidden_ref[band, :].astype(F32)
        inverse = lax.rsqrt(jnp.mean(hidden * hidden, axis=1, keepdims=True) + EPSILON)
        normed[band, :] = (hidden * inverse * gain_ref[...]).astype(BF16)
    for out_ref, group, out in zip(refs[len(heads) :], blocks, outs[len(heads) :]):
        for number, block in enumerate(group):
            start = pl.multiple_of(block(*place_now) * width, 128)
            out_ref[:rows, number * width : (number + 1) * width] = normed[:, pl.ds(start, width)]
        more = out_ref.shape[0] - rows
        for block in range(out_ref.shape[1] // lanes if more else 0):
            out_ref[rows:, block * lanes : (block + 1) * lanes] = extra_ref[
                block * more : (block + 1) * more, :
            ]
        out.start()
    for out in outs:
        out.wait()


def in_kernels(unit, rows):
    return unit % 64 == 0 and rows % BAND == 0


def prepared(weight, head_groups, pair, hidden, gain, groups, width, extra, place_now, kernels):
    rows, depth = hidden.shape
    total_width = len(groups[0]) * width
    more = extra.size // total_width
    if not kernels:
        now = [place_now[number] for number in range(4)]
        columns = [
            jnp.stack(
                [lax.dynamic_slice_in_dim(weight, head(*now) * pair, pair, 1) for head in group]
            )
            for group in head_groups
        ]
        hidden_float = hidden.astype(F32)
        inverse = lax.rsqrt(jnp.mean(hidden_float * hidden_float, axis=1, keepdims=True) + EPSILON)
        normed = (hidden_float * inverse * gain[None, :]).astype(BF16)
        results = []
        for group in groups:
            blocks = [
                lax.dynamic_slice_in_dim(normed, block(*now) * width, width, 1) for block in group
            ]
            rest = extra.reshape(more, total_width)
            results.append(jnp.concatenate([jnp.concatenate(blocks, axis=1), rest], axis=0))
        results[-1] = results[-1][:rows]
        return columns, results
    counts = [len(group) for group in head_groups]
    shapes = [(count, weight.shape[0], pair) for count in counts]
    shapes += [(rows + more, total_width)] * (len(groups) - 1) + [(rows, total_width)]
    results = pl.pallas_call(
        functools.partial(prepare_kernel, pair, head_groups, groups, width),
        out_shape=[jax.ShapeDtypeStruct(shape, BF16) for shape in shapes],
        in_specs=[pl.BlockSpec(memory_space=pltpu.SMEM)]
        + [pl.BlockSpec(memory_space=pltpu.HBM)] * 4,
        out_specs=[pl.BlockSpec(memory_space=pl.ANY)] * len(shapes),
        scratch_shapes=[pltpu.VMEM(shape, BF16) for shape in shapes]
        + [
            pltpu.VMEM(weight.shape, BF16),
            pltpu.VMEM((rows, depth), BF16),
            pltpu.VMEM((1, depth), F32),
            pltpu.VMEM(extra.shape, BF16),
            pltpu.VMEM((rows, depth), BF16),
            pltpu.SemaphoreType.DMA((3 + rows // BAND + len(shapes),)),
        ],
        compiler_params=pltpu.CompilerParams(vmem_limit_bytes=60 * 1024 * 1024),
        name="prepare",
    )(place_now, weight, hidden, gain[None, :], extra)
    return results[: len(counts)], results[len(counts) :]


def stage_kernel(pair, groups, place_ref, weight_ref, tokens_ref, *refs):
    place_now = [place_ref[number] for number in range(4)]
    for out_ref, heads in zip(refs, groups):
        for number, head in enumerate(heads):
            column = pl.multiple_of(head(*place_now) * pair, pair)
            out_ref[number] = weight_ref[:, pl.ds(column, pair)]
    refs[-1][...] = tokens_ref[...]


def staged(weight, groups, pair, tokens, place_now, kernels):
    if not kernels:
        now = [place_now[number] for number in range(4)]
        return [
            jnp.stack(
                [lax.dynamic_slice_in_dim(weight, head(*now) * pair, pair, 1) for head in heads]
            )
            for heads in groups
        ] + [tokens]
    shapes = [
        jax.ShapeDtypeStruct((len(heads), weight.shape[0], pair), BF16) for heads in groups
    ] + [jax.ShapeDtypeStruct(tokens.shape, BF16)]
    return call(
        functools.partial(stage_kernel, pair, groups),
        "stage",
        shapes,
        [place_now],
        [weight, tokens],
    )


def project_kernel(rows, heads, start, place, first_ref, kept_ref, traded_ref, *refs):
    token_refs, refs = refs[: 2 * CHIPS], refs[2 * CHIPS :]
    weight = refs[-1]
    out_refs = refs[-1 - heads : -1]
    blocks = refs[: -1 - heads]
    unit, pair = kept_ref.shape[1:]

    def put(head, tile, second, value):
        which = 1 - first_ref[tile] if second else first_ref[tile]
        base = pl.multiple_of(2 * unit * tile + which * unit, unit)
        weight[pl.ds(base, unit), head * pair : (head + 1) * pair] = value

    for head in range(heads):
        put(head, 0, 0, kept_ref[start + head])
        put(head, 0, 1, traded_ref[start + head])
        for number, block_ref in enumerate(blocks):
            put(head, 1 + number // 2, number % 2, block_ref[place + head])
    for number, token_ref in enumerate(token_refs):
        span = slice(number * rows, (number + 1) * rows)
        result = jnp.dot(token_ref[:rows, :], weight[...], preferred_element_type=F32).astype(BF16)
        for head, out_ref in enumerate(out_refs):
            out_ref[span, :] = result[:, head * pair : (head + 1) * pair]


def projected(tokens, heads, kept, traded, start, place, firsts, blocks, rows, kernels):
    unit, pair = kept.shape[1:]
    depth = tokens[0].shape[1]
    count = len(tokens) * rows
    firsts = jnp.stack(firsts).astype(jnp.int32)
    if not kernels:
        pieces = [kept[start : start + heads], traded[start : start + heads]]
        pieces += [block[place : place + heads] for block in blocks]
        ordered = []
        for tile in range(len(pieces) // 2):
            one, two = pieces[2 * tile : 2 * tile + 2]
            first = firsts[tile] == 0
            ordered += [jnp.where(first, one, two), jnp.where(first, two, one)]
        weight = jnp.concatenate(ordered, axis=1)
        tokens = jnp.concatenate([piece[:rows] for piece in tokens])
        result = jnp.einsum("td,hdc->htc", tokens, weight, preferred_element_type=F32)
        return list(result.astype(BF16))
    vmem = pl.BlockSpec(memory_space=pltpu.VMEM)
    smem = pl.BlockSpec(memory_space=pltpu.SMEM)
    return list(
        pl.pallas_call(
            functools.partial(project_kernel, rows, heads, start, place),
            out_shape=[jax.ShapeDtypeStruct((count, pair), BF16)] * heads,
            in_specs=[smem] + [vmem] * (2 + len(tokens) + len(blocks)),
            out_specs=[vmem] * heads,
            scratch_shapes=[pltpu.VMEM((depth, heads * pair), BF16)],
            compiler_params=pltpu.CompilerParams(vmem_limit_bytes=20 * 1024 * 1024),
            cost_estimate=pl.CostEstimate(
                flops=PROJECT_COST * 2 * heads * count * depth * pair,
                bytes_accessed=2 * count * depth,
                transcendentals=0,
            ),
            name="project",
        )(firsts, kept, traded, *tokens, *blocks)
    )


def query_kernel(lanes, place_ref, gain_ref, weight_ref, *refs):
    piece_refs, refs = refs[:-9], refs[-9:]
    results, own_ref, (stream, turned, parts, sems) = refs[:4], refs[4], refs[5:]
    unit = stream.shape[0] // KVH
    more = parts.shape[1]
    blocks = parts.shape[2] // lanes
    sources = [
        piece_ref.at[place] if len(piece_ref.shape) == 3 else piece_ref
        for piece_ref in piece_refs
        for place in range(CHIPS if len(piece_ref.shape) == 3 else 1)
    ]
    bases = [
        pl.multiple_of(
            ((place_ref[0] ^ number % CHIPS) * 2 + (place_ref[1] ^ number // CHIPS)) * unit, unit
        )
        for number in range(KVH)
    ]
    packed = sources[0].shape[1] != lanes
    copies = []
    for number, source in enumerate(sources):
        if packed:
            source, target = source.at[source.shape[0] - more :], parts.at[number]
        else:
            target = stream.at[pl.ds(bases[number], unit)]
        copies.append(pltpu.make_async_copy(source, target, sems.at[number]))
        copies[-1].start()
    for number, copy in enumerate(copies):
        copy.wait()
        for block in range(blocks if packed else 0):
            stream[pl.ds(pl.multiple_of(bases[number] + block * more, more), more), :] = parts[
                number, :, block * lanes : (block + 1) * lanes
            ]
    turned[...] = stream[...].astype(F32).T
    query_step(turned[...], gain_ref, weight_ref, *results)
    half = own_ref.shape[0]
    own_ref[...] = turned[pl.ds(pl.multiple_of(place_ref[1] * half, half), half), :].astype(BF16)


def query_step(rows, gain_ref, weight_ref, sent_ref, kept_ref, squares_sent_ref, squares_ref):
    squares = jnp.sum(rows * rows, axis=1, keepdims=True)
    scaled = (rows * gain_ref[...]).astype(BF16)
    partial = jnp.dot(scaled, weight_ref[...], preferred_element_type=F32)
    kept_ref[...] = partial
    sent_ref[...] = partial.astype(BF16)
    spread = jnp.broadcast_to(squares, squares_ref.shape)
    squares_ref[...] = spread
    across = spread.T[:8]
    high = across.astype(BF16)
    squares_sent_ref[:8] = high
    squares_sent_ref[8:] = (across - high.astype(F32)).astype(BF16)


def both_cores(place_ref, ours_ref, theirs_ref, rows):
    half = ours_ref.shape[0]
    for which, ref in ((place_ref[1], ours_ref), (1 - place_ref[1], theirs_ref)):
        rows[pl.ds(pl.multiple_of(which * half, half), half), :] = ref[...]


def later_query_kernel(place_ref, gain_ref, weight_ref, ours_ref, theirs_ref, *refs):
    results, rows = refs[:-1], refs[-1]
    both_cores(place_ref, ours_ref, theirs_ref, rows)
    query_step(rows[...].astype(F32), gain_ref, weight_ref, *results)


def own_rows_kernel(place_ref, ours_ref, theirs_ref, out_ref, rows, turned):
    both_cores(place_ref, ours_ref, theirs_ref, rows)
    unit = out_ref.shape[0]
    column = pl.multiple_of(place_ref[0] * 2 * unit, 2 * unit)
    turned[...] = rows[:, pl.ds(column, 2 * unit)].astype(F32).T
    out_ref[...] = turned[pl.ds(pl.multiple_of(place_ref[1] * unit, unit), unit), :].astype(BF16)


def spread_back(pair_ref, lanes):
    across = pair_ref[:8].astype(F32) + pair_ref[8:].astype(F32)
    return jnp.concatenate([across, jnp.zeros((lanes - 8, lanes), F32)], axis=0).T


def attend_kernel(depth, others, query_pos_ref, query_floor_ref, key_pos_ref, kv_ref, *refs):
    kept_ref, squares_ref = refs[:2]
    far = refs[2 : 2 + 2 * others]
    sent_ref, out_ref, totals_sent_ref, totals_ref = refs[2 + 2 * others :]
    lanes = kept_ref.shape[0]
    queries = kept_ref[...]
    squares = squares_ref[:, :1]
    for other in range(others):
        queries = queries + far[2 * other][...].astype(F32)
        squares = squares + spread_back(far[2 * other + 1], lanes)[:, :1]
    queries = (queries * lax.rsqrt(squares / depth + EPSILON)).astype(BF16)
    visible = (key_pos_ref[...] <= query_pos_ref[...]) & (key_pos_ref[...] >= query_floor_ref[...])
    keys, values = kv_ref[:, :HD], kv_ref[:, HD:]
    lane = lax.broadcasted_iota(jnp.int32, (lanes, lanes), 1)
    totals = jnp.zeros((lanes, lanes), F32)
    for head in range(queries.shape[1] // HD):
        span = slice(head * HD, (head + 1) * HD)
        scores = lax.dot_general(
            queries[:, span], keys, (((1,), (1,)), ((), ())), preferred_element_type=F32
        )
        capped = jnp.tanh(scores * (HD ** (-0.5) / CAP))
        weights = jnp.where(visible, jnp.exp2(capped * (CAP * LOG2_E)), 0.0)
        totals = jnp.where(lane == head, jnp.sum(weights, axis=1, keepdims=True), totals)
        weighted = jnp.dot(weights.astype(BF16), values, preferred_element_type=F32)
        out_ref[:, span] = weighted
        sent_ref[:, span] = weighted.astype(BF16)
    totals_ref[...] = totals
    across = totals.T[:8]
    high = across.astype(BF16)
    totals_sent_ref[:8] = high
    totals_sent_ref[8:] = (across - high.astype(F32)).astype(BF16)


def attended_of(others, kept_ref, totals_ref, far):
    lanes = kept_ref.shape[0]
    weighted = kept_ref[...]
    totals = totals_ref[...]
    for other in range(others):
        weighted = weighted + far[2 * other][...].astype(F32)
        totals = totals + spread_back(far[2 * other + 1], lanes)
    return jnp.concatenate(
        [
            (weighted[:, head * HD : (head + 1) * HD] / totals[:, head : head + 1]).astype(BF16)
            for head in range(weighted.shape[1] // HD)
        ],
        axis=1,
    )


def update_rows_kernel(others, place_ref, weight_ref, kept_ref, totals_ref, *refs):
    far, (own_ref, sent_ref, update) = refs[: 2 * others], refs[2 * others :]
    attended = attended_of(others, kept_ref, totals_ref, far)
    update[...] = lax.dot_general(
        attended, weight_ref[...], (((1,), (1,)), ((), ())), preferred_element_type=F32
    )
    half = own_ref.shape[0]
    for which, out_ref in ((place_ref[1], own_ref), (1 - place_ref[1], sent_ref)):
        rows = update[pl.ds(pl.multiple_of(which * half, half), half), :]
        out_ref[...] = rows.astype(out_ref.dtype)


def update_kernel(others, place_ref, weight_ref, kept_ref, totals_ref, *refs):
    far, (own_ref, sent_ref) = refs[: 2 * others], refs[2 * others :]
    unit = own_ref.shape[1]
    attended = attended_of(others, kept_ref, totals_ref, far)
    for core, out_ref in enumerate((own_ref, sent_ref)):
        for chip in range(CHIPS):
            base = ((place_ref[0] ^ chip) * 2 + (place_ref[1] ^ core)) * unit
            update = lax.dot_general(
                weight_ref[pl.ds(pl.multiple_of(base, unit), unit), :],
                attended,
                (((1,), (1,)), ((), ())),
                preferred_element_type=F32,
            )
            out_ref[chip] = update.astype(out_ref.dtype)


def call(kernel, name, out_shape, scalars, arrays, scratch=(), flops=0, loose=()):
    vmem = pl.BlockSpec(memory_space=pltpu.VMEM)
    smem = pl.BlockSpec(memory_space=pltpu.SMEM)
    return pl.pallas_call(
        kernel,
        out_shape=out_shape,
        in_specs=[smem] * len(scalars)
        + [vmem] * len(arrays)
        + [pl.BlockSpec(memory_space=pl.ANY)] * len(loose),
        out_specs=[vmem] * len(out_shape),
        scratch_shapes=list(scratch),
        compiler_params=pltpu.CompilerParams(vmem_limit_bytes=20 * 1024 * 1024),
        cost_estimate=pl.CostEstimate(
            flops=flops, bytes_accessed=sum(2 * a.size for a in arrays), transcendentals=0
        ),
        name=name,
    )(*scalars, *arrays, *loose)


def in_order(ours, theirs, core):
    low, high = jnp.where(core == 0, ours, theirs), jnp.where(core == 0, theirs, ours)
    return jnp.stack([low, high], axis=1).reshape(-1, ours.shape[-1])


def key_values_of(hidden, kv_gain, kv_weight, query_states, place_now, meanwhile):
    lane_count = lax.axis_size("row")
    tile_count = lane_count // KVH
    me = lax.axis_index("row")
    tile, chip, core = me // KVH, me // 2 % CHIPS, me % 2
    rows = hidden.shape[0]
    unit = kv_weight.shape[0]
    pair = 2 * HD
    share = lax.axis_size("groups") == 2
    part = lax.axis_index("groups") if share else 0

    order = [place for round_ in ROUNDS for place in round_]

    def kept_head(place):
        return lambda chip, core, tile, part: (chip ^ place) * 2 + core

    def sent_head(place):
        return lambda chip, core, tile, part: ((chip ^ place) * 2 + core) ^ part

    def other_head(place):
        return lambda chip, core, tile, part: (chip ^ place) * 2 + 1 - core

    def block(place, j):
        return lambda chip, core, tile, part: (tile ^ j) * CHIPS + (chip ^ place)

    kernels = in_kernels(unit, rows)
    width = 2 * unit
    sent, features = prepared(
        kv_weight,
        [[sent_head(place) for place in round_] for round_ in ROUNDS],
        pair,
        hidden,
        kv_gain,
        [[block(place, j) for j in range(tile_count)] for place in range(CHIPS)],
        width,
        query_states,
        place_now,
        kernels,
    )
    def to_tile(value, j, flip):
        if not share:
            return swapped(value, j * KVH)
        pairs = [
            (g * lane_count + d, g * lane_count + (d ^ (j * KVH) ^ (g if flip else 0)))
            for g in range(2)
            for d in range(lane_count)
        ]
        return lax.ppermute(value, ("groups", "row"), pairs)

    far = [[to_tile(value, j, True) for j in range(1, tile_count)] for value in sent]
    held = [features[0]] + [swapped(features[p], 2 * p) for p in range(1, CHIPS)]

    kv_weight, own, _ = lax.optimization_barrier((kv_weight, held[0], far[0]))
    kept, traded, own = staged(
        kv_weight,
        [[kept_head(place) for place in order], [other_head(place) for place in order]],
        pair,
        own,
        place_now,
        kernels,
    )
    traded = swapped(traded, 1)
    held[1], kept, own = lax.optimization_barrier((held[1], kept, own))

    def shared(number):
        start = sum(len(round_) for round_ in ROUNDS[:number])
        return [
            swapped(value, 1, "groups")
            if share
            else to_tile(traded[start : start + len(ROUNDS[number])], j, False)
            for j, value in enumerate(far[number], 1)
        ]

    firsts = [core] + [core ^ part] * (tile_count - 1)
    halves = [shared(number) for number in range(len(ROUNDS))]
    held[2], held[3], halves[0], far = lax.optimization_barrier((held[2], held[3], halves[0], far))
    tokens = held + [swapped(piece, 1) for piece in held]
    tokens[0] = own
    last_rows = swapped(held[2][rows:], 2)
    total = None
    done = 0
    for number, round_ in enumerate(ROUNDS):
        blocks = [piece for pair_ in zip(far[number], halves[number]) for piece in pair_]
        partials = []
        for inner in range(0, len(round_), HEADS_AT_ONCE[number]):
            partials += projected(
                tokens,
                HEADS_AT_ONCE[number],
                kept,
                traded,
                done + inner,
                inner,
                firsts,
                blocks,
                rows,
                kernels,
            )
        done += len(round_)
        if number == 0:
            partials, tokens, last_rows = lax.optimization_barrier((partials, tokens, last_rows))
            query_rows = tokens[: CHIPS - 1] + [last_rows] + tokens[CHIPS:-1] + [swapped(last_rows, 1)]
            results = meanwhile(query_rows)
        for partial, place in zip(partials, round_):
            if place:
                partial = swapped(partial, 2 * place)
            pieces = partial.reshape(2, CHIPS, rows, pair).astype(F32)
            pieces = jnp.stack([pieces[:, j ^ place] for j in range(CHIPS)], axis=1)
            total = pieces if total is None else total + pieces
    key_values = total.astype(BF16).reshape(2 * CHIPS * rows, pair)
    sources = jnp.stack(
        [tile * KVH + (chip ^ j) * 2 + (core ^ e) for e in range(2) for j in range(CHIPS)]
    )
    key_pos = (sources[:, None] * rows + jnp.arange(rows, dtype=jnp.int32)[None, :]).reshape(-1)
    return key_values, key_pos, results


def gather_rows(own):
    ours = [own] + [swapped(own, 2 * place) for place in range(1, CHIPS)]
    theirs = swapped(jnp.stack(ours), 1)
    return ours + [theirs]


def scatter_rows(kept, sent):
    both = kept + swapped(sent, 1).astype(F32)
    total = both[0]
    for place in range(1, CHIPS):
        total = total + swapped(both[place].astype(BF16), 2 * place).astype(F32)
    return total


def reduce_rows(kept, sent):
    both = (kept + swapped(sent, 1).astype(F32)).astype(BF16)
    halves = jnp.split(both, 2, axis=1)
    for masks in ((2, 4), (4, 2)):
        halves = [
            (half.astype(F32) + swapped(half, mask).astype(F32)).astype(BF16)
            for half, mask in zip(halves, masks)
        ]
    return jnp.concatenate(halves, axis=1)


def attend_rows(queries, query_pos, query_floor, key_values, key_pos):
    row_count = queries.shape[0]
    head_count = queries.shape[1] // HD
    key_part = key_values[:, :HD]
    value_part = key_values[:, HD:]
    grouped = queries.reshape(row_count, head_count, HD)
    scores = jnp.einsum("rhd,kd->rhk", grouped, key_part, preferred_element_type=F32) * HD ** (-0.5)
    capped = CAP * jnp.tanh(scores / CAP)
    visible = (key_pos[None, :] <= query_pos[:, None]) & (key_pos[None, :] >= query_floor[:, None])
    weights = jnp.where(visible[:, None, :], jnp.exp(capped), 0.0)
    totals = jnp.sum(weights, axis=2)
    weighted = jnp.einsum(
        "rhk,kd->rhd", weights.astype(BF16), value_part, preferred_element_type=F32
    )
    return weighted.reshape(row_count, head_count * HD), totals


def on_device(
    hidden, kv_gain, kv_weight, query_states, query_gain, query_weight, output_weight, block_bounds
):
    tile_count = lax.axis_size("row") // KVH
    tile = lax.axis_index("row") // KVH
    depth = hidden.shape[1]
    slice_depth = query_weight.shape[2]
    query_count = query_states.shape[1]
    row_number = jnp.arange(query_count, dtype=jnp.int32)
    query_pos = jnp.repeat(block_bounds[:, 1], QBLK) + row_number % QBLK
    query_floor = jnp.repeat(block_bounds[:, 0], QBLK)

    me = lax.axis_index("row")
    chip, core = me // 2 % CHIPS, me % 2
    part = lax.axis_index("groups") if lax.axis_size("groups") == 2 else 0
    place_now = jnp.stack([chip, core, tile, part]).astype(jnp.int32)
    unit, rows = query_states.shape[0], hidden.shape[0]
    kernels = in_kernels(unit, rows)
    width = query_weight.shape[3]
    own_rows = query_states
    small = jax.ShapeDtypeStruct((16, query_count), BF16)
    spread = jax.ShapeDtypeStruct((query_count, query_count), F32)
    wide = [jax.ShapeDtypeStruct((query_count, width), kind) for kind in (BF16, F32)]
    flops = 2 * query_count * slice_depth * width
    halved = jax.ShapeDtypeStruct((query_count // 2, slice_depth), BF16)

    def query_parts(section, pieces):
        gain = lax.dynamic_slice_in_dim(query_gain[section], tile * slice_depth, slice_depth)
        if not kernels:
            pieces = [
                part
                for piece in pieces
                for part in (piece if piece.ndim == 3 else [piece[-(own_rows.size // piece.shape[1]) :]])
            ]
            pieces = [piece.reshape(own_rows.shape) for piece in pieces]
            ours, theirs = (
                jnp.stack(natural(half, chip)) for half in (pieces[:CHIPS], pieces[CHIPS:])
            )
            stream = in_order(ours, theirs, core).astype(F32)
            scaled = (stream * gain[:, None]).astype(BF16)
            partial = lax.dot_general(
                scaled, query_weight[section, 0], (((0,), (0,)), ((), ())), preferred_element_type=F32
            )
            squares = jnp.sum(stream * stream, axis=0)
            return partial.astype(BF16), partial, squares.astype(BF16), squares
        return call(
            functools.partial(query_kernel, query_count),
            "query",
            wide + [small, spread, halved],
            [place_now],
            [gain[None, :], query_weight[section, 0]],
            [
                pltpu.VMEM((slice_depth, query_count), BF16),
                pltpu.VMEM((query_count, slice_depth), F32),
                pltpu.VMEM((KVH, own_rows.size // (2 * unit * tile_count), 2 * unit * tile_count), BF16),
                pltpu.SemaphoreType.DMA((KVH,)),
            ],
            flops,
            pieces,
        )

    key_values, key_pos, parts = key_values_of(
        hidden, kv_gain, kv_weight, query_states, place_now, functools.partial(query_parts, 0)
    )
    positions = [query_pos[:, None], query_floor[:, None], key_pos[None, :]]
    if kernels:
        stream, parts = parts[4], parts[:4]
    sections = query_gain.shape[0]
    for section in range(sections):
        if section and not kernels:
            parts = query_parts(section, gather_rows(own_rows))
        sent, partial, squares_sent, squares = parts
        if kernels:
            far = zip(over_tiles(sent, tile_count)[1:], over_tiles(squares_sent, tile_count)[1:])
            sent, weighted, totals_sent, totals = call(
                functools.partial(attend_kernel, depth, tile_count - 1),
                "attend",
                wide + [small, spread],
                [],
                positions + [key_values, partial, squares] + [value for pair in far for value in pair],
                (),
                flops // 2,
            )
            far = zip(over_tiles(sent, tile_count)[1:], over_tiles(totals_sent, tile_count)[1:])
            arrays = [output_weight[section, 0], weighted, totals]
            arrays += [value for pair in far for value in pair]
            if section + 1 < sections:
                kept, sent = call(
                    functools.partial(update_rows_kernel, tile_count - 1),
                    "update",
                    [jax.ShapeDtypeStruct(halved.shape, F32), halved],
                    [place_now],
                    arrays,
                    [pltpu.VMEM((query_count, slice_depth), F32)],
                    flops,
                )
                stream = (stream.astype(F32) + reduce_rows(kept, sent).astype(F32)).astype(BF16)
                theirs = swapped(stream, 1)
                gain = lax.dynamic_slice_in_dim(
                    query_gain[section + 1], tile * slice_depth, slice_depth
                )
                parts = call(
                    later_query_kernel,
                    "query",
                    wide + [small, spread],
                    [place_now],
                    [gain[None, :], query_weight[section + 1, 0], stream, theirs],
                    [pltpu.VMEM((query_count, slice_depth), BF16)],
                    flops,
                )
                own_rows = call(
                    own_rows_kernel,
                    "own_rows",
                    [jax.ShapeDtypeStruct(own_rows.shape, BF16)],
                    [place_now],
                    [stream, theirs],
                    [
                        pltpu.VMEM((query_count, slice_depth), BF16),
                        pltpu.VMEM((2 * unit, query_count), F32),
                    ],
                )[0]
                continue
            shape = (CHIPS, unit, query_count)
            kept, sent = call(
                functools.partial(update_kernel, tile_count - 1),
                "update",
                [jax.ShapeDtypeStruct(shape, F32), jax.ShapeDtypeStruct(shape, BF16)],
                [place_now],
                arrays,
                (),
                flops,
            )
        else:
            square_sum = sum(over_tiles(squares_sent, tile_count)[1:], squares)
            query_sum = sum(over_tiles(sent, tile_count)[1:], partial)
            inverse = lax.rsqrt(square_sum / depth + EPSILON)
            queries = (query_sum * inverse[:, None]).astype(BF16)
            weighted, totals = attend_rows(queries, query_pos, query_floor, key_values, key_pos)
            total_sum = sum(over_tiles(totals.astype(BF16), tile_count)[1:], totals)
            weighted_sum = sum(over_tiles(weighted.astype(BF16), tile_count)[1:], weighted)
            attended = (
                (weighted_sum.reshape(query_count, QPK, HD) / total_sum[:, :, None])
                .reshape(query_count, QPK * HD)
                .astype(BF16)
            )
            update = lax.dot_general(
                output_weight[section, 0],
                attended,
                (((1,), (1,)), ((), ())),
                preferred_element_type=F32,
            )
            split = update.reshape(CHIPS, 2, unit, query_count)
            kept = jnp.where(core == 0, split[:, 0], split[:, 1])
            sent = jnp.where(core == 0, split[:, 1], split[:, 0]).astype(BF16)
            kept, sent = (jnp.stack(natural(value, chip)) for value in (kept, sent))
        own_rows = (own_rows.astype(F32) + scatter_rows(kept, sent)).astype(BF16)
    return own_rows


def solution(mesh):
    in_specs = (
        P(("groups", "row"), None),
        P(),
        P("row", None),
        P("row", "groups"),
        P(),
        P(None, "row", None, None),
        P(None, "row", None, None),
        P("groups", None),
    )
    return jax.shard_map(
        on_device, mesh=mesh, in_specs=in_specs, out_specs=P("row", "groups"), check_vma=False
    )
```

```python
import functools

import jax
import jax.numpy as jnp
from jax import lax
from jax.experimental import pallas as pl
from jax.experimental.pallas import tpu as pltpu
from jax.sharding import PartitionSpec as P

KVH = 8
HD = 128
QPK = 5
QBLK = 64
CAP = 30.0
EPSILON = 1e-05
LOG2_E = 1.4426950408889634
BF16 = jnp.bfloat16
F32 = jnp.float32

CHIPS = KVH // 2
ROUNDS = ((2, 1), (3, 0))
PROJECT_COST = 8
BAND = 32
HEADS_AT_ONCE = (2, 2)


def swapped(value, mask, axis="row"):
    pairs = [(source, source ^ mask) for source in range(lax.axis_size(axis))]
    return lax.ppermute(value, axis, pairs)


def over_tiles(value, tile_count):
    values = [value]
    mask = 1
    while mask < tile_count:
        if len(values) == 1:
            values.append(swapped(values[0], mask * KVH))
        else:
            got = swapped(jnp.stack(values), mask * KVH)
            values.extend(got[place] for place in range(len(values)))
        mask *= 2
    return values


def natural(pieces, index):
    pieces = list(pieces)
    bit = 1
    while bit < len(pieces):
        upper = index // bit % 2 == 1
        pieces = [jnp.where(upper, pieces[j ^ bit], pieces[j]) for j in range(len(pieces))]
        bit *= 2
    return pieces


def here():
    me = lax.axis_index("row")
    part = lax.axis_index("groups") if lax.axis_size("groups") == 2 else 0
    return [me // 2 % CHIPS, me % 2, me // KVH, part]


def prepare_kernel(
    pair, heads, blocks, width, weight_any, hidden_any, gain_any, extra_any, *refs
):
    weight_ref, hidden_ref, gain_ref, extra_ref, normed, sems = refs[-6:]
    results = len(heads) + len(blocks)
    targets, refs = refs[:results], refs[results:-6]
    place_now = here()
    rows = hidden_ref.shape[0]
    lanes = extra_ref.shape[1]
    bands = [slice(band, band + BAND) for band in range(0, rows, BAND)]
    pairs = [(weight_any, weight_ref), (gain_any, gain_ref), (extra_any, extra_ref)]
    pairs += [(hidden_any.at[band], hidden_ref.at[band]) for band in bands]
    copies = [
        pltpu.make_async_copy(source, target, sems.at[number])
        for number, (source, target) in enumerate(pairs)
    ]
    outs = [
        pltpu.make_async_copy(source, target, sems.at[len(copies) + number])
        for number, (source, target) in enumerate(zip(refs, targets))
    ]
    for copy in copies:
        copy.start()
    copies[0].wait()
    for head_ref, group, out in zip(refs, heads, outs):
        for number, head in enumerate(group):
            column = pl.multiple_of(head(*place_now) * pair, pair)
            head_ref[number] = weight_ref[:, pl.ds(column, pair)]
        out.start()
    copies[1].wait()
    copies[2].wait()
    for band, copy in zip(bands, copies[3:]):
        copy.wait()
        hidden = hidden_ref[band, :].astype(F32)
        inverse = lax.rsqrt(jnp.mean(hidden * hidden, axis=1, keepdims=True) + EPSILON)
        normed[band, :] = (hidden * inverse * gain_ref[...]).astype(BF16)
    for out_ref, group, out in zip(refs[len(heads) :], blocks, outs[len(heads) :]):
        for number, block in enumerate(group):
            start = pl.multiple_of(block(*place_now) * width, 128)
            out_ref[:rows, number * width : (number + 1) * width] = normed[:, pl.ds(start, width)]
        more = out_ref.shape[0] - rows
        for block in range(out_ref.shape[1] // lanes if more else 0):
            out_ref[rows:, block * lanes : (block + 1) * lanes] = extra_ref[
                block * more : (block + 1) * more, :
            ]
        out.start()
    for out in outs:
        out.wait()


def in_kernels(unit, rows):
    return unit % 64 == 0 and rows % BAND == 0


def prepared(weight, head_groups, pair, hidden, gain, groups, width, extra, place_now, kernels):
    rows, depth = hidden.shape
    total_width = len(groups[0]) * width
    more = extra.size // total_width
    if not kernels:
        now = [place_now[number] for number in range(4)]
        columns = [
            jnp.stack(
                [lax.dynamic_slice_in_dim(weight, head(*now) * pair, pair, 1) for head in group]
            )
            for group in head_groups
        ]
        hidden_float = hidden.astype(F32)
        inverse = lax.rsqrt(jnp.mean(hidden_float * hidden_float, axis=1, keepdims=True) + EPSILON)
        normed = (hidden_float * inverse * gain[None, :]).astype(BF16)
        results = []
        for group in groups:
            blocks = [
                lax.dynamic_slice_in_dim(normed, block(*now) * width, width, 1) for block in group
            ]
            rest = extra.reshape(more, total_width)
            results.append(jnp.concatenate([jnp.concatenate(blocks, axis=1), rest], axis=0))
        results[-1] = results[-1][:rows]
        return columns, results
    counts = [len(group) for group in head_groups]
    shapes = [(count, weight.shape[0], pair) for count in counts]
    shapes += [(rows + more, total_width)] * (len(groups) - 1) + [(rows, total_width)]
    results = pl.pallas_call(
        functools.partial(prepare_kernel, pair, head_groups, groups, width),
        out_shape=[jax.ShapeDtypeStruct(shape, BF16) for shape in shapes],
        in_specs=[pl.BlockSpec(memory_space=pltpu.HBM)] * 4,
        out_specs=[pl.BlockSpec(memory_space=pl.ANY)] * len(shapes),
        scratch_shapes=[pltpu.VMEM(shape, BF16) for shape in shapes]
        + [
            pltpu.VMEM(weight.shape, BF16),
            pltpu.VMEM((rows, depth), BF16),
            pltpu.VMEM((1, depth), F32),
            pltpu.VMEM(extra.shape, BF16),
            pltpu.VMEM((rows, depth), BF16),
            pltpu.SemaphoreType.DMA((3 + rows // BAND + len(shapes),)),
        ],
        compiler_params=pltpu.CompilerParams(vmem_limit_bytes=60 * 1024 * 1024),
        name="prepare",
    )(weight, hidden, gain[None, :], extra)
    return results[: len(counts)], results[len(counts) :]


def stage_kernel(pair, groups, place_ref, weight_ref, tokens_ref, *refs):
    place_now = [place_ref[number] for number in range(4)]
    for out_ref, heads in zip(refs, groups):
        for number, head in enumerate(heads):
            column = pl.multiple_of(head(*place_now) * pair, pair)
            out_ref[number] = weight_ref[:, pl.ds(column, pair)]
    refs[-1][...] = tokens_ref[...]


def staged(weight, groups, pair, tokens, place_now, kernels):
    if not kernels:
        now = [place_now[number] for number in range(4)]
        return [
            jnp.stack(
                [lax.dynamic_slice_in_dim(weight, head(*now) * pair, pair, 1) for head in heads]
            )
            for heads in groups
        ] + [tokens]
    shapes = [
        jax.ShapeDtypeStruct((len(heads), weight.shape[0], pair), BF16) for heads in groups
    ] + [jax.ShapeDtypeStruct(tokens.shape, BF16)]
    return call(
        functools.partial(stage_kernel, pair, groups),
        "stage",
        shapes,
        [place_now],
        [weight, tokens],
    )


def project_kernel(rows, heads, start, place, first_ref, kept_ref, traded_ref, *refs):
    token_refs, refs = refs[: 2 * CHIPS], refs[2 * CHIPS :]
    weight = refs[-1]
    out_refs = refs[-1 - heads : -1]
    blocks = refs[: -1 - heads]
    unit, pair = kept_ref.shape[1:]

    def put(head, tile, second, value):
        which = 1 - first_ref[tile] if second else first_ref[tile]
        base = pl.multiple_of(2 * unit * tile + which * unit, unit)
        weight[pl.ds(base, unit), head * pair : (head + 1) * pair] = value

    for head in range(heads):
        put(head, 0, 0, kept_ref[start + head])
        put(head, 0, 1, traded_ref[start + head])
        for number, block_ref in enumerate(blocks):
            put(head, 1 + number // 2, number % 2, block_ref[place + head])
    for number, token_ref in enumerate(token_refs):
        span = slice(number * rows, (number + 1) * rows)
        result = jnp.dot(token_ref[:rows, :], weight[...], preferred_element_type=F32).astype(BF16)
        for head, out_ref in enumerate(out_refs):
            out_ref[span, :] = result[:, head * pair : (head + 1) * pair]


def projected(tokens, heads, kept, traded, start, place, firsts, blocks, rows, kernels):
    unit, pair = kept.shape[1:]
    depth = tokens[0].shape[1]
    count = len(tokens) * rows
    firsts = jnp.stack(firsts).astype(jnp.int32)
    if not kernels:
        pieces = [kept[start : start + heads], traded[start : start + heads]]
        pieces += [block[place : place + heads] for block in blocks]
        ordered = []
        for tile in range(len(pieces) // 2):
            one, two = pieces[2 * tile : 2 * tile + 2]
            first = firsts[tile] == 0
            ordered += [jnp.where(first, one, two), jnp.where(first, two, one)]
        weight = jnp.concatenate(ordered, axis=1)
        tokens = jnp.concatenate([piece[:rows] for piece in tokens])
        result = jnp.einsum("td,hdc->htc", tokens, weight, preferred_element_type=F32)
        return list(result.astype(BF16))
    vmem = pl.BlockSpec(memory_space=pltpu.VMEM)
    smem = pl.BlockSpec(memory_space=pltpu.SMEM)
    return list(
        pl.pallas_call(
            functools.partial(project_kernel, rows, heads, start, place),
            out_shape=[jax.ShapeDtypeStruct((count, pair), BF16)] * heads,
            in_specs=[smem] + [vmem] * (2 + len(tokens) + len(blocks)),
            out_specs=[vmem] * heads,
            scratch_shapes=[pltpu.VMEM((depth, heads * pair), BF16)],
            compiler_params=pltpu.CompilerParams(vmem_limit_bytes=20 * 1024 * 1024),
            cost_estimate=pl.CostEstimate(
                flops=PROJECT_COST * 2 * heads * count * depth * pair,
                bytes_accessed=2 * count * depth,
                transcendentals=0,
            ),
            name="project",
        )(firsts, kept, traded, *tokens, *blocks)
    )


def query_kernel(lanes, place_ref, gain_ref, weight_ref, *refs):
    piece_refs, refs = refs[:-9], refs[-9:]
    results, own_ref, (stream, turned, parts, sems) = refs[:4], refs[4], refs[5:]
    unit = stream.shape[0] // KVH
    more = parts.shape[1]
    blocks = parts.shape[2] // lanes
    sources = [
        piece_ref.at[place] if len(piece_ref.shape) == 3 else piece_ref
        for piece_ref in piece_refs
        for place in range(CHIPS if len(piece_ref.shape) == 3 else 1)
    ]
    bases = [
        pl.multiple_of(
            ((place_ref[0] ^ number % CHIPS) * 2 + (place_ref[1] ^ number // CHIPS)) * unit, unit
        )
        for number in range(KVH)
    ]
    packed = sources[0].shape[1] != lanes
    copies = []
    for number, source in enumerate(sources):
        if packed:
            source, target = source.at[source.shape[0] - more :], parts.at[number]
        else:
            target = stream.at[pl.ds(bases[number], unit)]
        copies.append(pltpu.make_async_copy(source, target, sems.at[number]))
        copies[-1].start()
    for number, copy in enumerate(copies):
        copy.wait()
        for block in range(blocks if packed else 0):
            stream[pl.ds(pl.multiple_of(bases[number] + block * more, more), more), :] = parts[
                number, :, block * lanes : (block + 1) * lanes
            ]
    turned[...] = stream[...].astype(F32).T
    query_step(turned[...], gain_ref, weight_ref, *results)
    half = own_ref.shape[0]
    own_ref[...] = turned[pl.ds(pl.multiple_of(place_ref[1] * half, half), half), :].astype(BF16)


def query_step(rows, gain_ref, weight_ref, sent_ref, kept_ref, squares_sent_ref, squares_ref):
    squares = jnp.sum(rows * rows, axis=1, keepdims=True)
    scaled = (rows * gain_ref[...]).astype(BF16)
    partial = jnp.dot(scaled, weight_ref[...], preferred_element_type=F32)
    kept_ref[...] = partial
    sent_ref[...] = partial.astype(BF16)
    spread = jnp.broadcast_to(squares, squares_ref.shape)
    squares_ref[...] = spread
    across = spread.T[:8]
    high = across.astype(BF16)
    squares_sent_ref[:8] = high
    squares_sent_ref[8:] = (across - high.astype(F32)).astype(BF16)


def both_cores(place_ref, ours_ref, theirs_ref, rows):
    half = ours_ref.shape[0]
    for which, ref in ((place_ref[1], ours_ref), (1 - place_ref[1], theirs_ref)):
        rows[pl.ds(pl.multiple_of(which * half, half), half), :] = ref[...]


def later_query_kernel(place_ref, gain_ref, weight_ref, ours_ref, theirs_ref, *refs):
    results, rows = refs[:-1], refs[-1]
    both_cores(place_ref, ours_ref, theirs_ref, rows)
    query_step(rows[...].astype(F32), gain_ref, weight_ref, *results)


def own_rows_kernel(place_ref, ours_ref, theirs_ref, out_ref, rows, turned):
    both_cores(place_ref, ours_ref, theirs_ref, rows)
    unit = out_ref.shape[0]
    column = pl.multiple_of(place_ref[0] * 2 * unit, 2 * unit)
    turned[...] = rows[:, pl.ds(column, 2 * unit)].astype(F32).T
    out_ref[...] = turned[pl.ds(pl.multiple_of(place_ref[1] * unit, unit), unit), :].astype(BF16)


def spread_back(pair_ref, lanes):
    across = pair_ref[:8].astype(F32) + pair_ref[8:].astype(F32)
    return jnp.concatenate([across, jnp.zeros((lanes - 8, lanes), F32)], axis=0).T


def attend_kernel(depth, others, query_pos_ref, query_floor_ref, key_pos_ref, kv_ref, *refs):
    kept_ref, squares_ref = refs[:2]
    far = refs[2 : 2 + 2 * others]
    sent_ref, out_ref, totals_sent_ref, totals_ref = refs[2 + 2 * others :]
    lanes = kept_ref.shape[0]
    queries = kept_ref[...]
    squares = squares_ref[:, :1]
    for other in range(others):
        queries = queries + far[2 * other][...].astype(F32)
        squares = squares + spread_back(far[2 * other + 1], lanes)[:, :1]
    queries = (queries * lax.rsqrt(squares / depth + EPSILON)).astype(BF16)
    visible = (key_pos_ref[...] <= query_pos_ref[...]) & (key_pos_ref[...] >= query_floor_ref[...])
    keys, values = kv_ref[:, :HD], kv_ref[:, HD:]
    lane = lax.broadcasted_iota(jnp.int32, (lanes, lanes), 1)
    totals = jnp.zeros((lanes, lanes), F32)
    heads = queries.shape[1] // HD
    stacked = jnp.concatenate([queries[:, h * HD : (h + 1) * HD] for h in range(heads)], axis=0)
    scores = lax.dot_general(
        stacked, keys, (((1,), (1,)), ((), ())), preferred_element_type=F32
    )
    capped = jnp.tanh(scores * (HD ** (-0.5) / CAP))
    weights = jnp.exp2(capped * (CAP * LOG2_E)).reshape(heads, lanes, -1)
    weights = jnp.where(visible[None], weights, 0.0)
    sums = jnp.sum(weights, axis=2, keepdims=True)
    weighted = jnp.dot(
        weights.astype(BF16).reshape(heads * lanes, -1), values, preferred_element_type=F32
    )
    for head in range(heads):
        span = slice(head * HD, (head + 1) * HD)
        totals = jnp.where(lane == head, sums[head], totals)
        part = weighted[head * lanes : (head + 1) * lanes]
        out_ref[:, span] = part
        sent_ref[:, span] = part.astype(BF16)
    totals_ref[...] = totals
    across = totals.T[:8]
    high = across.astype(BF16)
    totals_sent_ref[:8] = high
    totals_sent_ref[8:] = (across - high.astype(F32)).astype(BF16)


def attended_of(others, kept_ref, totals_ref, far):
    lanes = kept_ref.shape[0]
    weighted = kept_ref[...]
    totals = totals_ref[...]
    for other in range(others):
        weighted = weighted + far[2 * other][...].astype(F32)
        totals = totals + spread_back(far[2 * other + 1], lanes)
    return jnp.concatenate(
        [
            (weighted[:, head * HD : (head + 1) * HD] / totals[:, head : head + 1]).astype(BF16)
            for head in range(weighted.shape[1] // HD)
        ],
        axis=1,
    )


def update_rows_kernel(others, place_ref, weight_ref, kept_ref, totals_ref, *refs):
    far, (own_ref, sent_ref, update) = refs[: 2 * others], refs[2 * others :]
    attended = attended_of(others, kept_ref, totals_ref, far)
    update[...] = lax.dot_general(
        attended, weight_ref[...], (((1,), (1,)), ((), ())), preferred_element_type=F32
    )
    half = own_ref.shape[0]
    for which, out_ref in ((place_ref[1], own_ref), (1 - place_ref[1], sent_ref)):
        rows = update[pl.ds(pl.multiple_of(which * half, half), half), :]
        out_ref[...] = rows.astype(out_ref.dtype)


def update_kernel(others, place_ref, weight_ref, kept_ref, totals_ref, *refs):
    far, (own_ref, sent_ref) = refs[: 2 * others], refs[2 * others :]
    unit = own_ref.shape[1]
    attended = attended_of(others, kept_ref, totals_ref, far)
    for core, out_ref in enumerate((own_ref, sent_ref)):
        for chip in range(CHIPS):
            base = ((place_ref[0] ^ chip) * 2 + (place_ref[1] ^ core)) * unit
            update = lax.dot_general(
                weight_ref[pl.ds(pl.multiple_of(base, unit), unit), :],
                attended,
                (((1,), (1,)), ((), ())),
                preferred_element_type=F32,
            )
            out_ref[chip] = update.astype(out_ref.dtype)


def call(kernel, name, out_shape, scalars, arrays, scratch=(), flops=0, loose=()):
    vmem = pl.BlockSpec(memory_space=pltpu.VMEM)
    smem = pl.BlockSpec(memory_space=pltpu.SMEM)
    return pl.pallas_call(
        kernel,
        out_shape=out_shape,
        in_specs=[smem] * len(scalars)
        + [vmem] * len(arrays)
        + [pl.BlockSpec(memory_space=pl.ANY)] * len(loose),
        out_specs=[vmem] * len(out_shape),
        scratch_shapes=list(scratch),
        compiler_params=pltpu.CompilerParams(vmem_limit_bytes=20 * 1024 * 1024),
        cost_estimate=pl.CostEstimate(
            flops=flops, bytes_accessed=sum(2 * a.size for a in arrays), transcendentals=0
        ),
        name=name,
    )(*scalars, *arrays, *loose)


def in_order(ours, theirs, core):
    low, high = jnp.where(core == 0, ours, theirs), jnp.where(core == 0, theirs, ours)
    return jnp.stack([low, high], axis=1).reshape(-1, ours.shape[-1])


def key_values_of(hidden, kv_gain, kv_weight, query_states, place_now, meanwhile):
    lane_count = lax.axis_size("row")
    tile_count = lane_count // KVH
    me = lax.axis_index("row")
    tile, chip, core = me // KVH, me // 2 % CHIPS, me % 2
    rows = hidden.shape[0]
    unit = kv_weight.shape[0]
    pair = 2 * HD
    share = lax.axis_size("groups") == 2
    part = lax.axis_index("groups") if share else 0

    order = [place for round_ in ROUNDS for place in round_]

    def kept_head(place):
        return lambda chip, core, tile, part: (chip ^ place) * 2 + core

    def sent_head(place):
        return lambda chip, core, tile, part: ((chip ^ place) * 2 + core) ^ part

    def other_head(place):
        return lambda chip, core, tile, part: (chip ^ place) * 2 + 1 - core

    def block(place, j):
        return lambda chip, core, tile, part: (tile ^ j) * CHIPS + (chip ^ place)

    kernels = in_kernels(unit, rows)
    width = 2 * unit
    sent, features = prepared(
        kv_weight,
        [[sent_head(place) for place in round_] for round_ in ROUNDS],
        pair,
        hidden,
        kv_gain,
        [[block(place, j) for j in range(tile_count)] for place in range(CHIPS)],
        width,
        query_states,
        place_now,
        kernels,
    )
    def to_tile(value, j, flip):
        if not share:
            return swapped(value, j * KVH)
        pairs = [
            (g * lane_count + d, g * lane_count + (d ^ (j * KVH) ^ (g if flip else 0)))
            for g in range(2)
            for d in range(lane_count)
        ]
        return lax.ppermute(value, ("groups", "row"), pairs)

    far = [[to_tile(value, j, True) for j in range(1, tile_count)] for value in sent]
    held = [features[0]] + [swapped(features[p], 2 * p) for p in range(1, CHIPS)]

    kv_weight, own, _ = lax.optimization_barrier((kv_weight, held[0], far[0]))
    kept, traded, own = staged(
        kv_weight,
        [[kept_head(place) for place in order], [other_head(place) for place in order]],
        pair,
        own,
        place_now,
        kernels,
    )
    traded = swapped(traded, 1)
    held[1], kept, own = lax.optimization_barrier((held[1], kept, own))

    def shared(number):
        start = sum(len(round_) for round_ in ROUNDS[:number])
        return [
            swapped(value, 1, "groups")
            if share
            else to_tile(traded[start : start + len(ROUNDS[number])], j, False)
            for j, value in enumerate(far[number], 1)
        ]

    firsts = [core] + [core ^ part] * (tile_count - 1)
    halves = [shared(number) for number in range(len(ROUNDS))]
    held[2], held[3], halves[0], far = lax.optimization_barrier((held[2], held[3], halves[0], far))
    tokens = held + [swapped(piece, 1) for piece in held]
    tokens[0] = own
    last_rows = swapped(held[2][rows:], 2)
    total = None
    done = 0
    for number, round_ in enumerate(ROUNDS):
        blocks = [piece for pair_ in zip(far[number], halves[number]) for piece in pair_]
        partials = []
        for inner in range(0, len(round_), HEADS_AT_ONCE[number]):
            partials += projected(
                tokens,
                HEADS_AT_ONCE[number],
                kept,
                traded,
                done + inner,
                inner,
                firsts,
                blocks,
                rows,
                kernels,
            )
        done += len(round_)
        if number == 0:
            partials, tokens, last_rows = lax.optimization_barrier((partials, tokens, last_rows))
            query_rows = tokens[: CHIPS - 1] + [last_rows] + tokens[CHIPS:-1] + [swapped(last_rows, 1)]
            results = meanwhile(query_rows)
        for partial, place in zip(partials, round_):
            if place:
                partial = swapped(partial, 2 * place)
            pieces = partial.reshape(2, CHIPS, rows, pair).astype(F32)
            pieces = jnp.stack([pieces[:, j ^ place] for j in range(CHIPS)], axis=1)
            total = pieces if total is None else total + pieces
    key_values = total.astype(BF16).reshape(2 * CHIPS * rows, pair)
    sources = jnp.stack(
        [tile * KVH + (chip ^ j) * 2 + (core ^ e) for e in range(2) for j in range(CHIPS)]
    )
    key_pos = (sources[:, None] * rows + jnp.arange(rows, dtype=jnp.int32)[None, :]).reshape(-1)
    return key_values, key_pos, results


def gather_rows(own):
    ours = [own] + [swapped(own, 2 * place) for place in range(1, CHIPS)]
    theirs = swapped(jnp.stack(ours), 1)
    return ours + [theirs]


def scatter_rows(kept, sent):
    both = kept + swapped(sent, 1).astype(F32)
    total = both[0]
    for place in range(1, CHIPS):
        total = total + swapped(both[place].astype(BF16), 2 * place).astype(F32)
    return total


def reduce_rows(kept, sent):
    both = (kept + swapped(sent, 1).astype(F32)).astype(BF16)
    halves = jnp.split(both, 2, axis=1)
    for masks in ((2, 4), (4, 2)):
        halves = [
            (half.astype(F32) + swapped(half, mask).astype(F32)).astype(BF16)
            for half, mask in zip(halves, masks)
        ]
    return jnp.concatenate(halves, axis=1)


def attend_rows(queries, query_pos, query_floor, key_values, key_pos):
    row_count = queries.shape[0]
    head_count = queries.shape[1] // HD
    key_part = key_values[:, :HD]
    value_part = key_values[:, HD:]
    grouped = queries.reshape(row_count, head_count, HD)
    scores = jnp.einsum("rhd,kd->rhk", grouped, key_part, preferred_element_type=F32) * HD ** (-0.5)
    capped = CAP * jnp.tanh(scores / CAP)
    visible = (key_pos[None, :] <= query_pos[:, None]) & (key_pos[None, :] >= query_floor[:, None])
    weights = jnp.where(visible[:, None, :], jnp.exp(capped), 0.0)
    totals = jnp.sum(weights, axis=2)
    weighted = jnp.einsum(
        "rhk,kd->rhd", weights.astype(BF16), value_part, preferred_element_type=F32
    )
    return weighted.reshape(row_count, head_count * HD), totals


def on_device(
    hidden, kv_gain, kv_weight, query_states, query_gain, query_weight, output_weight, block_bounds
):
    tile_count = lax.axis_size("row") // KVH
    tile = lax.axis_index("row") // KVH
    depth = hidden.shape[1]
    slice_depth = query_weight.shape[2]
    query_count = query_states.shape[1]
    row_number = jnp.arange(query_count, dtype=jnp.int32)
    query_pos = jnp.repeat(block_bounds[:, 1], QBLK) + row_number % QBLK
    query_floor = jnp.repeat(block_bounds[:, 0], QBLK)

    me = lax.axis_index("row")
    chip, core = me // 2 % CHIPS, me % 2
    part = lax.axis_index("groups") if lax.axis_size("groups") == 2 else 0
    place_now = jnp.stack([chip, core, tile, part]).astype(jnp.int32)
    unit, rows = query_states.shape[0], hidden.shape[0]
    kernels = in_kernels(unit, rows)
    width = query_weight.shape[3]
    own_rows = query_states
    small = jax.ShapeDtypeStruct((16, query_count), BF16)
    spread = jax.ShapeDtypeStruct((query_count, query_count), F32)
    wide = [jax.ShapeDtypeStruct((query_count, width), kind) for kind in (BF16, F32)]
    flops = 2 * query_count * slice_depth * width
    halved = jax.ShapeDtypeStruct((query_count // 2, slice_depth), BF16)

    def query_parts(section, pieces):
        gain = lax.dynamic_slice_in_dim(query_gain[section], tile * slice_depth, slice_depth)
        if not kernels:
            pieces = [
                part
                for piece in pieces
                for part in (piece if piece.ndim == 3 else [piece[-(own_rows.size // piece.shape[1]) :]])
            ]
            pieces = [piece.reshape(own_rows.shape) for piece in pieces]
            ours, theirs = (
                jnp.stack(natural(half, chip)) for half in (pieces[:CHIPS], pieces[CHIPS:])
            )
            stream = in_order(ours, theirs, core).astype(F32)
            scaled = (stream * gain[:, None]).astype(BF16)
            partial = lax.dot_general(
                scaled, query_weight[section, 0], (((0,), (0,)), ((), ())), preferred_element_type=F32
            )
            squares = jnp.sum(stream * stream, axis=0)
            return partial.astype(BF16), partial, squares.astype(BF16), squares
        return call(
            functools.partial(query_kernel, query_count),
            "query",
            wide + [small, spread, halved],
            [place_now],
            [gain[None, :], query_weight[section, 0]],
            [
                pltpu.VMEM((slice_depth, query_count), BF16),
                pltpu.VMEM((query_count, slice_depth), F32),
                pltpu.VMEM((KVH, own_rows.size // (2 * unit * tile_count), 2 * unit * tile_count), BF16),
                pltpu.SemaphoreType.DMA((KVH,)),
            ],
            flops,
            pieces,
        )

    key_values, key_pos, parts = key_values_of(
        hidden, kv_gain, kv_weight, query_states, place_now, functools.partial(query_parts, 0)
    )
    positions = [query_pos[:, None], query_floor[:, None], key_pos[None, :]]
    if kernels:
        stream, parts = parts[4], parts[:4]
    sections = query_gain.shape[0]
    for section in range(sections):
        if section and not kernels:
            parts = query_parts(section, gather_rows(own_rows))
        sent, partial, squares_sent, squares = parts
        if kernels:
            far = zip(over_tiles(sent, tile_count)[1:], over_tiles(squares_sent, tile_count)[1:])
            sent, weighted, totals_sent, totals = call(
                functools.partial(attend_kernel, depth, tile_count - 1),
                "attend",
                wide + [small, spread],
                [],
                positions + [key_values, partial, squares] + [value for pair in far for value in pair],
                (),
                flops // 2,
            )
            far = zip(over_tiles(sent, tile_count)[1:], over_tiles(totals_sent, tile_count)[1:])
            arrays = [output_weight[section, 0], weighted, totals]
            arrays += [value for pair in far for value in pair]
            if section + 1 < sections:
                kept, sent = call(
                    functools.partial(update_rows_kernel, tile_count - 1),
                    "update",
                    [jax.ShapeDtypeStruct(halved.shape, F32), halved],
                    [place_now],
                    arrays,
                    [pltpu.VMEM((query_count, slice_depth), F32)],
                    flops,
                )
                stream = (stream.astype(F32) + reduce_rows(kept, sent).astype(F32)).astype(BF16)
                theirs = swapped(stream, 1)
                gain = lax.dynamic_slice_in_dim(
                    query_gain[section + 1], tile * slice_depth, slice_depth
                )
                parts = call(
                    later_query_kernel,
                    "query",
                    wide + [small, spread],
                    [place_now],
                    [gain[None, :], query_weight[section + 1, 0], stream, theirs],
                    [pltpu.VMEM((query_count, slice_depth), BF16)],
                    flops,
                )
                own_rows = call(
                    own_rows_kernel,
                    "own_rows",
                    [jax.ShapeDtypeStruct(own_rows.shape, BF16)],
                    [place_now],
                    [stream, theirs],
                    [
                        pltpu.VMEM((query_count, slice_depth), BF16),
                        pltpu.VMEM((2 * unit, query_count), F32),
                    ],
                )[0]
                continue
            shape = (CHIPS, unit, query_count)
            kept, sent = call(
                functools.partial(update_kernel, tile_count - 1),
                "update",
                [jax.ShapeDtypeStruct(shape, F32), jax.ShapeDtypeStruct(shape, BF16)],
                [place_now],
                arrays,
                (),
                flops,
            )
        else:
            square_sum = sum(over_tiles(squares_sent, tile_count)[1:], squares)
            query_sum = sum(over_tiles(sent, tile_count)[1:], partial)
            inverse = lax.rsqrt(square_sum / depth + EPSILON)
            queries = (query_sum * inverse[:, None]).astype(BF16)
            weighted, totals = attend_rows(queries, query_pos, query_floor, key_values, key_pos)
            total_sum = sum(over_tiles(totals.astype(BF16), tile_count)[1:], totals)
            weighted_sum = sum(over_tiles(weighted.astype(BF16), tile_count)[1:], weighted)
            attended = (
                (weighted_sum.reshape(query_count, QPK, HD) / total_sum[:, :, None])
                .reshape(query_count, QPK * HD)
                .astype(BF16)
            )
            update = lax.dot_general(
                output_weight[section, 0],
                attended,
                (((1,), (1,)), ((), ())),
                preferred_element_type=F32,
            )
            split = update.reshape(CHIPS, 2, unit, query_count)
            kept = jnp.where(core == 0, split[:, 0], split[:, 1])
            sent = jnp.where(core == 0, split[:, 1], split[:, 0]).astype(BF16)
            kept, sent = (jnp.stack(natural(value, chip)) for value in (kept, sent))
        own_rows = (own_rows.astype(F32) + scatter_rows(kept, sent)).astype(BF16)
    return own_rows


def solution(mesh):
    in_specs = (
        P(("groups", "row"), None),
        P(),
        P("row", None),
        P("row", "groups"),
        P(),
        P(None, "row", None, None),
        P(None, "row", None, None),
        P("groups", None),
    )
    return jax.shard_map(
        on_device, mesh=mesh, in_specs=in_specs, out_specs=P("row", "groups"), check_vma=False
    )
```

```python
import functools

import jax
import jax.numpy as jnp
from jax import lax
from jax.experimental import pallas as pl
from jax.experimental.pallas import tpu as pltpu
from jax.sharding import PartitionSpec as P

KVH = 8
HD = 128
QPK = 5
QBLK = 64
CAP = 30.0
EPSILON = 1e-05
LOG2_E = 1.4426950408889634
BF16 = jnp.bfloat16
F32 = jnp.float32

CHIPS = KVH // 2
ROUNDS = ((2, 1), (3, 0))
PROJECT_COST = 8
BAND = 32
HEADS_AT_ONCE = (2, 2)


def swapped(value, mask, axis="row"):
    pairs = [(source, source ^ mask) for source in range(lax.axis_size(axis))]
    return lax.ppermute(value, axis, pairs)


def over_tiles(value, tile_count):
    values = [value]
    mask = 1
    while mask < tile_count:
        if len(values) == 1:
            values.append(swapped(values[0], mask * KVH))
        else:
            got = swapped(jnp.stack(values), mask * KVH)
            values.extend(got[place] for place in range(len(values)))
        mask *= 2
    return values


def natural(pieces, index):
    pieces = list(pieces)
    bit = 1
    while bit < len(pieces):
        upper = index // bit % 2 == 1
        pieces = [jnp.where(upper, pieces[j ^ bit], pieces[j]) for j in range(len(pieces))]
        bit *= 2
    return pieces


def here():
    me = lax.axis_index("row")
    part = lax.axis_index("groups") if lax.axis_size("groups") == 2 else 0
    return [me // 2 % CHIPS, me % 2, me // KVH, part]


def prepare_kernel(
    pair, heads, blocks, width, weight_any, hidden_any, gain_any, extra_any, *refs
):
    weight_ref, hidden_ref, gain_ref, extra_ref, normed, sems = refs[-6:]
    results = len(heads) + len(blocks)
    targets, refs = refs[:results], refs[results:-6]
    place_now = here()
    rows = hidden_ref.shape[0]
    lanes = extra_ref.shape[1]
    bands = [slice(band, band + BAND) for band in range(0, rows, BAND)]
    pairs = [(weight_any, weight_ref), (gain_any, gain_ref), (extra_any, extra_ref)]
    pairs += [(hidden_any.at[band], hidden_ref.at[band]) for band in bands]
    copies = [
        pltpu.make_async_copy(source, target, sems.at[number])
        for number, (source, target) in enumerate(pairs)
    ]
    outs = [
        pltpu.make_async_copy(source, target, sems.at[len(copies) + number])
        for number, (source, target) in enumerate(zip(refs, targets))
    ]
    for copy in copies:
        copy.start()
    copies[0].wait()
    for head_ref, group, out in zip(refs, heads, outs):
        for number, head in enumerate(group):
            column = pl.multiple_of(head(*place_now) * pair, pair)
            head_ref[number] = weight_ref[:, pl.ds(column, pair)]
        out.start()
    copies[1].wait()
    copies[2].wait()
    for band, copy in zip(bands, copies[3:]):
        copy.wait()
        hidden = hidden_ref[band, :].astype(F32)
        inverse = lax.rsqrt(jnp.mean(hidden * hidden, axis=1, keepdims=True) + EPSILON)
        normed[band, :] = (hidden * inverse * gain_ref[...]).astype(BF16)
    for out_ref, group, out in zip(refs[len(heads) :], blocks, outs[len(heads) :]):
        for number, block in enumerate(group):
            start = pl.multiple_of(block(*place_now) * width, 128)
            out_ref[:rows, number * width : (number + 1) * width] = normed[:, pl.ds(start, width)]
        more = out_ref.shape[0] - rows
        for block in range(out_ref.shape[1] // lanes if more else 0):
            out_ref[rows:, block * lanes : (block + 1) * lanes] = extra_ref[
                block * more : (block + 1) * more, :
            ]
        out.start()
    for out in outs:
        out.wait()


def in_kernels(unit, rows):
    return unit % 64 == 0 and rows % BAND == 0


def prepared(weight, head_groups, pair, hidden, gain, groups, width, extra, place_now, kernels):
    rows, depth = hidden.shape
    total_width = len(groups[0]) * width
    more = extra.size // total_width
    if not kernels:
        now = [place_now[number] for number in range(4)]
        columns = [
            jnp.stack(
                [lax.dynamic_slice_in_dim(weight, head(*now) * pair, pair, 1) for head in group]
            )
            for group in head_groups
        ]
        hidden_float = hidden.astype(F32)
        inverse = lax.rsqrt(jnp.mean(hidden_float * hidden_float, axis=1, keepdims=True) + EPSILON)
        normed = (hidden_float * inverse * gain[None, :]).astype(BF16)
        results = []
        for group in groups:
            blocks = [
                lax.dynamic_slice_in_dim(normed, block(*now) * width, width, 1) for block in group
            ]
            rest = extra.reshape(more, total_width)
            results.append(jnp.concatenate([jnp.concatenate(blocks, axis=1), rest], axis=0))
        results[-1] = results[-1][:rows]
        return columns, results
    counts = [len(group) for group in head_groups]
    shapes = [(count, weight.shape[0], pair) for count in counts]
    shapes += [(rows + more, total_width)] * (len(groups) - 1) + [(rows, total_width)]
    results = pl.pallas_call(
        functools.partial(prepare_kernel, pair, head_groups, groups, width),
        out_shape=[jax.ShapeDtypeStruct(shape, BF16) for shape in shapes],
        in_specs=[pl.BlockSpec(memory_space=pltpu.HBM)] * 4,
        out_specs=[pl.BlockSpec(memory_space=pl.ANY)] * len(shapes),
        scratch_shapes=[pltpu.VMEM(shape, BF16) for shape in shapes]
        + [
            pltpu.VMEM(weight.shape, BF16),
            pltpu.VMEM((rows, depth), BF16),
            pltpu.VMEM((1, depth), F32),
            pltpu.VMEM(extra.shape, BF16),
            pltpu.VMEM((rows, depth), BF16),
            pltpu.SemaphoreType.DMA((3 + rows // BAND + len(shapes),)),
        ],
        compiler_params=pltpu.CompilerParams(vmem_limit_bytes=60 * 1024 * 1024),
        name="prepare",
    )(weight, hidden, gain[None, :], extra)
    return results[: len(counts)], results[len(counts) :]


def stage_kernel(pair, groups, place_ref, weight_ref, tokens_ref, *refs):
    place_now = [place_ref[number] for number in range(4)]
    for out_ref, heads in zip(refs, groups):
        for number, head in enumerate(heads):
            column = pl.multiple_of(head(*place_now) * pair, pair)
            out_ref[number] = weight_ref[:, pl.ds(column, pair)]
    refs[-1][...] = tokens_ref[...]


def staged(weight, groups, pair, tokens, place_now, kernels):
    if not kernels:
        now = [place_now[number] for number in range(4)]
        return [
            jnp.stack(
                [lax.dynamic_slice_in_dim(weight, head(*now) * pair, pair, 1) for head in heads]
            )
            for heads in groups
        ] + [tokens]
    shapes = [
        jax.ShapeDtypeStruct((len(heads), weight.shape[0], pair), BF16) for heads in groups
    ] + [jax.ShapeDtypeStruct(tokens.shape, BF16)]
    return call(
        functools.partial(stage_kernel, pair, groups),
        "stage",
        shapes,
        [place_now],
        [weight, tokens],
    )


def project_kernel(rows, heads, start, place, first_ref, kept_ref, traded_ref, *refs):
    token_refs, refs = refs[: 2 * CHIPS], refs[2 * CHIPS :]
    weight = refs[-1]
    out_refs = refs[-1 - heads : -1]
    blocks = refs[: -1 - heads]
    unit, pair = kept_ref.shape[1:]

    def put(head, tile, second, value):
        which = 1 - first_ref[tile] if second else first_ref[tile]
        base = pl.multiple_of(2 * unit * tile + which * unit, unit)
        weight[pl.ds(base, unit), head * pair : (head + 1) * pair] = value

    for head in range(heads):
        put(head, 0, 0, kept_ref[start + head])
        put(head, 0, 1, traded_ref[start + head])
        for number, block_ref in enumerate(blocks):
            put(head, 1 + number // 2, number % 2, block_ref[place + head])
    for number, token_ref in enumerate(token_refs):
        span = slice(number * rows, (number + 1) * rows)
        result = jnp.dot(token_ref[:rows, :], weight[...], preferred_element_type=F32).astype(BF16)
        for head, out_ref in enumerate(out_refs):
            out_ref[span, :] = result[:, head * pair : (head + 1) * pair]


def projected(tokens, heads, kept, traded, start, place, firsts, blocks, rows, kernels):
    unit, pair = kept.shape[1:]
    depth = tokens[0].shape[1]
    count = len(tokens) * rows
    firsts = jnp.stack(firsts).astype(jnp.int32)
    if not kernels:
        pieces = [kept[start : start + heads], traded[start : start + heads]]
        pieces += [block[place : place + heads] for block in blocks]
        ordered = []
        for tile in range(len(pieces) // 2):
            one, two = pieces[2 * tile : 2 * tile + 2]
            first = firsts[tile] == 0
            ordered += [jnp.where(first, one, two), jnp.where(first, two, one)]
        weight = jnp.concatenate(ordered, axis=1)
        tokens = jnp.concatenate([piece[:rows] for piece in tokens])
        result = jnp.einsum("td,hdc->htc", tokens, weight, preferred_element_type=F32)
        return list(result.astype(BF16))
    vmem = pl.BlockSpec(memory_space=pltpu.VMEM)
    smem = pl.BlockSpec(memory_space=pltpu.SMEM)
    return list(
        pl.pallas_call(
            functools.partial(project_kernel, rows, heads, start, place),
            out_shape=[jax.ShapeDtypeStruct((count, pair), BF16)] * heads,
            in_specs=[smem] + [vmem] * (2 + len(tokens) + len(blocks)),
            out_specs=[vmem] * heads,
            scratch_shapes=[pltpu.VMEM((depth, heads * pair), BF16)],
            compiler_params=pltpu.CompilerParams(vmem_limit_bytes=20 * 1024 * 1024),
            cost_estimate=pl.CostEstimate(
                flops=PROJECT_COST * 2 * heads * count * depth * pair,
                bytes_accessed=2 * count * depth,
                transcendentals=0,
            ),
            name="project",
        )(firsts, kept, traded, *tokens, *blocks)
    )


def query_kernel(lanes, gain_ref, weight_ref, *refs):
    place_ref = here()
    piece_refs, refs = refs[:-9], refs[-9:]
    results, own_ref, (stream, turned, parts, sems) = refs[:4], refs[4], refs[5:]
    unit = stream.shape[0] // KVH
    more = parts.shape[1]
    blocks = parts.shape[2] // lanes
    sources = [
        piece_ref.at[place] if len(piece_ref.shape) == 3 else piece_ref
        for piece_ref in piece_refs
        for place in range(CHIPS if len(piece_ref.shape) == 3 else 1)
    ]
    bases = [
        pl.multiple_of(
            ((place_ref[0] ^ number % CHIPS) * 2 + (place_ref[1] ^ number // CHIPS)) * unit, unit
        )
        for number in range(KVH)
    ]
    packed = sources[0].shape[1] != lanes
    copies = []
    for number, source in enumerate(sources):
        if packed:
            source, target = source.at[source.shape[0] - more :], parts.at[number]
        else:
            target = stream.at[pl.ds(bases[number], unit)]
        copies.append(pltpu.make_async_copy(source, target, sems.at[number]))
        copies[-1].start()
    for number, copy in enumerate(copies):
        copy.wait()
        for block in range(blocks if packed else 0):
            stream[pl.ds(pl.multiple_of(bases[number] + block * more, more), more), :] = parts[
                number, :, block * lanes : (block + 1) * lanes
            ]
    turned[...] = stream[...].astype(F32).T
    query_step(turned[...], gain_ref, weight_ref, *results)
    half = own_ref.shape[0]
    own_ref[...] = turned[pl.ds(pl.multiple_of(place_ref[1] * half, half), half), :].astype(BF16)


def query_step(rows, gain_ref, weight_ref, sent_ref, kept_ref, squares_sent_ref, squares_ref):
    squares = jnp.sum(rows * rows, axis=1, keepdims=True)
    scaled = (rows * gain_ref[...]).astype(BF16)
    partial = jnp.dot(scaled, weight_ref[...], preferred_element_type=F32)
    kept_ref[...] = partial
    sent_ref[...] = partial.astype(BF16)
    spread = jnp.broadcast_to(squares, squares_ref.shape)
    squares_ref[...] = spread
    across = spread.T[:8]
    squares_sent_ref[...] = parted(across)


def both_cores(place_ref, ours_ref, theirs_ref, rows):
    half = ours_ref.shape[0]
    for which, ref in ((place_ref[1], ours_ref), (1 - place_ref[1], theirs_ref)):
        rows[pl.ds(pl.multiple_of(which * half, half), half), :] = ref[...]


def later_query_kernel(gain_ref, weight_ref, ours_ref, theirs_ref, *refs):
    results, rows = refs[:-1], refs[-1]
    both_cores(here(), ours_ref, theirs_ref, rows)
    query_step(rows[...].astype(F32), gain_ref, weight_ref, *results)


def own_rows_kernel(ours_ref, theirs_ref, out_ref, rows, turned):
    place_ref = here()
    both_cores(place_ref, ours_ref, theirs_ref, rows)
    unit = out_ref.shape[0]
    column = pl.multiple_of(place_ref[0] * 2 * unit, 2 * unit)
    turned[...] = rows[:, pl.ds(column, 2 * unit)].astype(F32).T
    out_ref[...] = turned[pl.ds(pl.multiple_of(place_ref[1] * unit, unit), unit), :].astype(BF16)


def parted(across):
    high = across.astype(BF16).astype(F32)
    return jnp.concatenate([high, across - high], axis=0).astype(BF16)


def spread_back(pair_ref, lanes):
    pair = pair_ref[...].astype(F32)
    across = pair[:8] + pair[8:]
    return jnp.concatenate([across, jnp.zeros((lanes - 8, lanes), F32)], axis=0).T


def attend_kernel(depth, others, query_pos_ref, query_floor_ref, key_pos_ref, kv_ref, *refs):
    kept_ref, squares_ref = refs[:2]
    far = refs[2 : 2 + 2 * others]
    sent_ref, out_ref, totals_sent_ref, totals_ref = refs[2 + 2 * others :]
    lanes = kept_ref.shape[0]
    queries = kept_ref[...]
    squares = squares_ref[:, :1]
    for other in range(others):
        queries = queries + far[2 * other][...].astype(F32)
        squares = squares + spread_back(far[2 * other + 1], lanes)[:, :1]
    queries = (queries * lax.rsqrt(squares / depth + EPSILON)).astype(BF16)
    visible = (key_pos_ref[...] <= query_pos_ref[...]) & (key_pos_ref[...] >= query_floor_ref[...])
    keys, values = kv_ref[:, :HD], kv_ref[:, HD:]
    lane = lax.broadcasted_iota(jnp.int32, (lanes, lanes), 1)
    totals = jnp.zeros((lanes, lanes), F32)
    heads = queries.shape[1] // HD
    stacked = jnp.concatenate([queries[:, h * HD : (h + 1) * HD] for h in range(heads)], axis=0)
    scores = lax.dot_general(
        stacked, keys, (((1,), (1,)), ((), ())), preferred_element_type=F32
    )
    capped = jnp.tanh(scores * (HD ** (-0.5) / CAP))
    weights = jnp.exp2(capped * (CAP * LOG2_E)).reshape(heads, lanes, -1)
    weights = jnp.where(visible[None], weights, 0.0)
    sums = jnp.sum(weights, axis=2, keepdims=True)
    weighted = jnp.dot(
        weights.astype(BF16).reshape(heads * lanes, -1), values, preferred_element_type=F32
    )
    for head in range(heads):
        span = slice(head * HD, (head + 1) * HD)
        totals = jnp.where(lane == head, sums[head], totals)
        part = weighted[head * lanes : (head + 1) * lanes]
        out_ref[:, span] = part
        sent_ref[:, span] = part.astype(BF16)
    totals_ref[...] = totals
    totals_sent_ref[...] = parted(totals.T[:8])


def attended_of(others, kept_ref, totals_ref, far):
    lanes = kept_ref.shape[0]
    weighted = kept_ref[...]
    totals = totals_ref[...]
    for other in range(others):
        weighted = weighted + far[2 * other][...].astype(F32)
        totals = totals + spread_back(far[2 * other + 1], lanes)
    return jnp.concatenate(
        [
            (weighted[:, head * HD : (head + 1) * HD] / totals[:, head : head + 1]).astype(BF16)
            for head in range(weighted.shape[1] // HD)
        ],
        axis=1,
    )


def update_rows_kernel(others, weight_ref, kept_ref, totals_ref, *refs):
    place_ref = here()
    far, (own_ref, sent_ref, update) = refs[: 2 * others], refs[2 * others :]
    attended = attended_of(others, kept_ref, totals_ref, far)
    update[...] = lax.dot_general(
        attended, weight_ref[...], (((1,), (1,)), ((), ())), preferred_element_type=F32
    )
    half = own_ref.shape[0]
    for which, out_ref in ((place_ref[1], own_ref), (1 - place_ref[1], sent_ref)):
        rows = update[pl.ds(pl.multiple_of(which * half, half), half), :]
        out_ref[...] = rows.astype(out_ref.dtype)


def update_kernel(others, weight_ref, kept_ref, totals_ref, *refs):
    place_ref = here()
    far, (own_ref, sent_ref) = refs[: 2 * others], refs[2 * others :]
    unit = own_ref.shape[1]
    attended = attended_of(others, kept_ref, totals_ref, far)
    for core, out_ref in enumerate((own_ref, sent_ref)):
        for chip in range(CHIPS):
            base = ((place_ref[0] ^ chip) * 2 + (place_ref[1] ^ core)) * unit
            update = lax.dot_general(
                weight_ref[pl.ds(pl.multiple_of(base, unit), unit), :],
                attended,
                (((1,), (1,)), ((), ())),
                preferred_element_type=F32,
            )
            out_ref[chip] = update.astype(out_ref.dtype)


def call(kernel, name, out_shape, scalars, arrays, scratch=(), flops=0, loose=()):
    vmem = pl.BlockSpec(memory_space=pltpu.VMEM)
    smem = pl.BlockSpec(memory_space=pltpu.SMEM)
    return pl.pallas_call(
        kernel,
        out_shape=out_shape,
        in_specs=[smem] * len(scalars)
        + [vmem] * len(arrays)
        + [pl.BlockSpec(memory_space=pl.ANY)] * len(loose),
        out_specs=[vmem] * len(out_shape),
        scratch_shapes=list(scratch),
        compiler_params=pltpu.CompilerParams(vmem_limit_bytes=20 * 1024 * 1024),
        cost_estimate=pl.CostEstimate(
            flops=flops, bytes_accessed=sum(2 * a.size for a in arrays), transcendentals=0
        ),
        name=name,
    )(*scalars, *arrays, *loose)


def in_order(ours, theirs, core):
    low, high = jnp.where(core == 0, ours, theirs), jnp.where(core == 0, theirs, ours)
    return jnp.stack([low, high], axis=1).reshape(-1, ours.shape[-1])


def key_values_of(hidden, kv_gain, kv_weight, query_states, place_now, meanwhile):
    lane_count = lax.axis_size("row")
    tile_count = lane_count // KVH
    me = lax.axis_index("row")
    tile, chip, core = me // KVH, me // 2 % CHIPS, me % 2
    rows = hidden.shape[0]
    unit = kv_weight.shape[0]
    pair = 2 * HD
    share = lax.axis_size("groups") == 2
    part = lax.axis_index("groups") if share else 0

    order = [place for round_ in ROUNDS for place in round_]

    def kept_head(place):
        return lambda chip, core, tile, part: (chip ^ place) * 2 + core

    def sent_head(place):
        return lambda chip, core, tile, part: ((chip ^ place) * 2 + core) ^ part

    def other_head(place):
        return lambda chip, core, tile, part: (chip ^ place) * 2 + 1 - core

    def block(place, j):
        return lambda chip, core, tile, part: (tile ^ j) * CHIPS + (chip ^ place)

    kernels = in_kernels(unit, rows)
    width = 2 * unit
    sent, features = prepared(
        kv_weight,
        [[sent_head(place) for place in round_] for round_ in ROUNDS],
        pair,
        hidden,
        kv_gain,
        [[block(place, j) for j in range(tile_count)] for place in range(CHIPS)],
        width,
        query_states,
        place_now,
        kernels,
    )
    def to_tile(value, j, flip):
        if not share:
            return swapped(value, j * KVH)
        pairs = [
            (g * lane_count + d, g * lane_count + (d ^ (j * KVH) ^ (g if flip else 0)))
            for g in range(2)
            for d in range(lane_count)
        ]
        return lax.ppermute(value, ("groups", "row"), pairs)

    far = [[to_tile(value, j, True) for j in range(1, tile_count)] for value in sent]
    held = [features[0]] + [swapped(features[p], 2 * p) for p in range(1, CHIPS)]

    kv_weight, own, _ = lax.optimization_barrier((kv_weight, held[0], far[0]))
    kept, traded, own = staged(
        kv_weight,
        [[kept_head(place) for place in order], [other_head(place) for place in order]],
        pair,
        own,
        place_now,
        kernels,
    )
    traded = swapped(traded, 1)
    held[1], kept, own = lax.optimization_barrier((held[1], kept, own))

    def shared(number):
        start = sum(len(round_) for round_ in ROUNDS[:number])
        return [
            swapped(value, 1, "groups")
            if share
            else to_tile(traded[start : start + len(ROUNDS[number])], j, False)
            for j, value in enumerate(far[number], 1)
        ]

    firsts = [core] + [core ^ part] * (tile_count - 1)
    halves = [shared(number) for number in range(len(ROUNDS))]
    held[2], held[3], halves[0], far = lax.optimization_barrier((held[2], held[3], halves[0], far))
    tokens = held + [swapped(piece, 1) for piece in held]
    tokens[0] = own
    last_rows = swapped(held[2][rows:], 2)
    total = None
    done = 0
    for number, round_ in enumerate(ROUNDS):
        blocks = [piece for pair_ in zip(far[number], halves[number]) for piece in pair_]
        partials = []
        for inner in range(0, len(round_), HEADS_AT_ONCE[number]):
            partials += projected(
                tokens,
                HEADS_AT_ONCE[number],
                kept,
                traded,
                done + inner,
                inner,
                firsts,
                blocks,
                rows,
                kernels,
            )
        done += len(round_)
        if number == 0:
            partials, tokens, last_rows = lax.optimization_barrier((partials, tokens, last_rows))
            query_rows = tokens[: CHIPS - 1] + [last_rows] + tokens[CHIPS:-1] + [swapped(last_rows, 1)]
            results = meanwhile(query_rows)
        for partial, place in zip(partials, round_):
            if place:
                partial = swapped(partial, 2 * place)
            pieces = partial.reshape(2, CHIPS, rows, pair).astype(F32)
            pieces = jnp.stack([pieces[:, j ^ place] for j in range(CHIPS)], axis=1)
            total = pieces if total is None else total + pieces
    key_values = total.astype(BF16).reshape(2 * CHIPS * rows, pair)
    sources = jnp.stack(
        [tile * KVH + (chip ^ j) * 2 + (core ^ e) for e in range(2) for j in range(CHIPS)]
    )
    key_pos = (sources[:, None] * rows + jnp.arange(rows, dtype=jnp.int32)[None, :]).reshape(-1)
    return key_values, key_pos, results


def gather_rows(own):
    ours = [own] + [swapped(own, 2 * place) for place in range(1, CHIPS)]
    theirs = swapped(jnp.stack(ours), 1)
    return ours + [theirs]


def scatter_rows(kept, sent):
    both = kept + swapped(sent, 1).astype(F32)
    total = both[0]
    for place in range(1, CHIPS):
        total = total + swapped(both[place].astype(BF16), 2 * place).astype(F32)
    return total


def reduce_rows(kept, sent):
    both = (kept + swapped(sent, 1).astype(F32)).astype(BF16)
    halves = jnp.split(both, 2, axis=1)
    for masks in ((2, 4), (4, 2)):
        halves = [
            (half.astype(F32) + swapped(half, mask).astype(F32)).astype(BF16)
            for half, mask in zip(halves, masks)
        ]
    return jnp.concatenate(halves, axis=1)


def attend_rows(queries, query_pos, query_floor, key_values, key_pos):
    row_count = queries.shape[0]
    head_count = queries.shape[1] // HD
    key_part = key_values[:, :HD]
    value_part = key_values[:, HD:]
    grouped = queries.reshape(row_count, head_count, HD)
    scores = jnp.einsum("rhd,kd->rhk", grouped, key_part, preferred_element_type=F32) * HD ** (-0.5)
    capped = CAP * jnp.tanh(scores / CAP)
    visible = (key_pos[None, :] <= query_pos[:, None]) & (key_pos[None, :] >= query_floor[:, None])
    weights = jnp.where(visible[:, None, :], jnp.exp(capped), 0.0)
    totals = jnp.sum(weights, axis=2)
    weighted = jnp.einsum(
        "rhk,kd->rhd", weights.astype(BF16), value_part, preferred_element_type=F32
    )
    return weighted.reshape(row_count, head_count * HD), totals


def on_device(
    hidden, kv_gain, kv_weight, query_states, query_gain, query_weight, output_weight, block_bounds
):
    tile_count = lax.axis_size("row") // KVH
    tile = lax.axis_index("row") // KVH
    depth = hidden.shape[1]
    slice_depth = query_weight.shape[2]
    query_count = query_states.shape[1]
    row_number = jnp.arange(query_count, dtype=jnp.int32)
    query_pos = jnp.repeat(block_bounds[:, 1], QBLK) + row_number % QBLK
    query_floor = jnp.repeat(block_bounds[:, 0], QBLK)

    me = lax.axis_index("row")
    chip, core = me // 2 % CHIPS, me % 2
    part = lax.axis_index("groups") if lax.axis_size("groups") == 2 else 0
    place_now = jnp.stack([chip, core, tile, part]).astype(jnp.int32)
    unit, rows = query_states.shape[0], hidden.shape[0]
    kernels = in_kernels(unit, rows)
    width = query_weight.shape[3]
    own_rows = query_states
    small = jax.ShapeDtypeStruct((16, query_count), BF16)
    spread = jax.ShapeDtypeStruct((query_count, query_count), F32)
    wide = [jax.ShapeDtypeStruct((query_count, width), kind) for kind in (BF16, F32)]
    flops = 2 * query_count * slice_depth * width
    halved = jax.ShapeDtypeStruct((query_count // 2, slice_depth), BF16)

    def query_parts(section, pieces):
        gain = lax.dynamic_slice_in_dim(query_gain[section], tile * slice_depth, slice_depth)
        if not kernels:
            pieces = [
                part
                for piece in pieces
                for part in (piece if piece.ndim == 3 else [piece[-(own_rows.size // piece.shape[1]) :]])
            ]
            pieces = [piece.reshape(own_rows.shape) for piece in pieces]
            ours, theirs = (
                jnp.stack(natural(half, chip)) for half in (pieces[:CHIPS], pieces[CHIPS:])
            )
            stream = in_order(ours, theirs, core).astype(F32)
            scaled = (stream * gain[:, None]).astype(BF16)
            partial = lax.dot_general(
                scaled, query_weight[section, 0], (((0,), (0,)), ((), ())), preferred_element_type=F32
            )
            squares = jnp.sum(stream * stream, axis=0)
            return partial.astype(BF16), partial, squares.astype(BF16), squares
        return call(
            functools.partial(query_kernel, query_count),
            "query",
            wide + [small, spread, halved],
            [],
            [gain[None, :], query_weight[section, 0]],
            [
                pltpu.VMEM((slice_depth, query_count), BF16),
                pltpu.VMEM((query_count, slice_depth), F32),
                pltpu.VMEM((KVH, own_rows.size // (2 * unit * tile_count), 2 * unit * tile_count), BF16),
                pltpu.SemaphoreType.DMA((KVH,)),
            ],
            flops,
            pieces,
        )

    key_values, key_pos, parts = key_values_of(
        hidden, kv_gain, kv_weight, query_states, place_now, functools.partial(query_parts, 0)
    )
    positions = [query_pos[:, None], query_floor[:, None], key_pos[None, :]]
    if kernels:
        stream, parts = parts[4], parts[:4]
    sections = query_gain.shape[0]
    for section in range(sections):
        if section and not kernels:
            parts = query_parts(section, gather_rows(own_rows))
        sent, partial, squares_sent, squares = parts
        if kernels:
            far = zip(over_tiles(sent, tile_count)[1:], over_tiles(squares_sent, tile_count)[1:])
            sent, weighted, totals_sent, totals = call(
                functools.partial(attend_kernel, depth, tile_count - 1),
                "attend",
                wide + [small, spread],
                [],
                positions + [key_values, partial, squares] + [value for pair in far for value in pair],
                (),
                flops // 2,
            )
            far = zip(over_tiles(sent, tile_count)[1:], over_tiles(totals_sent, tile_count)[1:])
            arrays = [output_weight[section, 0], weighted, totals]
            arrays += [value for pair in far for value in pair]
            if section + 1 < sections:
                kept, sent = call(
                    functools.partial(update_rows_kernel, tile_count - 1),
                    "update",
                    [jax.ShapeDtypeStruct(halved.shape, F32), halved],
                    [],
                    arrays,
                    [pltpu.VMEM((query_count, slice_depth), F32)],
                    flops,
                )
                stream = (stream.astype(F32) + reduce_rows(kept, sent).astype(F32)).astype(BF16)
                theirs = swapped(stream, 1)
                gain = lax.dynamic_slice_in_dim(
                    query_gain[section + 1], tile * slice_depth, slice_depth
                )
                parts = call(
                    later_query_kernel,
                    "query",
                    wide + [small, spread],
                    [],
                    [gain[None, :], query_weight[section + 1, 0], stream, theirs],
                    [pltpu.VMEM((query_count, slice_depth), BF16)],
                    flops,
                )
                own_rows = call(
                    own_rows_kernel,
                    "own_rows",
                    [jax.ShapeDtypeStruct(own_rows.shape, BF16)],
                    [],
                    [stream, theirs],
                    [
                        pltpu.VMEM((query_count, slice_depth), BF16),
                        pltpu.VMEM((2 * unit, query_count), F32),
                    ],
                )[0]
                continue
            shape = (CHIPS, unit, query_count)
            kept, sent = call(
                functools.partial(update_kernel, tile_count - 1),
                "update",
                [jax.ShapeDtypeStruct(shape, F32), jax.ShapeDtypeStruct(shape, BF16)],
                [],
                arrays,
                (),
                flops,
            )
        else:
            square_sum = sum(over_tiles(squares_sent, tile_count)[1:], squares)
            query_sum = sum(over_tiles(sent, tile_count)[1:], partial)
            inverse = lax.rsqrt(square_sum / depth + EPSILON)
            queries = (query_sum * inverse[:, None]).astype(BF16)
            weighted, totals = attend_rows(queries, query_pos, query_floor, key_values, key_pos)
            total_sum = sum(over_tiles(totals.astype(BF16), tile_count)[1:], totals)
            weighted_sum = sum(over_tiles(weighted.astype(BF16), tile_count)[1:], weighted)
            attended = (
                (weighted_sum.reshape(query_count, QPK, HD) / total_sum[:, :, None])
                .reshape(query_count, QPK * HD)
                .astype(BF16)
            )
            update = lax.dot_general(
                output_weight[section, 0],
                attended,
                (((1,), (1,)), ((), ())),
                preferred_element_type=F32,
            )
            split = update.reshape(CHIPS, 2, unit, query_count)
            kept = jnp.where(core == 0, split[:, 0], split[:, 1])
            sent = jnp.where(core == 0, split[:, 1], split[:, 0]).astype(BF16)
            kept, sent = (jnp.stack(natural(value, chip)) for value in (kept, sent))
        own_rows = (own_rows.astype(F32) + scatter_rows(kept, sent)).astype(BF16)
    return own_rows


def solution(mesh):
    in_specs = (
        P(("groups", "row"), None),
        P(),
        P("row", None),
        P("row", "groups"),
        P(),
        P(None, "row", None, None),
        P(None, "row", None, None),
        P("groups", None),
    )
    return jax.shard_map(
        on_device, mesh=mesh, in_specs=in_specs, out_specs=P("row", "groups"), check_vma=False
    )
```
